32 devices in a mesh: section: 2 (over y), seq: 4 (over x, core), tensor: 4 (over z).
Axes of the slice: x: 2, y: 2, z: 4, core: 2. Of those that a mesh axis runs over, the one named last changes fastest.
Arguments:
- inputs: bfloat16 [2, 4096, 1024], P(None, ('seq', 'tensor')), may hold values from -6 to 6
- cotangent: bfloat16 [2, 4096, 1024], P(None, ('seq', 'tensor')), may hold values from -6 to 6
- lengths: int32 [2, 4], replicated, may hold values from 1 to 3584, 4096 in all within a row
- w_query: bfloat16 [2, 1024, 1024], P('section', 'seq', 'tensor'), may hold values from -0.1875 to 0.1875
- w_key: bfloat16 [2, 1024, 1024], P('section', 'seq', 'tensor'), may hold values from -0.1875 to 0.1875
- w_value: bfloat16 [2, 1024, 1024], P('section', 'seq', 'tensor'), may hold values from -0.1875 to 0.1875
- w_out: bfloat16 [2, 1024, 1024], P('section', 'tensor', 'seq'), may hold values from -0.75 to 0.75
- w_gate: bfloat16 [2, 1024, 2816], P('section', 'seq', 'tensor'), may hold values from -0.1875 to 0.1875
- w_up: bfloat16 [2, 1024, 2816], P('section', 'seq', 'tensor'), may hold values from -0.1875 to 0.1875
- w_down: bfloat16 [2, 2816, 1024], P('section', 'tensor', 'seq'), may hold values from -0.109375 to 0.109375
- attn_gain: float32 [2, 1024], P('section'), may hold values from 0.5 to 1.5
- mlp_gain: float32 [2, 1024], P('section'), may hold values from 0.5 to 1.5
Outputs:
- layer_out: bfloat16 [2, 2, 4096, 1024], P('section', None, ('seq', 'tensor'))
- input_grad: float32 [2, 2, 4096, 1024], P('section', None, ('seq', 'tensor'))
- grad_query: float32 [2, 1024, 1024], P('section', 'seq', 'tensor')
- grad_key: float32 [2, 1024, 1024], P('section', 'seq', 'tensor')
- grad_value: float32 [2, 1024, 1024], P('section', 'seq', 'tensor')
- grad_out: float32 [2, 1024, 1024], P('section', 'tensor', 'seq')
- grad_gate: float32 [2, 1024, 2816], P('section', 'seq', 'tensor')
- grad_up: float32 [2, 1024, 2816], P('section', 'seq', 'tensor')
- grad_down: float32 [2, 2816, 1024], P('section', 'tensor', 'seq')
- grad_attn_gain: float32 [2, 1024], P('section', ('seq', 'tensor'))
- grad_mlp_gain: float32 [2, 1024], P('section', ('seq', 'tensor'))
The draws below stay inside these ranges and needn't reach their ends.
Inputs may be any that keep to these rules, and one draw needn't show every extreme that they name: `lengths`: each row lists the 4 documents of one micro-batch's packed row in order; they sum to 4096, and the longest has exactly 3584 tokens.
All inputs are finite; a program needn't handle non-finite values.
Results may differ from the reference program's by a relative error of at most 0.029.
Values may be sent and summed in bfloat16 or wider, within the bound.
A program may use at most 256 MiB of HBM per device.

```python
import functools
import math
import jax
import jax.numpy as jnp
import numpy as np
from jax import lax

D = 1024
HS = 64
FF = 2816
GROUP = 1024
MICRO = 2
DOCS = 4
ROW = 4096
HD = 1024


def shard_levels(stream_key, shape, pieces, least, high):
    level, own = 1.0, jax.random.fold_in(stream_key, 6)
    for axis_at, parts in pieces:
        heights = jnp.exp(jax.random.uniform(jax.random.fold_in(own, axis_at), (parts,), jnp.float32, least / len(pieces), high / len(pieces)))
        level = level * jnp.repeat(heights, shape[axis_at] // parts).reshape([-1 if axis == axis_at else 1 for axis in range(len(shape))])
    return level


def profile(amount, total, reach, skew):
    loads = [(1 << 20) // math.isqrt(grade ** skew) + 1 for grade in range(2, amount + 1)]
    spare, holding = total - reach - (amount - 1), [1] * (amount - 1)
    while spare > 0:
        free = [i for i in range(amount - 1) if holding[i] < reach]
        pool, budget = sum([loads[i] for i in free]), spare
        for i in free:
            addition = min(reach - holding[i], max(1, budget * loads[i] // pool), spare)
            holding[i] = holding[i] + addition
            spare = spare - addition
    return np.array([reach] + holding)


def uneven_parts(rng, count, total, most, slope):
    if count == 2:
        one = jax.random.randint(rng, (), max(1, total - most), min(most, total - 1) + 1)
        return jnp.stack([one, total - one])
    sizes = jnp.asarray(profile(count, total, most, slope), jnp.int32)
    pairs = (count - 1) // 2
    source_of, sink = sizes[1:1 + 2 * pairs:2], sizes[2:2 + 2 * pairs:2]
    slack = jnp.minimum(source_of - 1, most - sink)
    passed = jax.random.randint(jax.random.fold_in(rng, 1), (pairs,), 0, 1 << 20) % (slack + 1)
    sizes = sizes.at[1:1 + 2 * pairs:2].set(source_of - passed).at[2:2 + 2 * pairs:2].set(sink + passed)
    return sizes[jax.random.permutation(jax.random.fold_in(rng, 2), count)]


def noise(own_key, extent, width, limit, split=(), kind=jnp.bfloat16):
    level = shard_levels(own_key, extent, split, -0.22, 0.18) if split else 1.0
    drawn = jax.random.normal(own_key, extent, jnp.float32) * width * level
    return jnp.minimum(jnp.maximum(drawn, -limit), limit).astype(kind)


def setup_inputs(seed: int = 0) -> dict:
    key_list = jax.random.split(jax.random.key(seed), 13)
    inputs = noise(key_list[0], (MICRO, ROW, D), 1.0, 6.0, ((1, 16),))
    cotangent = noise(key_list[1], (MICRO, ROW, D), 1.0, 6.0, ((1, 16),))
    lengths = jax.vmap(lambda own: uneven_parts(own, DOCS, ROW, ROW - GROUP // 2, 2))(jax.random.split(key_list[2], MICRO)).reshape((MICRO, DOCS)).astype(jnp.int32)
    w_query = noise(key_list[3], (2, D, HD), D ** -0.5, 0.1875, ((0, 2), (1, 4), (2, 4)))
    w_key = noise(key_list[4], (2, D, HD), D ** -0.5, 0.1875, ((0, 2), (1, 4), (2, 4)))
    w_value = noise(key_list[5], (2, D, HD), D ** -0.5, 0.1875, ((0, 2), (1, 4), (2, 4)))
    w_out = noise(key_list[6], (2, HD, D), (HD // 16) ** -0.5, 0.75, ((0, 2), (1, 4), (2, 4)))
    w_gate = noise(key_list[7], (2, D, FF), D ** -0.5, 0.1875, ((0, 2), (1, 4), (2, 4)))
    w_up = noise(key_list[8], (2, D, FF), D ** -0.5, 0.1875, ((0, 2), (1, 4), (2, 4)))
    w_down = noise(key_list[9], (2, FF, D), FF ** -0.5, 0.109375, ((0, 2), (1, 4), (2, 4)))
    attn_gain = jnp.clip(1.0 + 0.1 * jax.random.normal(key_list[10], (2, D), jnp.float32), 0.5, 1.5)
    mlp_gain = jnp.clip(1.0 + 0.1 * jax.random.normal(key_list[11], (2, D), jnp.float32), 0.5, 1.5)
    return {"inputs": inputs, "cotangent": cotangent, "lengths": lengths, "w_query": w_query, "w_key": w_key, "w_value": w_value, "w_out": w_out, "w_gate": w_gate, "w_up": w_up, "w_down": w_down, "attn_gain": attn_gain, "mlp_gain": mlp_gain}


@jax.custom_vjp
def low(v):
    return lax.optimization_barrier(v.astype(jnp.bfloat16)).astype(jnp.float32)

@jax.custom_vjp
def low_back(v):
    return v

def low_keep(v):
    return (low(v), None)

def low_pass(kept, grad):
    return (grad,)

def back_keep(v):
    return (v, None)

def back_low(kept, grad):
    return (low(grad),)
low.defvjp(low_keep, low_pass)
low_back.defvjp(back_keep, back_low)
EPSILON = 1e-05
NEGATIVE = -1e+30
HIGHEST = lax.Precision.HIGHEST

def product(left, right):
    return jnp.dot(left, right, precision=HIGHEST, preferred_element_type=jnp.float32)

def doc_table(length_row, places):
    doc_ends = jnp.cumsum(length_row).astype(jnp.int32)
    doc_starts = (doc_ends - length_row).astype(jnp.int32)
    segment = lax.optimization_barrier(jnp.sum((places[:, None] >= doc_ends[None, :]).astype(jnp.int32), axis=1))
    member = segment[:, None] == jnp.arange(length_row.shape[0], dtype=jnp.int32)[None, :]
    offset = lax.optimization_barrier(jnp.sum(jnp.where(member, doc_starts[None, :], 0), axis=1))
    return (segment, (places - offset).astype(jnp.int32))

def rotate(matrix, within, direction):
    row_count = matrix.shape[0]
    head_count = matrix.shape[1] // HS
    half_size = HS // 2
    frequency = jnp.exp(jnp.arange(half_size, dtype=jnp.float32) * (-math.log(10000.0) / half_size))
    angles = within.astype(jnp.float32)[:, None] * frequency[None, :]
    cosine = jnp.cos(angles)[:, None, :]
    sine_part = direction * jnp.sin(angles)[:, None, :]
    paired = matrix.reshape(row_count, head_count, 2, half_size)
    former = paired[:, :, 0, :]
    latter = paired[:, :, 1, :]
    turned = jnp.stack([former * cosine - latter * sine_part, latter * cosine + former * sine_part], axis=2)
    return turned.reshape(row_count, head_count * HS)

def normed(values, gain_row):
    inverse = lax.rsqrt(lax.optimization_barrier(jnp.mean(values * values, axis=-1, keepdims=True)) + EPSILON)
    return low(values * inverse * gain_row)

def attend(queries, key_rows, value_rows, segment):
    row_count = queries.shape[0]
    head_count = queries.shape[1] // HS
    block_rows = min(512, row_count)
    query_heads = queries.reshape(row_count, head_count, HS)
    key_heads = key_rows.reshape(row_count, head_count, HS)
    value_heads = value_rows.reshape(row_count, head_count, HS)
    places = jnp.arange(row_count, dtype=jnp.int32)

    def one_block(first_row):
        block_query = lax.dynamic_slice_in_dim(query_heads, first_row, block_rows, 0)
        query_places = first_row + jnp.arange(block_rows, dtype=jnp.int32)
        query_segment = lax.dynamic_slice_in_dim(segment, first_row, block_rows, 0)
        scores = low_back(jnp.einsum('qhd,khd->hqk', block_query, key_heads, precision=HIGHEST) * HS ** (-0.5))
        allowed = (places[None, :] <= query_places[:, None]) & (segment[None, :] == query_segment[:, None])
        masked = jnp.where(allowed[None], scores, NEGATIVE)
        largest = lax.optimization_barrier(jnp.max(masked, axis=2, keepdims=True))
        weights = jnp.where(allowed[None], jnp.exp(masked - largest), 0.0)
        totals = lax.optimization_barrier(jnp.sum(weights, axis=2))
        mixed = jnp.einsum('hqk,khd->qhd', low(weights), value_heads, precision=HIGHEST)
        return (mixed / jnp.transpose(totals)[:, :, None]).reshape(block_rows, head_count * HS)
    firsts = jnp.arange(row_count // block_rows, dtype=jnp.int32) * block_rows
    return lax.map(jax.checkpoint(one_block), firsts).reshape(row_count, head_count * HS)

def layer(residual, matrices, gain_pair, earlier_values, segment, within):
    w_query, w_key, w_value, w_out, w_gate, w_up, w_down = matrices
    normed_in = normed(residual, gain_pair[0])
    queries = low(rotate(low_back(product(normed_in, w_query)), within, 1.0))
    key_rows = low(rotate(low_back(product(normed_in, w_key)), within, 1.0))
    value_raw = low_back(product(normed_in, w_value))
    if earlier_values is None:
        value_rows = low(value_raw)
    else:
        value_rows = low(0.5 * value_raw + 0.5 * earlier_values)
    attended = low(low_back(attend(queries, key_rows, value_rows, segment)))
    middle = residual + low_back(product(attended, w_out))
    normed_mid = normed(middle, gain_pair[1])
    gate_rows = low_back(product(normed_mid, w_gate))
    up_rows = low_back(product(normed_mid, w_up))
    hidden = low(jax.nn.silu(gate_rows) * up_rows)
    return (middle + low_back(product(hidden, w_down)), value_rows)

def lower_half(segment, within, residual, matrices, gain_pair):
    result, value_rows = layer(residual, matrices, gain_pair, None, segment, within)
    return (low(result), value_rows)

def upper_half(segment, within, first_out, earlier_values, matrices, gain_pair):
    return layer(first_out, matrices, gain_pair, earlier_values, segment, within)[0]

def reference(inputs, cotangent, lengths, w_query, w_key, w_value, w_out, w_gate, w_up, w_down, attn_gain, mlp_gain):
    matrices = tuple((weight.astype(jnp.float32) for weight in (w_query, w_key, w_value, w_out, w_gate, w_up, w_down)))
    gains_all = (attn_gain.astype(jnp.float32), mlp_gain.astype(jnp.float32))
    places = jnp.arange(ROW, dtype=jnp.int32)

    def micro_step(carry_sums, item):
        row_in, grad_top, length_row = item
        segment, within = doc_table(length_row, places)
        first_set = tuple((weight[0] for weight in matrices))
        second_set = tuple((weight[1] for weight in matrices))
        first_gains = (gains_all[0][0], gains_all[1][0])
        second_gains = (gains_all[0][1], gains_all[1][1])
        (first_out, earlier_values), lower_vjp = jax.vjp(functools.partial(lower_half, segment, within), row_in.astype(jnp.float32), first_set, first_gains)
        second_out, upper_vjp = jax.vjp(functools.partial(upper_half, segment, within), first_out, earlier_values, second_set, second_gains)
        grad_first, grad_values, grad_second_set, grad_second_gains = upper_vjp(grad_top.astype(jnp.float32))
        grad_inputs, grad_first_set, grad_first_gains = lower_vjp((grad_first, grad_values))
        weight_sums, gain_sums = carry_sums
        weight_sums = tuple((total + jnp.stack([one, two]) for total, one, two in zip(weight_sums, grad_first_set, grad_second_set)))
        gain_sums = tuple((total + jnp.stack([one, two]) for total, one, two in zip(gain_sums, grad_first_gains, grad_second_gains)))
        return ((weight_sums, gain_sums), (first_out, second_out, grad_inputs, grad_first))
    start_sums = (tuple((jnp.zeros_like(weight) for weight in matrices)), tuple((jnp.zeros_like(gain_row) for gain_row in gains_all)))
    (weight_sums, gain_sums), (first_outs, second_outs, grad_inputs, grad_firsts) = lax.scan(micro_step, start_sums, (inputs, cotangent, lengths))
    layer_out = jnp.stack([first_outs, second_outs]).astype(jnp.bfloat16)
    input_grad = jnp.stack([grad_inputs, grad_firsts])
    return (layer_out, input_grad, weight_sums[0], weight_sums[1], weight_sums[2], weight_sums[3], weight_sums[4], weight_sums[5], weight_sums[6], gain_sums[0], gain_sums[1])
```

```python
import functools
import math

import jax
import jax.numpy as jnp
from jax import lax
from jax.experimental import pallas as pl
from jax.experimental.pallas import tpu as pltpu
from jax.sharding import PartitionSpec as P

HS = 64


EPSILON = 1e-05
NEGATIVE = -1e30


def shifted(shard, axis, by):
    peers = lax.axis_size(axis)
    pairs = [(i, i + by) for i in range(peers) if 0 <= i + by < peers]
    return lax.ppermute(shard, axis, pairs)


def product(left, right):
    return jnp.dot(left, right, preferred_element_type=jnp.float32)


def inner_rows(left, right):
    return lax.dot_general(
        left, right, (((0,), (0,)), ((), ())), preferred_element_type=jnp.float32
    )


def against(left, right):
    return lax.dot_general(
        left, right, (((1,), (1,)), ((), ())), preferred_element_type=jnp.float32
    )


def doc_table(length_row, places):
    doc_ends = jnp.cumsum(length_row)
    doc_starts = doc_ends - length_row
    segment = jnp.sum((places[:, None] >= doc_ends[None, :]).astype(jnp.int32), axis=1)
    member = segment[:, None] == jnp.arange(length_row.shape[0], dtype=jnp.int32)[None, :]
    offset = jnp.sum(jnp.where(member, doc_starts[None, :], 0), axis=1)
    return (segment, places - offset)


def rotate(matrix, within, direction):
    row_count = matrix.shape[0]
    head_count = matrix.shape[1] // HS
    half_size = HS // 2
    frequency = jnp.exp(jnp.arange(half_size, dtype=jnp.float32) * (-math.log(10000.0) / half_size))
    angles = within.astype(jnp.float32)[:, None] * frequency[None, :]
    cosine = jnp.cos(angles)[:, None, :]
    sine_part = direction * jnp.sin(angles)[:, None, :]
    paired = matrix.reshape(row_count, head_count, 2, half_size)
    former = paired[:, :, 0, :]
    latter = paired[:, :, 1, :]
    turned = jnp.stack(
        [former * cosine - latter * sine_part, latter * cosine + former * sine_part], axis=2
    )
    return turned.reshape(row_count, head_count * HS)


def norm_rows(values, gain_row):
    inverse = lax.rsqrt(jnp.mean(values * values, axis=-1, keepdims=True) + EPSILON)
    unit_rows = values * inverse
    return (unit_rows, inverse, (unit_rows * gain_row).astype(jnp.bfloat16))


def norm_back(grad_normed, unit_rows, inverse, gain_row):
    shaped = grad_normed * gain_row
    inner = jnp.mean(shaped * unit_rows, axis=-1, keepdims=True)
    return (inverse * (shaped - unit_rows * inner), jnp.sum(grad_normed * unit_rows, axis=0))


def spread(values):
    return lax.all_gather(values, "tensor", axis=0, tiled=True)


def fold_rows(values):
    return lax.psum_scatter(
        values.astype(jnp.bfloat16), "tensor", scatter_dimension=0, tiled=True
    ).astype(jnp.float32)


def allowed_mask(places, segment, key_places, key_segment):
    return (key_places[None, :] <= places[:, None]) & (key_segment[None, :] == segment[:, None])


def project(normed_all, matrices, within, mixin, on_first):
    query_rows = rotate(product(normed_all, matrices[0]), within, 1.0).astype(jnp.bfloat16)
    key_rows = rotate(product(normed_all, matrices[1]), within, 1.0).astype(jnp.bfloat16)
    value_raw = product(normed_all, matrices[2])
    value_rows = jnp.where(
        on_first, value_raw, 0.5 * value_raw + 0.5 * mixin.astype(jnp.float32)
    ).astype(jnp.bfloat16)
    return (query_rows, key_rows, value_rows)


def cycle_attend(query_rows, key_rows, value_rows, places, segment, length_row):
    row_count = query_rows.shape[0]
    head_count = query_rows.shape[1] // HS
    query_heads = query_rows.reshape(row_count, head_count, HS)
    largest = jnp.full((head_count, row_count), NEGATIVE, jnp.float32)
    piece_keys = lax.all_gather(key_rows, "seq", axis=0, tiled=True)
    piece_values = lax.all_gather(value_rows, "seq", axis=0, tiled=True)
    piece_rows = piece_keys.shape[0]
    key_places = jnp.arange(piece_rows, dtype=jnp.int32)
    key_segment = doc_table(length_row, key_places)[0]
    allowed = allowed_mask(places, segment, key_places, key_segment)
    scores = jnp.einsum(
        "qhd,khd->hqk",
        query_heads,
        piece_keys.reshape(piece_rows, head_count, HS),
        preferred_element_type=jnp.float32,
    ) * HS ** (-0.5)
    masked = jnp.where(allowed[None], scores, NEGATIVE)
    newest = jnp.maximum(largest, jnp.max(masked, axis=2))
    weights = jnp.where(allowed[None], jnp.exp(masked - newest[:, :, None]), 0.0)
    totals = jnp.sum(weights, axis=2)
    summed = jnp.einsum(
        "hqk,khd->hqd",
        weights.astype(jnp.bfloat16),
        piece_values.reshape(piece_rows, head_count, HS),
        preferred_element_type=jnp.float32,
    )
    largest, totals, summed = (newest, totals, summed)
    attended = summed / totals[:, :, None]
    return jnp.transpose(attended, (1, 0, 2)).reshape(row_count, head_count * HS)


def forward_layer(residual, mixin, on_first, matrices, gain_pair, places, length_row):
    segment, within = doc_table(length_row, places)
    normed_in = norm_rows(residual, gain_pair[0])[2]
    normed_all = spread(normed_in)
    query_rows, key_rows, value_rows = project(normed_all, matrices, within, mixin, on_first)
    attended = cycle_attend(query_rows, key_rows, value_rows, places, segment, length_row)
    middle = residual + fold_rows(product(attended.astype(jnp.bfloat16), matrices[3]))
    normed_mid = norm_rows(middle, gain_pair[1])[2]
    normed_mid_all = spread(normed_mid)
    gate_rows = product(normed_mid_all, matrices[4])
    up_rows = product(normed_mid_all, matrices[5])
    hidden = (jax.nn.silu(gate_rows) * up_rows).astype(jnp.bfloat16)
    return (middle + fold_rows(product(hidden, matrices[6])), value_rows)


def backward_layer(
    residual, mixin, grad_top, extra_values, on_first, matrices, gain_pair, places, length_row
):
    segment, within = doc_table(length_row, places)
    unit_in, inverse_in, normed_in = norm_rows(residual, gain_pair[0])
    normed_all = spread(normed_in)
    query_rows, key_rows, value_rows = project(normed_all, matrices, within, mixin, on_first)
    all_keys, all_values = (
        lax.all_gather(key_rows, "seq", axis=0, tiled=True),
        lax.all_gather(value_rows, "seq", axis=0, tiled=True),
    )
    row_count = query_rows.shape[0]
    head_count = query_rows.shape[1] // HS
    total_rows = all_keys.shape[0]
    block_count = total_rows // row_count
    query_heads = query_rows.reshape(row_count, head_count, HS)
    key_blocks = all_keys.reshape(block_count, row_count, head_count, HS)
    value_blocks = all_values.reshape(block_count, row_count, head_count, HS)
    block_numbers = jnp.arange(block_count, dtype=jnp.int32)

    def block_scores(block_number, block_keys):
        key_places = block_number * row_count + jnp.arange(row_count, dtype=jnp.int32)
        key_segment = doc_table(length_row, key_places)[0]
        allowed = allowed_mask(places, segment, key_places, key_segment)
        scores = jnp.einsum(
            "qhd,khd->hqk", query_heads, block_keys, preferred_element_type=jnp.float32
        ) * HS ** (-0.5)
        return (allowed, jnp.where(allowed[None], scores, NEGATIVE))

    def first_pass(running, block_item):
        largest, totals, summed = running
        block_number, block_keys, block_values = block_item
        allowed, masked = block_scores(block_number, block_keys)
        newest = jnp.maximum(largest, jnp.max(masked, axis=2))
        rescale = jnp.exp(largest - newest)
        weights = jnp.where(allowed[None], jnp.exp(masked - newest[:, :, None]), 0.0)
        totals = totals * rescale + jnp.sum(weights, axis=2)
        summed = summed * rescale[:, :, None] + jnp.einsum(
            "hqk,khd->hqd",
            weights.astype(jnp.bfloat16),
            block_values,
            preferred_element_type=jnp.float32,
        )
        return ((newest, totals, summed), None)

    start_state = (
        jnp.full((head_count, row_count), NEGATIVE, jnp.float32),
        jnp.zeros((head_count, row_count), jnp.float32),
        jnp.zeros((head_count, row_count, HS), jnp.float32),
    )
    (largest, totals, summed), _ = lax.scan(
        first_pass, start_state, (block_numbers, key_blocks, value_blocks)
    )
    attended = summed / totals[:, :, None]
    attended_low = (
        jnp.transpose(attended, (1, 0, 2)).reshape(row_count, head_count * HS).astype(jnp.bfloat16)
    )
    middle = residual + fold_rows(product(attended_low, matrices[3]))
    unit_mid, inverse_mid, normed_mid = norm_rows(middle, gain_pair[1])
    normed_mid_all = spread(normed_mid)
    gate_rows = product(normed_mid_all, matrices[4])
    up_rows = product(normed_mid_all, matrices[5])
    sigmoid_gate = jax.nn.sigmoid(gate_rows)
    activated = gate_rows * sigmoid_gate
    hidden = (activated * up_rows).astype(jnp.bfloat16)
    grad_top_all = spread(grad_top.astype(jnp.bfloat16))
    grad_w_down = inner_rows(hidden, grad_top_all)
    grad_hidden = against(grad_top_all, matrices[6])
    grad_gate = (
        grad_hidden * up_rows * sigmoid_gate * (1.0 + gate_rows * (1.0 - sigmoid_gate))
    ).astype(jnp.bfloat16)
    grad_up = (grad_hidden * activated).astype(jnp.bfloat16)
    grad_w_gate = inner_rows(normed_mid_all, grad_gate)
    grad_w_up = inner_rows(normed_mid_all, grad_up)
    grad_normed_mid = fold_rows(against(grad_gate, matrices[4]) + against(grad_up, matrices[5]))
    grad_middle, grad_gain_mid = norm_back(grad_normed_mid, unit_mid, inverse_mid, gain_pair[1])
    grad_middle = grad_middle + grad_top
    grad_middle_all = spread(grad_middle.astype(jnp.bfloat16))
    grad_w_out = inner_rows(attended_low, grad_middle_all)
    grad_attended = against(grad_middle_all, matrices[3]).astype(jnp.bfloat16)
    grad_heads = jnp.transpose(grad_attended.reshape(row_count, head_count, HS), (1, 0, 2))
    delta = jnp.sum(grad_heads.astype(jnp.float32) * attended, axis=2)
    scaled_grad = grad_heads.astype(jnp.float32) / totals[:, :, None]
    scaled_high = scaled_grad.astype(jnp.bfloat16)
    scaled_rest = (scaled_grad - scaled_high.astype(jnp.float32)).astype(jnp.bfloat16)
    inverse_totals = 1.0 / totals[:, :, None]

    def second_pass(grad_sum, block_item):
        block_number, block_keys, block_values = block_item
        allowed, masked = block_scores(block_number, block_keys)
        weights = jnp.where(allowed[None], jnp.exp(masked - largest[:, :, None]), 0.0)
        low_weights = weights.astype(jnp.bfloat16)
        along = jnp.einsum(
            "hqd,khd->hqk", grad_heads, block_values, preferred_element_type=jnp.float32
        )
        grad_scores = (weights * inverse_totals * (along - delta[:, :, None])).astype(jnp.bfloat16)
        grad_sum = grad_sum + jnp.einsum(
            "hqk,khd->qhd", grad_scores, block_keys, preferred_element_type=jnp.float32
        ) * HS ** (-0.5)
        block_key_grad = jnp.einsum(
            "hqk,qhd->khd", grad_scores, query_heads, preferred_element_type=jnp.float32
        ) * HS ** (-0.5)
        block_value_grad = jnp.einsum(
            "hqk,hqd->khd", low_weights, scaled_high, preferred_element_type=jnp.float32
        ) + jnp.einsum("hqk,hqd->khd", low_weights, scaled_rest, preferred_element_type=jnp.float32)
        return (grad_sum, (block_key_grad, block_value_grad))

    grad_queries, (grad_keys, grad_values) = lax.scan(
        second_pass,
        jnp.zeros((row_count, head_count, HS), jnp.float32),
        (block_numbers, key_blocks, value_blocks),
    )
    own_keys, own_values = (
        lax.psum_scatter(
            grad_keys.reshape(total_rows, head_count * HS).astype(jnp.bfloat16),
            "seq",
            scatter_dimension=0,
            tiled=True,
        ).astype(jnp.float32),
        lax.psum_scatter(
            grad_values.reshape(total_rows, head_count * HS).astype(jnp.bfloat16),
            "seq",
            scatter_dimension=0,
            tiled=True,
        ).astype(jnp.float32),
    )
    grad_value_raw = jnp.where(on_first, own_values + extra_values, 0.5 * own_values).astype(
        jnp.bfloat16
    )
    send_values = 0.5 * own_values
    grad_query_raw = rotate(grad_queries.reshape(row_count, head_count * HS), within, -1.0).astype(
        jnp.bfloat16
    )
    grad_key_raw = rotate(own_keys, within, -1.0).astype(jnp.bfloat16)
    grad_w_query = inner_rows(normed_all, grad_query_raw)
    grad_w_key = inner_rows(normed_all, grad_key_raw)
    grad_w_value = inner_rows(normed_all, grad_value_raw)
    grad_normed_in = fold_rows(
        against(grad_query_raw, matrices[0])
        + against(grad_key_raw, matrices[1])
        + against(grad_value_raw, matrices[2])
    )
    grad_in, grad_gain_in = norm_back(grad_normed_in, unit_in, inverse_in, gain_pair[0])
    weight_terms = (
        grad_w_query,
        grad_w_key,
        grad_w_value,
        grad_w_out,
        grad_w_gate,
        grad_w_up,
        grad_w_down,
    )
    return (grad_in + grad_middle, send_values, weight_terms, (grad_gain_in, grad_gain_mid))


def on_device(
    inputs,
    cotangent,
    lengths,
    w_query,
    w_key,
    w_value,
    w_out,
    w_gate,
    w_up,
    w_down,
    attn_gain,
    mlp_gain,
):
    section_index = lax.axis_index("section")
    on_first = section_index == 0
    micro_count = inputs.shape[0]
    local_rows = inputs.shape[1]
    model_width = inputs.shape[2]
    group_rows = local_rows * lax.axis_size("tensor")
    head_width = w_query.shape[2]
    row_values = local_rows * model_width
    places = lax.axis_index("seq") * group_rows + jnp.arange(group_rows, dtype=jnp.int32)
    gain_pair = (attn_gain[0], mlp_gain[0])
    gathered = (
        lax.all_gather(w_query[0], "seq", axis=0, tiled=True),
        lax.all_gather(w_key[0], "seq", axis=0, tiled=True),
        lax.all_gather(w_value[0], "seq", axis=0, tiled=True),
        lax.all_gather(w_out[0], "seq", axis=1, tiled=True),
        lax.all_gather(w_gate[0], "seq", axis=0, tiled=True),
        lax.all_gather(w_up[0], "seq", axis=0, tiled=True),
        lax.all_gather(w_down[0], "seq", axis=1, tiled=True),
    )
    recv_rows = jnp.zeros((local_rows, model_width), jnp.bfloat16)
    recv_values = jnp.zeros((group_rows, head_width), jnp.bfloat16)
    kept_inputs = jnp.zeros((micro_count, local_rows, model_width), jnp.bfloat16)
    kept_values = jnp.zeros((micro_count, group_rows, head_width), jnp.bfloat16)
    kept_outputs = jnp.zeros((micro_count, local_rows, model_width), jnp.bfloat16)
    for moment in range(micro_count + 1):
        which = moment - section_index
        usable = (which >= 0) & (which < micro_count)
        slot_index = jnp.clip(which, 0, micro_count - 1)
        own_rows = lax.dynamic_index_in_dim(inputs, slot_index, 0, keepdims=False)
        layer_in = jnp.where(on_first, own_rows, recv_rows)
        length_row = lax.dynamic_index_in_dim(lengths, slot_index, 0, keepdims=False)
        result, value_rows = forward_layer(
            layer_in.astype(jnp.float32),
            recv_values,
            on_first,
            gathered,
            gain_pair,
            places,
            length_row,
        )
        result_low = result.astype(jnp.bfloat16)
        kept_inputs = jnp.where(
            usable,
            lax.dynamic_update_index_in_dim(kept_inputs, layer_in, slot_index, 0),
            kept_inputs,
        )
        kept_values = jnp.where(
            usable,
            lax.dynamic_update_index_in_dim(kept_values, recv_values, slot_index, 0),
            kept_values,
        )
        kept_outputs = jnp.where(
            usable,
            lax.dynamic_update_index_in_dim(kept_outputs, result_low, slot_index, 0),
            kept_outputs,
        )
        if moment < micro_count:
            packed = jnp.concatenate([result_low.reshape(-1), value_rows.reshape(-1)])
            arrived = shifted(packed, "section", 1)
            recv_rows = arrived[:row_values].reshape(local_rows, model_width)
            recv_values = arrived[row_values:].reshape(group_rows, head_width)
    grad_rows_in = jnp.zeros((local_rows, model_width), jnp.float32)
    grad_values_in = jnp.zeros((group_rows, head_width), jnp.float32)
    grad_inputs = jnp.zeros((micro_count, local_rows, model_width), jnp.float32)
    weight_sums = tuple((jnp.zeros(matrix.shape, jnp.float32) for matrix in gathered))
    share_sums = (
        jnp.zeros(w_query[0].shape, jnp.float32),
        jnp.zeros(w_key[0].shape, jnp.float32),
        jnp.zeros(w_value[0].shape, jnp.float32),
        jnp.zeros(w_out[0].shape, jnp.float32),
        jnp.zeros(w_gate[0].shape, jnp.float32),
        jnp.zeros(w_up[0].shape, jnp.float32),
        jnp.zeros(w_down[0].shape, jnp.float32),
    )
    gain_sums = (jnp.zeros((model_width,), jnp.float32), jnp.zeros((model_width,), jnp.float32))
    for moment in range(micro_count + 1):
        which = moment - (1 - section_index)
        usable = (which >= 0) & (which < micro_count)
        slot_index = jnp.clip(which, 0, micro_count - 1)
        matrices = (
            lax.all_gather(w_query[0], "seq", axis=0, tiled=True),
            lax.all_gather(w_key[0], "seq", axis=0, tiled=True),
            lax.all_gather(w_value[0], "seq", axis=0, tiled=True),
            lax.all_gather(w_out[0], "seq", axis=1, tiled=True),
            lax.all_gather(w_gate[0], "seq", axis=0, tiled=True),
            lax.all_gather(w_up[0], "seq", axis=0, tiled=True),
            lax.all_gather(w_down[0], "seq", axis=1, tiled=True),
        )
        layer_in = lax.dynamic_index_in_dim(kept_inputs, slot_index, 0, keepdims=False).astype(
            jnp.float32
        )
        mixin = lax.dynamic_index_in_dim(kept_values, slot_index, 0, keepdims=False)
        length_row = lax.dynamic_index_in_dim(lengths, slot_index, 0, keepdims=False)
        own_grad = lax.dynamic_index_in_dim(cotangent, slot_index, 0, keepdims=False).astype(
            jnp.float32
        )
        grad_top = jnp.where(usable, jnp.where(on_first, grad_rows_in, own_grad), 0.0)
        extra_values = jnp.where(usable & on_first, grad_values_in, 0.0)
        grad_in, send_values, weight_terms, gain_terms = backward_layer(
            layer_in,
            mixin,
            grad_top,
            extra_values,
            on_first,
            matrices,
            gain_pair,
            places,
            length_row,
        )
        gain_sums = (gain_sums[0] + gain_terms[0], gain_sums[1] + gain_terms[1])
        weight_sums = tuple((total + term for total, term in zip(weight_sums, weight_terms)))
        grad_inputs = jnp.where(
            usable,
            lax.dynamic_update_index_in_dim(grad_inputs, grad_in, slot_index, 0),
            grad_inputs,
        )
        if moment < micro_count:
            packed = jnp.concatenate([grad_in.reshape(-1), send_values.reshape(-1)])
            arrived = shifted(packed.astype(jnp.bfloat16), "section", -1).astype(packed.dtype)
            grad_rows_in = arrived[:row_values].reshape(local_rows, model_width)
            grad_values_in = arrived[row_values:].reshape(group_rows, head_width)
    share_sums = (
        lax.psum_scatter(
            weight_sums[0].astype(jnp.bfloat16), "seq", scatter_dimension=0, tiled=True
        ).astype(jnp.float32),
        lax.psum_scatter(
            weight_sums[1].astype(jnp.bfloat16), "seq", scatter_dimension=0, tiled=True
        ).astype(jnp.float32),
        lax.psum_scatter(
            weight_sums[2].astype(jnp.bfloat16), "seq", scatter_dimension=0, tiled=True
        ).astype(jnp.float32),
        lax.psum_scatter(
            weight_sums[3].astype(jnp.bfloat16), "seq", scatter_dimension=1, tiled=True
        ).astype(jnp.float32),
        lax.psum_scatter(
            weight_sums[4].astype(jnp.bfloat16), "seq", scatter_dimension=0, tiled=True
        ).astype(jnp.float32),
        lax.psum_scatter(
            weight_sums[5].astype(jnp.bfloat16), "seq", scatter_dimension=0, tiled=True
        ).astype(jnp.float32),
        lax.psum_scatter(
            weight_sums[6].astype(jnp.bfloat16), "seq", scatter_dimension=1, tiled=True
        ).astype(jnp.float32),
    )
    gain_shares = (
        lax.psum_scatter(gain_sums[0], ("seq", "tensor"), scatter_dimension=0, tiled=True),
        lax.psum_scatter(gain_sums[1], ("seq", "tensor"), scatter_dimension=0, tiled=True),
    )
    return (
        kept_outputs[None],
        grad_inputs[None],
        share_sums[0][None],
        share_sums[1][None],
        share_sums[2][None],
        share_sums[3][None],
        share_sums[4][None],
        share_sums[5][None],
        share_sums[6][None],
        gain_shares[0][None],
        gain_shares[1][None],
    )


MESH_ID = pl.DeviceIdType.MESH
LOW = jnp.bfloat16
F32 = jnp.float32
ORDERS = ((1, 2, 4), (2, 4, 1), (4, 1, 2))
LEVELS = ((0,), (1, 2, 4), (3, 5, 6), (7,))
NT = (((1,), (1,)), ((), ()))
NN = (((1,), (0,)), ((), ()))
TN = (((0,), (0,)), ((), ()))
VMEM_BYTES = 60 * 2**20


def dot(left, right, dims=NN):
    return lax.dot_general(left, right, dims, preferred_element_type=F32)


def flip(value, bit):
    if isinstance(bit, int):
        return 1 - value if bit else value
    return value + bit - 2 * value * bit


def spot():
    y, s, z = lax.axis_index("section"), lax.axis_index("seq"), lax.axis_index("tensor")
    return (y, lax.div(s, 2), lax.rem(s, 2), lax.div(z, 2), lax.rem(z, 2))


def device(at):
    y, x, c, h, p = at
    return (y, 2 * x + c, 2 * h + p)


def moved(at, mask, core=0):
    y, x, c, h, p = at
    if isinstance(mask, int):
        bits = (mask & 1, (mask >> 1) & 1, mask >> 2)
    else:
        bits = (lax.rem(mask, 2), lax.rem(lax.div(mask, 2), 2), lax.div(mask, 4))
    return (flip(y, bits[1]), flip(x, bits[0]), flip(c, core), h, flip(p, bits[2]))


def far_role(at):
    return flip(at[0], at[2])


def lane_of(at):
    return 2 * flip(at[3], far_role(at)) + at[4]


def block_of(at):
    return (2 * at[1] + at[2]) * 4 + lane_of(at)


def level_mask(level, i):
    if level == 0:
        return 0 * i
    if level == 1:
        return 1 + i + lax.div(i, 2)
    if level == 2:
        return 3 + i + lax.div(i + 1, 2)
    return 0 * i + 7


def last_bit(k, mask):
    return [bit for bit in ORDERS[k] if bit & mask][-1]


def parts_of(rows):
    units = rows // 16
    small = units // 3
    sizes = (16 * (units - 2 * small), 16 * small, 16 * small)
    return ((0, sizes[0]), (sizes[0], sizes[1]), (sizes[0] + sizes[1], sizes[2]))


def remote(src, dst, send, recv, at):
    return pltpu.make_async_remote_copy(
        src_ref=src, dst_ref=dst, send_sem=send, recv_sem=recv, device_id=device(at), device_id_type=MESH_ID
    )


def greet(at):
    barrier = pltpu.get_barrier_semaphore()
    for mask, core in ((1, 0), (2, 0), (4, 0), (0, 1)):
        pl.semaphore_signal(barrier, inc=1, device_id=device(moved(at, mask, core)), device_id_type=MESH_ID)
    pl.semaphore_wait(barrier, 4)


def gather(at, buf, sems, on_block):
    send, recv, csend, crecv = sems
    parts = parts_of(buf.shape[1])

    def rows(mask, k, core=0):
        return buf.at[block_of(moved(at, mask, core)), pl.ds(*parts[k])]

    def hop(k, target):
        bit = last_bit(k, target)
        ref = rows(target ^ bit, k)
        return remote(ref, ref, send.at[k, target], recv.at[k, target], moved(at, bit))

    def arrival(k, target):
        ref = rows(target, k)
        return remote(ref, ref, send.at[k, target], recv.at[k, target], moved(at, last_bit(k, target)))

    def across(mask, core=0):
        ref = buf.at[block_of(moved(at, mask, core))]
        return remote(ref, ref, csend.at[mask], crecv.at[mask], moved(at, 0, 1))

    def visit(level, core):
        def one(i, none):
            on_block(block_of(moved(at, level_mask(level, i), core)))
            return none

        lax.fori_loop(0, len(LEVELS[level]), one, 0)

    for i in range(3):
        for k in range(3):
            hop(k, ORDERS[k][i]).start()
    across(0).start()
    visit(0, 0)
    across(0, 1).wait_recv()
    visit(0, 1)
    for level in (1, 2, 3):
        for mask in LEVELS[level]:
            for k in range(3):
                arrival(k, mask).wait_recv()
                place = ORDERS[k].index(last_bit(k, mask))
                for bit in ORDERS[k][place + 1 :]:
                    hop(k, mask | bit).start()
            across(mask).start()
        visit(level, 0)
        for mask in LEVELS[level]:
            across(mask, 1).wait_recv()
        visit(level, 1)
    for k in range(3):
        for target in range(1, 8):
            hop(k, target).wait_send()
    for mask in range(8):
        across(mask).wait_send()


def scatter(at, total, boxes, sems, partial, copy=None):
    own, out_c, in_c, rin = boxes
    send, recv, csend, crecv = sems
    parts = parts_of(total.shape[0])

    def hop(k, target):
        rows = pl.ds(*parts[k])
        return remote(
            own.at[target - 1, rows],
            rin.at[target - 1, rows],
            send.at[k, target],
            recv.at[k, target],
            moved(at, last_bit(k, target)),
        )

    def across(mask):
        return remote(out_c.at[mask], in_c.at[mask], csend.at[mask], crecv.at[mask], moved(at, 0, 1))

    def emit(level):
        def one(i, none):
            mask = level_mask(level, i)
            out_c[mask] = partial(block_of(moved(at, mask, 1))).astype(LOW)
            return none

        lax.fori_loop(0, len(LEVELS[level]), one, 0)
        for mask in LEVELS[level]:
            across(mask).start()

    def keep(level):
        for mask in LEVELS[level]:
            across(mask).wait_recv()

        def one(i, none):
            mask = level_mask(level, i)
            mine = partial(block_of(moved(at, mask))) + in_c[mask].astype(F32)
            if level == 0:
                total[...] = mine
            else:
                own[mask - 1] = mine.astype(LOW)
            return none

        lax.fori_loop(0, len(LEVELS[level]), one, 0)
        for mask in LEVELS[level]:
            for k in range(3):
                if mask & ORDERS[k][2]:
                    hop(k, mask).start()

    def arrived(k, target):
        hop(k, target).wait_recv()
        return rin[target - 1, pl.ds(*parts[k])].astype(F32)

    emit(3)
    emit(2)
    keep(3)
    keep(2)
    emit(1)
    keep(1)
    if copy is not None:
        copy.wait()
    emit(0)
    keep(0)
    for mask_of in (lambda a, b: a | b, lambda a, b: b):
        for k in range(3):
            first, second, third = ORDERS[k]
            mask, rows = mask_of(first, second), pl.ds(*parts[k])
            own[mask - 1, rows] = (own[mask - 1, rows].astype(F32) + arrived(k, mask | third)).astype(LOW)
            hop(k, mask).start()
    for k in range(3):
        first, second, third = ORDERS[k]
        rows = pl.ds(*parts[k])
        own[first - 1, rows] = (
            own[first - 1, rows].astype(F32) + arrived(k, first | third) + arrived(k, first | second)
        ).astype(LOW)
        hop(k, first).start()
    for k in range(3):
        first, second, third = ORDERS[k]
        rows = pl.ds(*parts[k])
        total[rows] = total[rows] + arrived(k, third) + arrived(k, second) + arrived(k, first)
    for k in range(3):
        for target in range(1, 8):
            hop(k, target).wait_send()
    for mask in range(8):
        across(mask).wait_send()


def unit_of(values):
    inverse = lax.rsqrt(jnp.mean(values * values, axis=-1, keepdims=True) + EPSILON)
    return (values * inverse, inverse)


def back_of(grad_normed, values, gain_row):
    unit, inverse = unit_of(values)
    shaped = grad_normed * gain_row
    inner = jnp.mean(shaped * unit, axis=-1, keepdims=True)
    return (inverse * (shaped - unit * inner), jnp.sum(grad_normed * unit, axis=0, keepdims=True))


def span(b, rows):
    return pl.ds(pl.multiple_of(b * rows, rows), rows)


def turned(top, bottom, cosine, sine):
    return (top * cosine - bottom * sine, bottom * cosine + top * sine)


def project_block(b, buf, w_ref, cos_ref, sin_ref, mix_ref, qkv_ref):
    rows, half = buf.shape[1], HS // 2
    cols = span(b, rows)
    raw = dot(w_ref[...], buf[b], NT)
    cosine, sine = cos_ref[:, cols], sin_ref[:, cols]
    for first, scale in ((0, HS**-0.5), (HS, 1.0)):
        a, bb = turned(raw[first : first + half], raw[first + half : first + HS], cosine, sine)
        qkv_ref[first : first + half, cols] = (a.astype(LOW) * scale).astype(LOW)
        qkv_ref[first + half : first + HS, cols] = (bb.astype(LOW) * scale).astype(LOW)
    value = raw[2 * HS :]
    if mix_ref is not None:
        value = 0.5 * value + 0.5 * mix_ref[:, cols].astype(F32)
    qkv_ref[2 * HS :, cols] = value.astype(LOW)


def save(buf, out, sem):
    return pltpu.make_async_copy(buf, out, sem)


def first_kernel(x_ref, gain_ref, w_ref, cos_ref, sin_ref, qkv_ref, normed_ref, buf, ag_sems, sem):
    at = spot()
    greet(at)
    buf[block_of(at)] = (unit_of(x_ref[...].astype(F32))[0] * gain_ref[...]).astype(LOW)
    gather(at, buf, ag_sems, lambda b: project_block(b, buf, w_ref, cos_ref, sin_ref, None, qkv_ref))
    copy = save(buf, normed_ref, sem)
    copy.start()
    copy.wait()


def up_block(b, buf, f_ref, hidden_ref, one_ref, two_ref):
    rows = span(b, buf.shape[1])
    x = buf[b]
    gate, up = dot(x, f_ref[0], NT), dot(x, f_ref[1], NT)
    sigmoid = 1.0 / (1.0 + jnp.exp(-gate))
    activated = gate * sigmoid
    hidden_ref[rows] = (activated * up).astype(LOW)
    one_ref[rows] = (up * sigmoid * (1.0 + gate * (1.0 - sigmoid))).astype(LOW)
    two_ref[rows] = activated.astype(LOW)


def middle_kernel(
    att_ref, x_ref, wo_ref, f_ref, gain_mid_ref, gain_in_ref, w_ref, cos_ref, sin_ref, mix_ref,
    middle_ref, out_ref, hidden_ref, one_ref, two_ref, qkv_ref, nmid_ref, normed_ref,
    buf, total, own, out_c, in_c, rin, ag_sems, rs_sems, sem,
):
    at = spot()
    rows = x_ref.shape[0]
    greet(at)
    boxes = (own, out_c, in_c, rin)
    scatter(at, total, boxes, rs_sems, lambda b: dot(att_ref[span(b, rows)], wo_ref[...]))
    middle = x_ref[...].astype(F32) + total[...]
    middle_ref[...] = middle
    buf[block_of(at)] = (unit_of(middle)[0] * gain_mid_ref[...]).astype(LOW)
    gather(at, buf, ag_sems, lambda b: up_block(b, buf, f_ref, hidden_ref, one_ref, two_ref))
    copy = save(buf, nmid_ref, sem)
    copy.start()
    scatter(at, total, boxes, rs_sems, lambda b: dot(hidden_ref[span(b, rows)], f_ref[2]), copy)
    out = (middle_ref[...] + total[...]).astype(LOW)
    out_ref[...] = out
    buf[block_of(at)] = (unit_of(out.astype(F32))[0] * gain_in_ref[...]).astype(LOW)
    gather(at, buf, ag_sems, lambda b: project_block(b, buf, w_ref, cos_ref, sin_ref, mix_ref, qkv_ref))
    copy = save(buf, normed_ref, sem)
    copy.start()
    copy.wait()


def down_back(
    at, top, buf, total, boxes, ag_sems, rs_sems, sem, f_ref, one_ref, two_ref, wo_ref, gain_ref, middle_ref,
    dgate_ref, dup_ref, dmid_ref, gain_grad_ref, dout_ref, top_all_ref, dmid_all_ref,
):
    rows = buf.shape[1]
    buf[block_of(at)] = top.astype(LOW)

    def hidden_back(b):
        here = span(b, rows)
        grad = dot(buf[b], f_ref[2], NT)
        dgate_ref[here] = (grad * one_ref[here].astype(F32)).astype(LOW)
        dup_ref[here] = (grad * two_ref[here].astype(F32)).astype(LOW)

    gather(at, buf, ag_sems, hidden_back)
    copy = save(buf, top_all_ref, sem)
    copy.start()

    def partial(b):
        here = span(b, rows)
        return dot(dgate_ref[here], f_ref[0]) + dot(dup_ref[here], f_ref[1])

    scatter(at, total, boxes, rs_sems, partial, copy)
    grad, gain_grad = back_of(total[...], middle_ref[...], gain_ref[...])
    gain_grad_ref[...] = gain_grad
    grad = grad + top
    dmid_ref[...] = grad
    buf[block_of(at)] = grad.astype(LOW)

    def out_back(b):
        dout_ref[:, span(b, rows)] = dot(wo_ref[...], buf[b], NT).astype(LOW)

    gather(at, buf, ag_sems, out_back)
    copy = save(buf, dmid_all_ref, sem)
    copy.start()
    copy.wait()


def turn_kernel(
    att_ref, x_ref, wo_ref, f_ref, gain_ref, top_ref,
    out_ref, hidden_ref, dgate_ref, dup_ref, dmid_ref, gain_grad_ref, dout_ref, nmid_ref, top_all_ref, dmid_all_ref,
    buf, total, own, out_c, in_c, rin, middle_ref, one_ref, two_ref, ag_sems, rs_sems, sem,
):
    at = spot()
    rows = x_ref.shape[0]
    greet(at)
    boxes = (own, out_c, in_c, rin)
    scatter(at, total, boxes, rs_sems, lambda b: dot(att_ref[span(b, rows)], wo_ref[...]))
    middle = x_ref[...].astype(F32) + total[...]
    middle_ref[...] = middle
    buf[block_of(at)] = (unit_of(middle)[0] * gain_ref[...]).astype(LOW)
    gather(at, buf, ag_sems, lambda b: up_block(b, buf, f_ref, hidden_ref, one_ref, two_ref))
    copy = save(buf, nmid_ref, sem)
    copy.start()
    scatter(at, total, boxes, rs_sems, lambda b: dot(hidden_ref[span(b, rows)], f_ref[2]), copy)
    out_ref[...] = (middle_ref[...] + total[...]).astype(LOW)
    down_back(
        at, top_ref[...].astype(F32), buf, total, boxes, ag_sems, rs_sems, sem, f_ref, one_ref, two_ref, wo_ref,
        gain_ref, middle_ref, dgate_ref, dup_ref, dmid_ref, gain_grad_ref, dout_ref, top_all_ref, dmid_all_ref,
    )


def input_back(at, dqkv_ref, w_ref, x_ref, gain_ref, dmid_ref, gain_grad_ref, total, boxes, rs_sems):
    rows = total.shape[0]
    scatter(at, total, boxes, rs_sems, lambda b: dot(dqkv_ref[:, span(b, rows)], w_ref[...], TN))
    grad, gain_grad = back_of(total[...], x_ref[...].astype(F32), gain_ref[...])
    gain_grad_ref[...] = gain_grad
    return grad + dmid_ref[...]


def lower_kernel(
    dqkv_ref, x_ref, w_ref, gain_in_ref, dmid_above_ref, f_ref, one_ref, two_ref, wo_ref, gain_mid_ref, middle_ref,
    grad_ref, gain_in_grad_ref, dgate_ref, dup_ref, dmid_ref, gain_mid_grad_ref, dout_ref, top_all_ref, dmid_all_ref,
    buf, total, own, out_c, in_c, rin, ag_sems, rs_sems, sem,
):
    at = spot()
    greet(at)
    boxes = (own, out_c, in_c, rin)
    grad = input_back(at, dqkv_ref, w_ref, x_ref, gain_in_ref, dmid_above_ref, gain_in_grad_ref, total, boxes, rs_sems)
    grad_ref[...] = grad
    down_back(
        at, grad_ref[...], buf, total, boxes, ag_sems, rs_sems, sem, f_ref, one_ref, two_ref, wo_ref, gain_mid_ref,
        middle_ref, dgate_ref, dup_ref, dmid_ref, gain_mid_grad_ref, dout_ref, top_all_ref, dmid_all_ref,
    )


def last_kernel(
    dqkv_ref, x_ref, w_ref, gain_ref, dmid_ref, grad_ref, gain_grad_ref, total, own, out_c, in_c, rin, rs_sems
):
    at = spot()
    greet(at)
    boxes = (own, out_c, in_c, rin)
    grad_ref[...] = input_back(at, dqkv_ref, w_ref, x_ref, gain_ref, dmid_ref, gain_grad_ref, total, boxes, rs_sems)


VMEM_SPEC = pl.BlockSpec(memory_space=pltpu.VMEM)
ANY_SPEC = pl.BlockSpec(memory_space=pl.ANY)


def links():
    dma = pltpu.SemaphoreType.DMA
    return (dma((3, 8)), dma((3, 8)), dma((8,)), dma((8,)))


def sum_boxes(rows, width):
    return [
        pltpu.VMEM((rows, width), F32),
        pltpu.VMEM((7, rows, width), LOW),
        pltpu.VMEM((8, rows, width), LOW),
        pltpu.VMEM((8, rows, width), LOW),
        pltpu.VMEM((7, rows, width), LOW),
    ]


def reach(kernel, number, args, outs, scratch, name):
    return pl.pallas_call(
        kernel,
        out_shape=[jax.ShapeDtypeStruct(shape, dtype) for shape, dtype, _ in outs],
        in_specs=[VMEM_SPEC] * len(args),
        out_specs=[ANY_SPEC if far else VMEM_SPEC for _, _, far in outs],
        scratch_shapes=scratch,
        compiler_params=pltpu.CompilerParams(
            collective_id=number, has_side_effects=True, vmem_limit_bytes=VMEM_BYTES
        ),
        name=name,
    )(*args)


def head_homes(at, j):
    y, x, c, h, p = at
    return ((j % 2, j // 2, j % 2, h, p), (1 - j % 2, j // 2, j % 2, 1 - h, p))


def shard_homes(at):
    y, x, c, h, p = at
    half = flip(h, far_role(at))
    return [(layer, (layer, i // 2, i % 2, half, p)) for layer in range(2) for i in range(4)]


def weights_kernel(a_ref, f_ref, a_all, f_all, send, recv, local):
    at = spot()
    y, x, c, h, p = at
    s = 2 * x + c
    near = 1 - far_role(at)
    barrier = pltpu.get_barrier_semaphore()
    mine = []
    for layer, home in shard_homes(at):
        is_me = near * (1 - flip(y, layer)) * (1 - jnp.minimum(jnp.abs(s - (2 * home[1] + home[2])), 1))
        mine.append(is_me)

        @pl.when(is_me == 0)
        def _():
            pl.semaphore_signal(barrier, inc=1, device_id=device(home), device_id_type=MESH_ID)

    pl.semaphore_wait(barrier, 8 - near)
    wide = a_ref.shape[-1]
    cols = pl.ds(pl.multiple_of(s * wide, wide), wide)

    def pair(j):
        heads, units = pl.ds(j * HS, HS), pl.ds(j * (f_ref.shape[1] // 4), f_ref.shape[1] // 4)
        return ((a_ref.at[:, heads], a_all.at[y, :, :, cols]), (f_ref.at[:, units], f_all.at[y, :, :, cols]))

    for other in (1, 0):
        for j in range(4):
            home = head_homes(at, j)[other]
            for i, (src, dst) in enumerate(pair(j)):
                index = 4 * other + j
                copy = remote(src, dst, send.at[i, index], recv.at[i, y, s], home)
                if other:
                    copy.start()
                else:
                    is_me = near * (1 - jnp.minimum(jnp.abs(s - j), 1))

                    @pl.when(is_me == 0)
                    def _():
                        copy.start()

                    @pl.when(is_me == 1)
                    def _():
                        pltpu.make_async_copy(src, dst, local.at[i]).start()

    for layer in range(2):
        for k in range(4):
            is_me = mine[4 * layer + k]
            place = pl.ds(k * wide, wide)
            for i, all_ref in enumerate((a_all, f_all)):
                dst = all_ref.at[layer, :, :, place]

                @pl.when(is_me == 0)
                def _():
                    remote(dst, dst, send.at[i, 0], recv.at[i, layer, k], at).wait_recv()

                @pl.when(is_me == 1)
                def _():
                    pltpu.make_async_copy(dst, dst, local.at[i]).wait()

    for other in (1, 0):
        for j in range(4):
            for i, (src, dst) in enumerate(pair(j)):
                copy = remote(src, dst, send.at[i, 4 * other + j], recv.at[i, y, s], at)
                if other:
                    copy.wait_send()
                else:
                    is_me = near * (1 - jnp.minimum(jnp.abs(s - j), 1))

                    @pl.when(is_me == 0)
                    def _():
                        copy.wait_send()


def grads_kernel(a_ref, f_ref, a_in, f_in, send, recv, local):
    at = spot()
    y, x, c, h, p = at
    s = 2 * x + c
    near = 1 - far_role(at)
    wide = a_in.shape[-1]
    barrier = pltpu.get_barrier_semaphore()
    for other in (0, 1):
        for j in range(4):
            home = head_homes(at, j)[other]
            if other:
                pl.semaphore_signal(barrier, inc=1, device_id=device(home), device_id_type=MESH_ID)
            else:

                @pl.when(near * (1 - jnp.minimum(jnp.abs(s - j), 1)) == 0)
                def _():
                    pl.semaphore_signal(barrier, inc=1, device_id=device(home), device_id_type=MESH_ID)

    pl.semaphore_wait(barrier, 8 - near)
    role = far_role(at)
    for n, (layer, home) in enumerate(shard_homes(at)):
        k = 2 * home[1] + home[2]
        is_me = near * (1 - flip(y, layer)) * (1 - jnp.minimum(jnp.abs(s - k), 1))
        for i, (ref, into) in enumerate(((a_ref, a_in), (f_ref, f_in))):
            src, dst = ref.at[layer, :, :, pl.ds(k * wide, wide)], into.at[role, s]
            copy = remote(src, dst, send.at[i, n], recv.at[i, role, s], home)

            @pl.when(is_me == 0)
            def _():
                copy.start()

            @pl.when(is_me == 1)
            def _():
                pltpu.make_async_copy(src, dst, local.at[i]).start()

    for other in (0, 1):
        for j in range(4):
            for i, into in enumerate((a_in, f_in)):
                dst = into.at[other, j]
                arrival = remote(dst, dst, send.at[i, 0], recv.at[i, other, j], at)
                if other:
                    arrival.wait_recv()
                else:
                    is_me = near * (1 - jnp.minimum(jnp.abs(s - j), 1))

                    @pl.when(is_me == 0)
                    def _():
                        arrival.wait_recv()

                    @pl.when(is_me == 1)
                    def _():
                        pltpu.make_async_copy(dst, dst, local.at[i]).wait()

    for n, (layer, home) in enumerate(shard_homes(at)):
        k = 2 * home[1] + home[2]
        is_me = near * (1 - flip(y, layer)) * (1 - jnp.minimum(jnp.abs(s - k), 1))
        for i, (ref, into) in enumerate(((a_ref, a_in), (f_ref, f_in))):

            @pl.when(is_me == 0)
            def _():
                src, dst = ref.at[layer, :, :, pl.ds(k * wide, wide)], into.at[0, 0]
                remote(src, dst, send.at[i, n], recv.at[i, 0, 0], at).wait_send()


def attend_kernel(bounds, qkv_ref, start_ref, att_ref, flat_ref, lse_ref, key_n, val_t, *, bq, bk):
    qi = pl.program_id(0)
    length = qkv_ref.shape[1]

    @pl.when(qi == 0)
    def _():
        for i in range(length // bk):
            key_n[i * bk : (i + 1) * bk] = qkv_ref[HS : 2 * HS, i * bk : (i + 1) * bk].astype(F32).T.astype(LOW)
        val_t[:HS] = qkv_ref[2 * HS :]
        tail = lax.broadcasted_iota(jnp.int32, (16, length), 0)
        val_t[HS:] = jnp.where(tail == 0, 1.0, 0.0).astype(LOW)

    cols = span(qi, bq)
    query = qkv_ref[:HS, cols]
    start_row = start_ref[:, cols]
    place = qi * bq + lax.broadcasted_iota(jnp.int32, (1, bq), 1)

    def step(masked, kb, state):
        largest, summed = state
        scores = dot(key_n[span(kb, bk)], query)
        if masked:
            keys = kb * bk + lax.broadcasted_iota(jnp.int32, (bk, 1), 0)
            allowed = (keys <= place) & (keys >= start_row)
            scores = jnp.where(allowed, scores, NEGATIVE)
        newest = jnp.maximum(largest, jnp.max(scores, axis=0, keepdims=True))
        weights = jnp.exp(scores - newest)
        if masked:
            weights = jnp.where(allowed, weights, 0.0)
        summed = summed * jnp.exp(largest - newest) + dot(val_t[:, span(kb, bk)], weights.astype(LOW))
        return (newest, summed)

    state = (jnp.full((1, bq), NEGATIVE, F32), jnp.zeros((HS + 16, bq), F32))
    lo, mid, far, hi = (bounds[i, qi] for i in range(4))
    state = lax.fori_loop(lo, mid, functools.partial(step, True), state)
    state = lax.fori_loop(mid, far, functools.partial(step, False), state)
    largest, summed = lax.fori_loop(far, hi, functools.partial(step, True), state)
    totals = summed[HS : HS + 1]
    attended = summed[:HS] / totals
    att_ref[:, cols] = attended
    flat_ref[span(qi, bq)] = attended.T.astype(LOW)
    lse_ref[:, cols] = largest + jnp.log(totals)


def attend(qkv, start_row, bq, bk):
    length = qkv.shape[1]
    blocks = length // bq
    first = jnp.arange(blocks, dtype=jnp.int32) * bq
    final = first + bq - 1
    hi = final // bk + 1
    lo = start_row[0][first] // bk
    mid = jnp.clip(-(-start_row[0][final] // bk), lo, hi)
    far = jnp.maximum((first + 1) // bk, mid)
    whole = lambda shape: pl.BlockSpec(shape, lambda i, b: (0, 0))
    return pl.pallas_call(
        functools.partial(attend_kernel, bq=bq, bk=bk),
        out_shape=[
            jax.ShapeDtypeStruct((HS, length), F32),
            jax.ShapeDtypeStruct((length, HS), LOW),
            jax.ShapeDtypeStruct((1, length), F32),
        ],
        grid_spec=pltpu.PrefetchScalarGridSpec(
            num_scalar_prefetch=1,
            grid=(blocks,),
            in_specs=[whole(qkv.shape), whole(start_row.shape)],
            out_specs=[whole((HS, length)), whole((length, HS)), whole((1, length))],
            scratch_shapes=[pltpu.VMEM((length, HS), LOW), pltpu.VMEM((HS + 16, length), LOW)],
        ),
        compiler_params=pltpu.CompilerParams(vmem_limit_bytes=VMEM_BYTES),
        name="attend",
    )(jnp.stack([lo, mid, far, hi]), qkv, start_row)


def attend_back_kernel(
    bounds, qkv_ref, start_ref, att_ref, lse_ref, dout_ref, cos_ref, sin_ref, *rest, bq, bk, first
):
    if first:
        extra_ref, dqkv_ref, key_n, val_n, query_n, dout_n, delta, dq = rest
    else:
        dqkv_ref, send_ref, key_n, val_n, query_n, dout_n, delta, dq = rest
    ki = pl.program_id(0)
    length = qkv_ref.shape[1]
    half = HS // 2

    @pl.when(ki == 0)
    def _():
        for i in range(length // bk):
            part = slice(i * bk, (i + 1) * bk)
            query_n[part] = qkv_ref[:HS, part].astype(F32).T.astype(LOW)
            key_n[part] = qkv_ref[HS : 2 * HS, part].astype(F32).T.astype(LOW)
            val_n[part] = qkv_ref[2 * HS :, part].astype(F32).T.astype(LOW)
            dout_n[part] = dout_ref[:, part].astype(F32).T.astype(LOW)
        delta[...] = jnp.sum(dout_ref[...].astype(F32) * att_ref[...], axis=0, keepdims=True)
        dq[...] = jnp.zeros_like(dq)

    rows = span(ki, bk)
    key, value, key_t = key_n[rows], val_n[rows], qkv_ref[HS : 2 * HS, rows]
    keys = ki * bk + lax.broadcasted_iota(jnp.int32, (bk, 1), 0)

    def step(masked, qb, state):
        dk, dv = state
        cols = span(qb, bq)
        scores = dot(key, qkv_ref[:HS, cols])
        weights = jnp.exp(scores - lse_ref[:, cols])
        if masked:
            place = qb * bq + lax.broadcasted_iota(jnp.int32, (1, bq), 1)
            allowed = (keys <= place) & (keys >= start_ref[:, cols])
            weights = jnp.where(allowed, weights, 0.0)
        along = dot(value, dout_ref[:, cols])
        ds = (weights * (along - delta[:, cols])).astype(LOW)
        dv = dv + dot(weights.astype(LOW), dout_n[cols])
        dk = dk + dot(ds, query_n[cols])
        dq[:, cols] += dot(key_t, ds)
        return (dk, dv)

    state = (jnp.zeros((bk, HS), F32), jnp.zeros((bk, HS), F32))
    lo, mid, far, hi = (bounds[i, ki] for i in range(4))
    state = lax.fori_loop(lo, mid, functools.partial(step, True), state)
    state = lax.fori_loop(mid, far, functools.partial(step, False), state)
    dk, dv = lax.fori_loop(far, hi, functools.partial(step, True), state)
    dk, dv = dk.T, dv.T
    a, b = turned(dk[:half], dk[half:], cos_ref[:, rows], -sin_ref[:, rows])
    dqkv_ref[HS : HS + half, rows] = a.astype(LOW)
    dqkv_ref[HS + half : 2 * HS, rows] = b.astype(LOW)
    if first:
        dqkv_ref[2 * HS :, rows] = (dv + extra_ref[:, rows]).astype(LOW)
    else:
        dqkv_ref[2 * HS :, rows] = (0.5 * dv).astype(LOW)
        send_ref[:, rows] = 0.5 * dv

    @pl.when(ki == pl.num_programs(0) - 1)
    def _():
        scale = HS**-0.5
        a, b = turned(dq[:half] * scale, dq[half:] * scale, cos_ref[...], -sin_ref[...])
        dqkv_ref[:half] = a.astype(LOW)
        dqkv_ref[half:HS] = b.astype(LOW)


def attend_back(qkv, start_row, end_row, attended, lse, dout, tables, extra, bq, bk):
    length = qkv.shape[1]
    blocks = length // bk
    first = jnp.arange(blocks, dtype=jnp.int32) * bk
    final = first + bk - 1
    lo = first // bq
    hi = -(-end_row[0][final] // bq)
    mid = jnp.minimum(-(-final // bq), hi)
    far = jnp.maximum(jnp.minimum(end_row[0][first] // bq, hi), mid)
    whole = lambda shape: pl.BlockSpec(shape, lambda i, b: (0, 0))
    args = [qkv, start_row, attended, lse, dout, *tables]
    outs = [jax.ShapeDtypeStruct(qkv.shape, LOW)]
    if extra is None:
        outs.append(jax.ShapeDtypeStruct((HS, length), F32))
    else:
        args.append(extra)
    return pl.pallas_call(
        functools.partial(attend_back_kernel, bq=bq, bk=bk, first=extra is not None),
        out_shape=outs,
        grid_spec=pltpu.PrefetchScalarGridSpec(
            num_scalar_prefetch=1,
            grid=(blocks,),
            in_specs=[whole(arg.shape) for arg in args],
            out_specs=[whole(out.shape) for out in outs],
            scratch_shapes=[pltpu.VMEM((length, HS), LOW)] * 4
            + [pltpu.VMEM((1, length), F32), pltpu.VMEM((HS, length), F32)],
        ),
        compiler_params=pltpu.CompilerParams(vmem_limit_bytes=VMEM_BYTES),
        name="attend_back",
    )(jnp.stack([lo, mid, far, hi]), *args)


def number_of(y, s, z):
    return (y * 4 + s) * 4 + z


def far_pairs():
    return [
        (number_of(y, s, z), number_of(y, s, (z + 2) % 4))
        for y in range(2)
        for s in range(4)
        for z in range(4)
        if (y + s) % 2
    ]


def home_pairs(layer, micro):
    pairs = []
    for y in range(2):
        for s in range(4):
            for z in (2 * micro, 2 * micro + 1):
                lane = (z + 2) % 4 if (y + s) % 2 else z
                pairs.append((number_of(y, s, z), number_of(layer, s, lane)))
    return pairs


AXES = ("section", "seq", "tensor")


def to_home(values, layer):
    return [lax.ppermute(values, AXES, home_pairs(layer, micro)) for micro in range(2)]


def on_grid(
    inputs, cotangent, lengths, w_query, w_key, w_value, w_out, w_gate, w_up, w_down, attn_gain, mlp_gain
):
    at = spot()
    y, x, c, half, p = at
    far = far_role(at) == 1
    rows, width = inputs.shape[1:]
    length = 16 * rows
    units = w_gate.shape[2] // 4
    both = jnp.stack([lax.dynamic_index_in_dim(array, 1 - half, 0, keepdims=False) for array in (inputs, cotangent)])
    swapped = lax.ppermute(both, AXES, far_pairs())
    own_in = jnp.where(far, swapped[0], lax.dynamic_index_in_dim(inputs, half, 0, keepdims=False))
    own_top = jnp.where(far, swapped[1], lax.dynamic_index_in_dim(cotangent, half, 0, keepdims=False))
    length_row = lax.dynamic_index_in_dim(lengths, half, 0, keepdims=False)
    places = jnp.arange(length, dtype=jnp.int32)
    segment, within = doc_table(length_row, places)
    start_row = (places - within)[None]
    ends = jnp.cumsum(length_row)
    member = segment[None, :] == jnp.arange(length_row.shape[0], dtype=jnp.int32)[:, None]
    end_row = jnp.sum(jnp.where(member, ends[:, None], 0), axis=0)[None].astype(jnp.int32)
    frequency = jnp.exp(jnp.arange(HS // 2, dtype=F32) * (-math.log(10000.0) / (HS // 2)))
    angles = within.astype(F32)[None, :] * frequency[:, None]
    tables = (jnp.cos(angles), jnp.sin(angles))
    a_own = jnp.stack([w_query[0].T, w_key[0].T, w_value[0].T, w_out[0]])
    f_own = jnp.stack([w_gate[0].T, w_up[0].T, w_down[0]])
    a_all, f_all = pl.pallas_call(
        weights_kernel,
        out_shape=[
            jax.ShapeDtypeStruct((2, 4, HS, width), LOW),
            jax.ShapeDtypeStruct((2, 3, units, width), LOW),
        ],
        in_specs=[ANY_SPEC] * 2,
        out_specs=[ANY_SPEC] * 2,
        scratch_shapes=[
            pltpu.SemaphoreType.DMA((2, 8)),
            pltpu.SemaphoreType.DMA((2, 2, 4)),
            pltpu.SemaphoreType.DMA((2,)),
        ],
        compiler_params=pltpu.CompilerParams(collective_id=0, has_side_effects=True),
        name="weights",
    )(a_own, f_own)
    gains = lax.all_gather(jnp.concatenate([attn_gain, mlp_gain]), "section", axis=0, tiled=False)
    gain_in, gain_mid = [gains[i, 0:1] for i in range(2)], [gains[i, 1:2] for i in range(2)]
    w_in = [a_all[i, :3].reshape(3 * HS, width) for i in range(2)]
    w_back = [a_all[i, 3] for i in range(2)]
    f_w = [f_all[i] for i in range(2)]
    buf = [pltpu.VMEM((16, rows, width), LOW)]
    boxes = sum_boxes(rows, width)
    sem = [pltpu.SemaphoreType.DMA]
    every = ((16, rows, width), LOW, True)
    turned_out = ((3 * HS, length), LOW, False)
    hidden_out = ((length, units), LOW, False)
    block_out = ((rows, width), F32, False)
    low_out = ((rows, width), LOW, False)
    gain_out = ((1, width), F32, False)
    dout_out = ((HS, length), LOW, False)

    qkv0, normed0 = reach(
        first_kernel, 1, [own_in, gain_in[0], w_in[0], *tables], [turned_out, every], buf + [links()] + sem, "first"
    )
    att0, flat0, lse0 = attend(qkv0, start_row, 512, 512)
    mid0, out0, hid0, one0, two0, qkv1, nmid0, normed1 = reach(
        middle_kernel,
        2,
        [flat0, own_in, w_back[0], f_w[0], gain_mid[0], gain_in[1], w_in[1], *tables, qkv0[2 * HS :]],
        [block_out, low_out, hidden_out, hidden_out, hidden_out, turned_out, every, every],
        buf + boxes + [links(), links()] + sem,
        "middle",
    )
    att1, flat1, lse1 = attend(qkv1, start_row, 512, 512)
    out1, hid1, dgate1, dup1, dmid1, gmid1, dout1, nmid1, top1, dmid_all1 = reach(
        turn_kernel,
        3,
        [flat1, out0, w_back[1], f_w[1], gain_mid[1], own_top],
        [low_out, hidden_out, hidden_out, hidden_out, block_out, gain_out, dout_out, every, every, every],
        buf
        + boxes
        + [pltpu.VMEM((rows, width), F32), pltpu.VMEM((length, units), LOW), pltpu.VMEM((length, units), LOW)]
        + [links(), links()]
        + sem,
        "turn",
    )
    dqkv1, extra = attend_back(qkv1, start_row, end_row, att1, lse1, dout1, tables, None, 512, 512)
    grad1, gin1, dgate0, dup0, dmid0, gmid0, dout0, top0, dmid_all0 = reach(
        lower_kernel,
        4,
        [dqkv1, out0, w_in[1], gain_in[1], dmid1, f_w[0], one0, two0, w_back[0], gain_mid[0], mid0],
        [block_out, gain_out, hidden_out, hidden_out, block_out, gain_out, dout_out, every, every],
        buf + boxes + [links(), links()] + sem,
        "lower",
    )
    (dqkv0,) = attend_back(qkv0, start_row, end_row, att0, lse0, dout0, tables, extra, 512, 512)
    grad0, gin0 = reach(
        last_kernel,
        5,
        [dqkv0, own_in, w_in[0], gain_in[0], dmid0],
        [block_out, gain_out],
        boxes + [links()],
        "last",
    )
    a_grads, f_grads = [], []
    for dqkv, normed, flat, dmid_all, dgate, dup, hid, nmid, top in (
        (dqkv0, normed0, flat0, dmid_all0, dgate0, dup0, hid0, nmid0, top0),
        (dqkv1, normed1, flat1, dmid_all1, dgate1, dup1, hid1, nmid1, top1),
    ):
        normed, dmid_all, nmid, top = (array.reshape(length, width) for array in (normed, dmid_all, nmid, top))
        grad_in = product(dqkv, normed).reshape(3, HS, width)
        a_grads.append(jnp.concatenate([grad_in, inner_rows(flat, dmid_all)[None]]).astype(LOW))
        f_grads.append(
            jnp.stack([inner_rows(dgate, nmid), inner_rows(dup, nmid), inner_rows(hid, top)]).astype(LOW)
        )
    a_in, f_in = pl.pallas_call(
        grads_kernel,
        out_shape=[
            jax.ShapeDtypeStruct((2, 4, 4, HS, width // 4), LOW),
            jax.ShapeDtypeStruct((2, 4, 3, units, width // 4), LOW),
        ],
        in_specs=[ANY_SPEC] * 2,
        out_specs=[ANY_SPEC] * 2,
        scratch_shapes=[
            pltpu.SemaphoreType.DMA((2, 8)),
            pltpu.SemaphoreType.DMA((2, 2, 4)),
            pltpu.SemaphoreType.DMA((2,)),
        ],
        compiler_params=pltpu.CompilerParams(collective_id=6, has_side_effects=True),
        name="grads",
    )(jnp.stack(a_grads), jnp.stack(f_grads))
    a_sum = jnp.sum(a_in.astype(F32), axis=0)
    f_sum = jnp.sum(f_in.astype(F32), axis=0)
    a_sum = jnp.transpose(a_sum, (1, 0, 2, 3)).reshape(4, 4 * HS, width // 4)
    f_sum = jnp.transpose(f_sum, (1, 0, 2, 3)).reshape(3, 4 * units, width // 4)
    on_first = y == 0
    outs = [to_home(out0, 0), to_home(out1, 1)]
    layer_out = jnp.stack([jnp.where(on_first, outs[0][m], outs[1][m]) for m in range(2)])
    grads = [to_home(grad0.astype(LOW), 0), to_home(grad1.astype(LOW), 1)]
    input_grad = jnp.stack([jnp.where(on_first, grads[0][m], grads[1][m]) for m in range(2)]).astype(F32)
    gain_grads = lax.psum(jnp.concatenate([gin0, gin1, gmid0, gmid1]), AXES)
    share = width // 16
    first_col = (4 * (2 * x + c) + 2 * half + p) * share
    gain_share = lax.dynamic_slice_in_dim(gain_grads, first_col, share, 1)
    gain_in_share = jnp.where(on_first, gain_share[0:1], gain_share[1:2])
    gain_mid_share = jnp.where(on_first, gain_share[2:3], gain_share[3:4])
    return (
        layer_out[None],
        input_grad[None],
        a_sum[0].T[None],
        a_sum[1].T[None],
        a_sum[2].T[None],
        a_sum[3][None],
        f_sum[0].T[None],
        f_sum[1].T[None],
        f_sum[2][None],
        gain_in_share,
        gain_mid_share,
    )


def solution(mesh):
    in_specs = (
        P(None, ("seq", "tensor"), None),
        P(None, ("seq", "tensor"), None),
        P(),
        P("section", "seq", "tensor"),
        P("section", "seq", "tensor"),
        P("section", "seq", "tensor"),
        P("section", "tensor", "seq"),
        P("section", "seq", "tensor"),
        P("section", "seq", "tensor"),
        P("section", "tensor", "seq"),
        P("section", None),
        P("section", None),
    )
    out_specs = (
        P("section", None, ("seq", "tensor"), None),
        P("section", None, ("seq", "tensor"), None),
        P("section", "seq", "tensor"),
        P("section", "seq", "tensor"),
        P("section", "seq", "tensor"),
        P("section", "tensor", "seq"),
        P("section", "seq", "tensor"),
        P("section", "seq", "tensor"),
        P("section", "tensor", "seq"),
        P("section", ("seq", "tensor")),
        P("section", ("seq", "tensor")),
    )
    grid = (mesh.shape["section"], mesh.shape["seq"], mesh.shape["tensor"]) == (2, 4, 4)
    return jax.shard_map(
        on_grid if grid else on_device, mesh=mesh, in_specs=in_specs, out_specs=out_specs, check_vma=False
    )
```

```python
import functools
import math

import jax
import jax.numpy as jnp
from jax import lax
from jax.experimental import pallas as pl
from jax.experimental.pallas import tpu as pltpu
from jax.sharding import PartitionSpec as P

HS = 64


EPSILON = 1e-05
NEGATIVE = -1e30


def shifted(shard, axis, by):
    peers = lax.axis_size(axis)
    pairs = [(i, i + by) for i in range(peers) if 0 <= i + by < peers]
    return lax.ppermute(shard, axis, pairs)


def product(left, right):
    return jnp.dot(left, right, preferred_element_type=jnp.float32)


def inner_rows(left, right):
    return lax.dot_general(
        left, right, (((0,), (0,)), ((), ())), preferred_element_type=jnp.float32
    )


def against(left, right):
    return lax.dot_general(
        left, right, (((1,), (1,)), ((), ())), preferred_element_type=jnp.float32
    )


def doc_table(length_row, places):
    doc_ends = jnp.cumsum(length_row)
    doc_starts = doc_ends - length_row
    segment = jnp.sum((places[:, None] >= doc_ends[None, :]).astype(jnp.int32), axis=1)
    member = segment[:, None] == jnp.arange(length_row.shape[0], dtype=jnp.int32)[None, :]
    offset = jnp.sum(jnp.where(member, doc_starts[None, :], 0), axis=1)
    return (segment, places - offset)


def rotate(matrix, within, direction):
    row_count = matrix.shape[0]
    head_count = matrix.shape[1] // HS
    half_size = HS // 2
    frequency = jnp.exp(jnp.arange(half_size, dtype=jnp.float32) * (-math.log(10000.0) / half_size))
    angles = within.astype(jnp.float32)[:, None] * frequency[None, :]
    cosine = jnp.cos(angles)[:, None, :]
    sine_part = direction * jnp.sin(angles)[:, None, :]
    paired = matrix.reshape(row_count, head_count, 2, half_size)
    former = paired[:, :, 0, :]
    latter = paired[:, :, 1, :]
    turned = jnp.stack(
        [former * cosine - latter * sine_part, latter * cosine + former * sine_part], axis=2
    )
    return turned.reshape(row_count, head_count * HS)


def norm_rows(values, gain_row):
    inverse = lax.rsqrt(jnp.mean(values * values, axis=-1, keepdims=True) + EPSILON)
    unit_rows = values * inverse
    return (unit_rows, inverse, (unit_rows * gain_row).astype(jnp.bfloat16))


def norm_back(grad_normed, unit_rows, inverse, gain_row):
    shaped = grad_normed * gain_row
    inner = jnp.mean(shaped * unit_rows, axis=-1, keepdims=True)
    return (inverse * (shaped - unit_rows * inner), jnp.sum(grad_normed * unit_rows, axis=0))


def spread(values):
    return lax.all_gather(values, "tensor", axis=0, tiled=True)


def fold_rows(values):
    return lax.psum_scatter(
        values.astype(jnp.bfloat16), "tensor", scatter_dimension=0, tiled=True
    ).astype(jnp.float32)


def allowed_mask(places, segment, key_places, key_segment):
    return (key_places[None, :] <= places[:, None]) & (key_segment[None, :] == segment[:, None])


def project(normed_all, matrices, within, mixin, on_first):
    query_rows = rotate(product(normed_all, matrices[0]), within, 1.0).astype(jnp.bfloat16)
    key_rows = rotate(product(normed_all, matrices[1]), within, 1.0).astype(jnp.bfloat16)
    value_raw = product(normed_all, matrices[2])
    value_rows = jnp.where(
        on_first, value_raw, 0.5 * value_raw + 0.5 * mixin.astype(jnp.float32)
    ).astype(jnp.bfloat16)
    return (query_rows, key_rows, value_rows)


def cycle_attend(query_rows, key_rows, value_rows, places, segment, length_row):
    row_count = query_rows.shape[0]
    head_count = query_rows.shape[1] // HS
    query_heads = query_rows.reshape(row_count, head_count, HS)
    largest = jnp.full((head_count, row_count), NEGATIVE, jnp.float32)
    piece_keys = lax.all_gather(key_rows, "seq", axis=0, tiled=True)
    piece_values = lax.all_gather(value_rows, "seq", axis=0, tiled=True)
    piece_rows = piece_keys.shape[0]
    key_places = jnp.arange(piece_rows, dtype=jnp.int32)
    key_segment = doc_table(length_row, key_places)[0]
    allowed = allowed_mask(places, segment, key_places, key_segment)
    scores = jnp.einsum(
        "qhd,khd->hqk",
        query_heads,
        piece_keys.reshape(piece_rows, head_count, HS),
        preferred_element_type=jnp.float32,
    ) * HS ** (-0.5)
    masked = jnp.where(allowed[None], scores, NEGATIVE)
    newest = jnp.maximum(largest, jnp.max(masked, axis=2))
    weights = jnp.where(allowed[None], jnp.exp(masked - newest[:, :, None]), 0.0)
    totals = jnp.sum(weights, axis=2)
    summed = jnp.einsum(
        "hqk,khd->hqd",
        weights.astype(jnp.bfloat16),
        piece_values.reshape(piece_rows, head_count, HS),
        preferred_element_type=jnp.float32,
    )
    largest, totals, summed = (newest, totals, summed)
    attended = summed / totals[:, :, None]
    return jnp.transpose(attended, (1, 0, 2)).reshape(row_count, head_count * HS)


def forward_layer(residual, mixin, on_first, matrices, gain_pair, places, length_row):
    segment, within = doc_table(length_row, places)
    normed_in = norm_rows(residual, gain_pair[0])[2]
    normed_all = spread(normed_in)
    query_rows, key_rows, value_rows = project(normed_all, matrices, within, mixin, on_first)
    attended = cycle_attend(query_rows, key_rows, value_rows, places, segment, length_row)
    middle = residual + fold_rows(product(attended.astype(jnp.bfloat16), matrices[3]))
    normed_mid = norm_rows(middle, gain_pair[1])[2]
    normed_mid_all = spread(normed_mid)
    gate_rows = product(normed_mid_all, matrices[4])
    up_rows = product(normed_mid_all, matrices[5])
    hidden = (jax.nn.silu(gate_rows) * up_rows).astype(jnp.bfloat16)
    return (middle + fold_rows(product(hidden, matrices[6])), value_rows)


def backward_layer(
    residual, mixin, grad_top, extra_values, on_first, matrices, gain_pair, places, length_row
):
    segment, within = doc_table(length_row, places)
    unit_in, inverse_in, normed_in = norm_rows(residual, gain_pair[0])
    normed_all = spread(normed_in)
    query_rows, key_rows, value_rows = project(normed_all, matrices, within, mixin, on_first)
    all_keys, all_values = (
        lax.all_gather(key_rows, "seq", axis=0, tiled=True),
        lax.all_gather(value_rows, "seq", axis=0, tiled=True),
    )
    row_count = query_rows.shape[0]
    head_count = query_rows.shape[1] // HS
    total_rows = all_keys.shape[0]
    block_count = total_rows // row_count
    query_heads = query_rows.reshape(row_count, head_count, HS)
    key_blocks = all_keys.reshape(block_count, row_count, head_count, HS)
    value_blocks = all_values.reshape(block_count, row_count, head_count, HS)
    block_numbers = jnp.arange(block_count, dtype=jnp.int32)

    def block_scores(block_number, block_keys):
        key_places = block_number * row_count + jnp.arange(row_count, dtype=jnp.int32)
        key_segment = doc_table(length_row, key_places)[0]
        allowed = allowed_mask(places, segment, key_places, key_segment)
        scores = jnp.einsum(
            "qhd,khd->hqk", query_heads, block_keys, preferred_element_type=jnp.float32
        ) * HS ** (-0.5)
        return (allowed, jnp.where(allowed[None], scores, NEGATIVE))

    def first_pass(running, block_item):
        largest, totals, summed = running
        block_number, block_keys, block_values = block_item
        allowed, masked = block_scores(block_number, block_keys)
        newest = jnp.maximum(largest, jnp.max(masked, axis=2))
        rescale = jnp.exp(largest - newest)
        weights = jnp.where(allowed[None], jnp.exp(masked - newest[:, :, None]), 0.0)
        totals = totals * rescale + jnp.sum(weights, axis=2)
        summed = summed * rescale[:, :, None] + jnp.einsum(
            "hqk,khd->hqd",
            weights.astype(jnp.bfloat16),
            block_values,
            preferred_element_type=jnp.float32,
        )
        return ((newest, totals, summed), None)

    start_state = (
        jnp.full((head_count, row_count), NEGATIVE, jnp.float32),
        jnp.zeros((head_count, row_count), jnp.float32),
        jnp.zeros((head_count, row_count, HS), jnp.float32),
    )
    (largest, totals, summed), _ = lax.scan(
        first_pass, start_state, (block_numbers, key_blocks, value_blocks)
    )
    attended = summed / totals[:, :, None]
    attended_low = (
        jnp.transpose(attended, (1, 0, 2)).reshape(row_count, head_count * HS).astype(jnp.bfloat16)
    )
    middle = residual + fold_rows(product(attended_low, matrices[3]))
    unit_mid, inverse_mid, normed_mid = norm_rows(middle, gain_pair[1])
    normed_mid_all = spread(normed_mid)
    gate_rows = product(normed_mid_all, matrices[4])
    up_rows = product(normed_mid_all, matrices[5])
    sigmoid_gate = jax.nn.sigmoid(gate_rows)
    activated = gate_rows * sigmoid_gate
    hidden = (activated * up_rows).astype(jnp.bfloat16)
    grad_top_all = spread(grad_top.astype(jnp.bfloat16))
    grad_w_down = inner_rows(hidden, grad_top_all)
    grad_hidden = against(grad_top_all, matrices[6])
    grad_gate = (
        grad_hidden * up_rows * sigmoid_gate * (1.0 + gate_rows * (1.0 - sigmoid_gate))
    ).astype(jnp.bfloat16)
    grad_up = (grad_hidden * activated).astype(jnp.bfloat16)
    grad_w_gate = inner_rows(normed_mid_all, grad_gate)
    grad_w_up = inner_rows(normed_mid_all, grad_up)
    grad_normed_mid = fold_rows(against(grad_gate, matrices[4]) + against(grad_up, matrices[5]))
    grad_middle, grad_gain_mid = norm_back(grad_normed_mid, unit_mid, inverse_mid, gain_pair[1])
    grad_middle = grad_middle + grad_top
    grad_middle_all = spread(grad_middle.astype(jnp.bfloat16))
    grad_w_out = inner_rows(attended_low, grad_middle_all)
    grad_attended = against(grad_middle_all, matrices[3]).astype(jnp.bfloat16)
    grad_heads = jnp.transpose(grad_attended.reshape(row_count, head_count, HS), (1, 0, 2))
    delta = jnp.sum(grad_heads.astype(jnp.float32) * attended, axis=2)
    scaled_grad = grad_heads.astype(jnp.float32) / totals[:, :, None]
    scaled_high = scaled_grad.astype(jnp.bfloat16)
    scaled_rest = (scaled_grad - scaled_high.astype(jnp.float32)).astype(jnp.bfloat16)
    inverse_totals = 1.0 / totals[:, :, None]

    def second_pass(grad_sum, block_item):
        block_number, block_keys, block_values = block_item
        allowed, masked = block_scores(block_number, block_keys)
        weights = jnp.where(allowed[None], jnp.exp(masked - largest[:, :, None]), 0.0)
        low_weights = weights.astype(jnp.bfloat16)
        along = jnp.einsum(
            "hqd,khd->hqk", grad_heads, block_values, preferred_element_type=jnp.float32
        )
        grad_scores = (weights * inverse_totals * (along - delta[:, :, None])).astype(jnp.bfloat16)
        grad_sum = grad_sum + jnp.einsum(
            "hqk,khd->qhd", grad_scores, block_keys, preferred_element_type=jnp.float32
        ) * HS ** (-0.5)
        block_key_grad = jnp.einsum(
            "hqk,qhd->khd", grad_scores, query_heads, preferred_element_type=jnp.float32
        ) * HS ** (-0.5)
        block_value_grad = jnp.einsum(
            "hqk,hqd->khd", low_weights, scaled_high, preferred_element_type=jnp.float32
        ) + jnp.einsum("hqk,hqd->khd", low_weights, scaled_rest, preferred_element_type=jnp.float32)
        return (grad_sum, (block_key_grad, block_value_grad))

    grad_queries, (grad_keys, grad_values) = lax.scan(
        second_pass,
        jnp.zeros((row_count, head_count, HS), jnp.float32),
        (block_numbers, key_blocks, value_blocks),
    )
    own_keys, own_values = (
        lax.psum_scatter(
            grad_keys.reshape(total_rows, head_count * HS).astype(jnp.bfloat16),
            "seq",
            scatter_dimension=0,
            tiled=True,
        ).astype(jnp.float32),
        lax.psum_scatter(
            grad_values.reshape(total_rows, head_count * HS).astype(jnp.bfloat16),
            "seq",
            scatter_dimension=0,
            tiled=True,
        ).astype(jnp.float32),
    )
    grad_value_raw = jnp.where(on_first, own_values + extra_values, 0.5 * own_values).astype(
        jnp.bfloat16
    )
    send_values = 0.5 * own_values
    grad_query_raw = rotate(grad_queries.reshape(row_count, head_count * HS), within, -1.0).astype(
        jnp.bfloat16
    )
    grad_key_raw = rotate(own_keys, within, -1.0).astype(jnp.bfloat16)
    grad_w_query = inner_rows(normed_all, grad_query_raw)
    grad_w_key = inner_rows(normed_all, grad_key_raw)
    grad_w_value = inner_rows(normed_all, grad_value_raw)
    grad_normed_in = fold_rows(
        against(grad_query_raw, matrices[0])
        + against(grad_key_raw, matrices[1])
        + against(grad_value_raw, matrices[2])
    )
    grad_in, grad_gain_in = norm_back(grad_normed_in, unit_in, inverse_in, gain_pair[0])
    weight_terms = (
        grad_w_query,
        grad_w_key,
        grad_w_value,
        grad_w_out,
        grad_w_gate,
        grad_w_up,
        grad_w_down,
    )
    return (grad_in + grad_middle, send_values, weight_terms, (grad_gain_in, grad_gain_mid))


def on_device(
    inputs,
    cotangent,
    lengths,
    w_query,
    w_key,
    w_value,
    w_out,
    w_gate,
    w_up,
    w_down,
    attn_gain,
    mlp_gain,
):
    section_index = lax.axis_index("section")
    on_first = section_index == 0
    micro_count = inputs.shape[0]
    local_rows = inputs.shape[1]
    model_width = inputs.shape[2]
    group_rows = local_rows * lax.axis_size("tensor")
    head_width = w_query.shape[2]
    row_values = local_rows * model_width
    places = lax.axis_index("seq") * group_rows + jnp.arange(group_rows, dtype=jnp.int32)
    gain_pair = (attn_gain[0], mlp_gain[0])
    gathered = (
        lax.all_gather(w_query[0], "seq", axis=0, tiled=True),
        lax.all_gather(w_key[0], "seq", axis=0, tiled=True),
        lax.all_gather(w_value[0], "seq", axis=0, tiled=True),
        lax.all_gather(w_out[0], "seq", axis=1, tiled=True),
        lax.all_gather(w_gate[0], "seq", axis=0, tiled=True),
        lax.all_gather(w_up[0], "seq", axis=0, tiled=True),
        lax.all_gather(w_down[0], "seq", axis=1, tiled=True),
    )
    recv_rows = jnp.zeros((local_rows, model_width), jnp.bfloat16)
    recv_values = jnp.zeros((group_rows, head_width), jnp.bfloat16)
    kept_inputs = jnp.zeros((micro_count, local_rows, model_width), jnp.bfloat16)
    kept_values = jnp.zeros((micro_count, group_rows, head_width), jnp.bfloat16)
    kept_outputs = jnp.zeros((micro_count, local_rows, model_width), jnp.bfloat16)
    for moment in range(micro_count + 1):
        which = moment - section_index
        usable = (which >= 0) & (which < micro_count)
        slot_index = jnp.clip(which, 0, micro_count - 1)
        own_rows = lax.dynamic_index_in_dim(inputs, slot_index, 0, keepdims=False)
        layer_in = jnp.where(on_first, own_rows, recv_rows)
        length_row = lax.dynamic_index_in_dim(lengths, slot_index, 0, keepdims=False)
        result, value_rows = forward_layer(
            layer_in.astype(jnp.float32),
            recv_values,
            on_first,
            gathered,
            gain_pair,
            places,
            length_row,
        )
        result_low = result.astype(jnp.bfloat16)
        kept_inputs = jnp.where(
            usable,
            lax.dynamic_update_index_in_dim(kept_inputs, layer_in, slot_index, 0),
            kept_inputs,
        )
        kept_values = jnp.where(
            usable,
            lax.dynamic_update_index_in_dim(kept_values, recv_values, slot_index, 0),
            kept_values,
        )
        kept_outputs = jnp.where(
            usable,
            lax.dynamic_update_index_in_dim(kept_outputs, result_low, slot_index, 0),
            kept_outputs,
        )
        if moment < micro_count:
            packed = jnp.concatenate([result_low.reshape(-1), value_rows.reshape(-1)])
            arrived = shifted(packed, "section", 1)
            recv_rows = arrived[:row_values].reshape(local_rows, model_width)
            recv_values = arrived[row_values:].reshape(group_rows, head_width)
    grad_rows_in = jnp.zeros((local_rows, model_width), jnp.float32)
    grad_values_in = jnp.zeros((group_rows, head_width), jnp.float32)
    grad_inputs = jnp.zeros((micro_count, local_rows, model_width), jnp.float32)
    weight_sums = tuple((jnp.zeros(matrix.shape, jnp.float32) for matrix in gathered))
    share_sums = (
        jnp.zeros(w_query[0].shape, jnp.float32),
        jnp.zeros(w_key[0].shape, jnp.float32),
        jnp.zeros(w_value[0].shape, jnp.float32),
        jnp.zeros(w_out[0].shape, jnp.float32),
        jnp.zeros(w_gate[0].shape, jnp.float32),
        jnp.zeros(w_up[0].shape, jnp.float32),
        jnp.zeros(w_down[0].shape, jnp.float32),
    )
    gain_sums = (jnp.zeros((model_width,), jnp.float32), jnp.zeros((model_width,), jnp.float32))
    for moment in range(micro_count + 1):
        which = moment - (1 - section_index)
        usable = (which >= 0) & (which < micro_count)
        slot_index = jnp.clip(which, 0, micro_count - 1)
        matrices = (
            lax.all_gather(w_query[0], "seq", axis=0, tiled=True),
            lax.all_gather(w_key[0], "seq", axis=0, tiled=True),
            lax.all_gather(w_value[0], "seq", axis=0, tiled=True),
            lax.all_gather(w_out[0], "seq", axis=1, tiled=True),
            lax.all_gather(w_gate[0], "seq", axis=0, tiled=True),
            lax.all_gather(w_up[0], "seq", axis=0, tiled=True),
            lax.all_gather(w_down[0], "seq", axis=1, tiled=True),
        )
        layer_in = lax.dynamic_index_in_dim(kept_inputs, slot_index, 0, keepdims=False).astype(
            jnp.float32
        )
        mixin = lax.dynamic_index_in_dim(kept_values, slot_index, 0, keepdims=False)
        length_row = lax.dynamic_index_in_dim(lengths, slot_index, 0, keepdims=False)
        own_grad = lax.dynamic_index_in_dim(cotangent, slot_index, 0, keepdims=False).astype(
            jnp.float32
        )
        grad_top = jnp.where(usable, jnp.where(on_first, grad_rows_in, own_grad), 0.0)
        extra_values = jnp.where(usable & on_first, grad_values_in, 0.0)
        grad_in, send_values, weight_terms, gain_terms = backward_layer(
            layer_in,
            mixin,
            grad_top,
            extra_values,
            on_first,
            matrices,
            gain_pair,
            places,
            length_row,
        )
        gain_sums = (gain_sums[0] + gain_terms[0], gain_sums[1] + gain_terms[1])
        weight_sums = tuple((total + term for total, term in zip(weight_sums, weight_terms)))
        grad_inputs = jnp.where(
            usable,
            lax.dynamic_update_index_in_dim(grad_inputs, grad_in, slot_index, 0),
            grad_inputs,
        )
        if moment < micro_count:
            packed = jnp.concatenate([grad_in.reshape(-1), send_values.reshape(-1)])
            arrived = shifted(packed.astype(jnp.bfloat16), "section", -1).astype(packed.dtype)
            grad_rows_in = arrived[:row_values].reshape(local_rows, model_width)
            grad_values_in = arrived[row_values:].reshape(group_rows, head_width)
    share_sums = (
        lax.psum_scatter(
            weight_sums[0].astype(jnp.bfloat16), "seq", scatter_dimension=0, tiled=True
        ).astype(jnp.float32),
        lax.psum_scatter(
            weight_sums[1].astype(jnp.bfloat16), "seq", scatter_dimension=0, tiled=True
        ).astype(jnp.float32),
        lax.psum_scatter(
            weight_sums[2].astype(jnp.bfloat16), "seq", scatter_dimension=0, tiled=True
        ).astype(jnp.float32),
        lax.psum_scatter(
            weight_sums[3].astype(jnp.bfloat16), "seq", scatter_dimension=1, tiled=True
        ).astype(jnp.float32),
        lax.psum_scatter(
            weight_sums[4].astype(jnp.bfloat16), "seq", scatter_dimension=0, tiled=True
        ).astype(jnp.float32),
        lax.psum_scatter(
            weight_sums[5].astype(jnp.bfloat16), "seq", scatter_dimension=0, tiled=True
        ).astype(jnp.float32),
        lax.psum_scatter(
            weight_sums[6].astype(jnp.bfloat16), "seq", scatter_dimension=1, tiled=True
        ).astype(jnp.float32),
    )
    gain_shares = (
        lax.psum_scatter(gain_sums[0], ("seq", "tensor"), scatter_dimension=0, tiled=True),
        lax.psum_scatter(gain_sums[1], ("seq", "tensor"), scatter_dimension=0, tiled=True),
    )
    return (
        kept_outputs[None],
        grad_inputs[None],
        share_sums[0][None],
        share_sums[1][None],
        share_sums[2][None],
        share_sums[3][None],
        share_sums[4][None],
        share_sums[5][None],
        share_sums[6][None],
        gain_shares[0][None],
        gain_shares[1][None],
    )


MESH_ID = pl.DeviceIdType.MESH
LOW = jnp.bfloat16
F32 = jnp.float32
ORDERS = ((1, 2, 4), (2, 4, 1), (4, 1, 2))
LEVELS = ((0,), (1, 2, 4), (3, 5, 6), (7,))
NT = (((1,), (1,)), ((), ()))
NN = (((1,), (0,)), ((), ()))
TN = (((0,), (0,)), ((), ()))
VMEM_BYTES = 52 * 2**20


def dot(left, right, dims=NN):
    return lax.dot_general(left, right, dims, preferred_element_type=F32)


def flip(value, bit):
    if isinstance(bit, int):
        return 1 - value if bit else value
    return value + bit - 2 * value * bit


def spot():
    y, s, z = lax.axis_index("section"), lax.axis_index("seq"), lax.axis_index("tensor")
    return (y, lax.div(s, 2), lax.rem(s, 2), lax.div(z, 2), lax.rem(z, 2))


def device(at):
    y, x, c, h, p = at
    return (y, 2 * x + c, 2 * h + p)


def moved(at, mask, core=0):
    y, x, c, h, p = at
    if isinstance(mask, int):
        bits = (mask & 1, (mask >> 1) & 1, mask >> 2)
    else:
        bits = (lax.rem(mask, 2), lax.rem(lax.div(mask, 2), 2), lax.div(mask, 4))
    return (flip(y, bits[1]), flip(x, bits[0]), flip(c, core), h, flip(p, bits[2]))


def far_role(at):
    return flip(at[0], at[2])


def lane_of(at):
    return 2 * flip(at[3], far_role(at)) + at[4]


def block_of(at):
    return (2 * at[1] + at[2]) * 4 + lane_of(at)


def level_mask(level, i):
    if level == 0:
        return 0 * i
    if level == 1:
        return 1 + i + lax.div(i, 2)
    if level == 2:
        return 3 + i + lax.div(i + 1, 2)
    return 0 * i + 7


def last_bit(k, mask):
    return [bit for bit in ORDERS[k] if bit & mask][-1]


def parts_of(rows):
    units = rows // 16
    small = units // 3
    sizes = (16 * (units - 2 * small), 16 * small, 16 * small)
    return ((0, sizes[0]), (sizes[0], sizes[1]), (sizes[0] + sizes[1], sizes[2]))


def remote(src, dst, send, recv, at):
    return pltpu.make_async_remote_copy(
        src_ref=src, dst_ref=dst, send_sem=send, recv_sem=recv, device_id=device(at), device_id_type=MESH_ID
    )


def greet(at, *pushes, peers=()):
    count = 4 + len(peers)
    for mask, core in ((1, 0), (2, 0), (4, 0), (0, 1)):
        signal(moved(at, mask, core))
    for peer in peers:
        signal(peer)
    for push in pushes:
        count = count + push.greet()
    pl.semaphore_wait(pltpu.get_barrier_semaphore(), count)


def gather(at, buf, sems, on_block, keep=None, ready=None):
    send, recv, csend, crecv = sems
    parts = parts_of(buf.shape[1])

    def rows(mask, k, core=0):
        return buf.at[block_of(moved(at, mask, core)), pl.ds(*parts[k])]

    def hop(k, target):
        bit = last_bit(k, target)
        ref = rows(target ^ bit, k)
        return remote(ref, ref, send.at[k, target], recv.at[k, target], moved(at, bit))

    def arrival(k, target):
        ref = rows(target, k)
        return remote(ref, ref, send.at[k, target], recv.at[k, target], moved(at, last_bit(k, target)))

    def across(mask, core=0):
        ref = buf.at[block_of(moved(at, mask, core))]
        return remote(ref, ref, csend.at[mask], crecv.at[mask], moved(at, 0, 1))

    def visit(level, core):
        def one(i, none):
            b = block_of(moved(at, level_mask(level, i), core))
            if keep is not None:
                pltpu.make_async_copy(buf.at[b], keep[0].at[b], keep[1].at[b]).start()
            on_block(b)
            return none

        lax.fori_loop(0, len(LEVELS[level]), one, 0)

    for i in range(2):
        for k in range(3):
            hop(k, ORDERS[k][i]).start()
        if i == 0:
            across(0).start()
    if ready is not None:
        ready()
    visit(0, 0)
    across(0, 1).wait_recv()
    visit(0, 1)
    for k in range(3):
        first, second, third = ORDERS[k]
        arrival(k, first).wait_recv()
        hop(k, first | second).start()
    for k in range(3):
        first, second, third = ORDERS[k]
        hop(k, third).start()
        hop(k, first | third).start()
    for k in range(3):
        first, second, third = ORDERS[k]
        arrival(k, second).wait_recv()
        hop(k, second | third).start()
    for k in range(3):
        first, second, third = ORDERS[k]
        arrival(k, first | second).wait_recv()
        hop(k, 7).start()
    for level in (1, 2, 3):
        for mask in LEVELS[level]:
            for k in range(3):
                first, second, third = ORDERS[k]
                if mask not in (first, second, first | second):
                    arrival(k, mask).wait_recv()
            across(mask).start()
        visit(level, 0)
        for mask in LEVELS[level]:
            across(mask, 1).wait_recv()
        visit(level, 1)
    for k in range(3):
        for target in range(1, 8):
            hop(k, target).wait_send()
    for mask in range(8):
        across(mask).wait_send()


def kept(buf, keep):
    for b in range(16):
        pltpu.make_async_copy(buf.at[b], keep[0].at[b], keep[1].at[b]).wait()


def scatter(at, total, boxes, sems, partial, before_last=None):
    out_c, in_c, rin = boxes
    send, recv, csend, crecv = sems
    parts = parts_of(total.shape[0])

    def hop(k, target):
        rows = pl.ds(*parts[k])
        return remote(
            in_c.at[target, rows],
            rin.at[target - 1, rows],
            send.at[k, target],
            recv.at[k, target],
            moved(at, last_bit(k, target)),
        )

    def across(mask):
        return remote(out_c.at[mask], in_c.at[mask], csend.at[mask], crecv.at[mask], moved(at, 0, 1))

    def emit(level):
        def one(i, none):
            mask = level_mask(level, i)
            out_c[mask] = partial(block_of(moved(at, mask, 1))).astype(LOW)
            return none

        lax.fori_loop(0, len(LEVELS[level]), one, 0)
        for mask in LEVELS[level]:
            across(mask).start()

    def settle(level):
        for mask in LEVELS[level]:
            across(mask).wait_recv()

        def one(i, none):
            mask = level_mask(level, i)
            mine = partial(block_of(moved(at, mask))) + in_c[mask].astype(F32)
            if level == 0:
                total[...] = mine
            else:
                in_c[mask] = mine.astype(LOW)
            return none

        lax.fori_loop(0, len(LEVELS[level]), one, 0)
        for mask in LEVELS[level]:
            for k in range(3):
                if mask & ORDERS[k][2]:
                    hop(k, mask).start()

    def arrived(k, target):
        hop(k, target).wait_recv()
        return rin[target - 1, pl.ds(*parts[k])].astype(F32)

    emit(3)
    emit(2)
    settle(3)
    settle(2)
    emit(1)
    settle(1)
    if before_last is not None:
        before_last()
    emit(0)
    settle(0)
    for mask_of in (lambda a, b: a | b, lambda a, b: b):
        for k in range(3):
            first, second, third = ORDERS[k]
            mask, rows = mask_of(first, second), pl.ds(*parts[k])
            in_c[mask, rows] = (in_c[mask, rows].astype(F32) + arrived(k, mask | third)).astype(LOW)
            hop(k, mask).start()
    for k in range(3):
        first, second, third = ORDERS[k]
        rows = pl.ds(*parts[k])
        in_c[first, rows] = (
            in_c[first, rows].astype(F32) + arrived(k, first | third) + arrived(k, first | second)
        ).astype(LOW)
        hop(k, first).start()
    for k in range(3):
        first, second, third = ORDERS[k]
        rows = pl.ds(*parts[k])
        total[rows] = total[rows] + arrived(k, third) + arrived(k, second) + arrived(k, first)
    for k in range(3):
        for target in range(1, 8):
            hop(k, target).wait_send()
    for mask in range(8):
        across(mask).wait_send()


def same(a, b):
    return 1 - jnp.minimum(jnp.abs(a - b), 1)


def signal(at):
    pl.semaphore_signal(pltpu.get_barrier_semaphore(), inc=1, device_id=device(at), device_id_type=MESH_ID)


class ToHeads:
    def __init__(self, at, layer, piece, place, sems):
        self.at, self.layer, self.piece, self.place = at, layer, piece, place
        self.send, self.recv, self.local = sems
        y, x, c, h, p = at
        self.s = 2 * x + c
        self.sends = same(y, layer)
        self.near = 1 - far_role(at)

    def is_me(self, j):
        return self.sends * self.near * same(self.s, j)

    def greet(self):
        half = flip(self.at[3], far_role(self.at))
        for k in range(4):

            @pl.when(self.is_me(k) == 0)
            def _(k=k):
                signal((self.layer, k // 2, k % 2, half, self.at[4]))

        return self.sends * (8 - self.near)

    def home(self, j, other):
        h, p = self.at[3], self.at[4]
        return (1 - j % 2, j // 2, j % 2, 1 - h, p) if other else (j % 2, j // 2, j % 2, h, p)

    def copy(self, j, other):
        return remote(
            self.piece(j), self.place(self.s), self.send.at[4 * other + j], self.recv.at[self.s], self.home(j, other)
        )

    def start(self):
        for j in range(4):

            @pl.when(self.sends == 1)
            def _(j=j):
                self.copy(j, 1).start()

        for j in range(4):

            @pl.when(self.sends - self.is_me(j) == 1)
            def _(j=j):
                self.copy(j, 0).start()

            @pl.when(self.is_me(j) == 1)
            def _(j=j):
                pltpu.make_async_copy(self.piece(j), self.place(j), self.local).start()

    def finish(self):
        for k in range(4):
            dst = self.place(k)

            @pl.when(self.is_me(k) == 0)
            def _(k=k, dst=dst):
                remote(dst, dst, self.send.at[0], self.recv.at[k], self.at).wait_recv()

            @pl.when(self.is_me(k) == 1)
            def _(k=k, dst=dst):
                pltpu.make_async_copy(self.piece(k), dst, self.local).wait()

        for j in range(4):

            @pl.when(self.sends == 1)
            def _(j=j):
                self.copy(j, 1).wait_send()

            @pl.when(self.sends - self.is_me(j) == 1)
            def _(j=j):
                self.copy(j, 0).wait_send()


class ToShards:
    def __init__(self, at, layer, piece, place, sems):
        self.at, self.layer, self.piece, self.place = at, layer, piece, place
        self.send, self.recv, self.local = sems
        y, x, c, h, p = at
        self.s = 2 * x + c
        self.gets = same(y, layer)
        self.role = far_role(at)

    def is_me(self, k):
        return self.gets * (1 - self.role) * same(self.s, k)

    def greet(self):
        h, p = self.at[3], self.at[4]
        for j in range(4):

            @pl.when(self.gets == 1)
            def _(j=j):
                signal((1 - j % 2, j // 2, j % 2, 1 - h, p))

            @pl.when(self.gets - self.is_me(j) == 1)
            def _(j=j):
                signal((j % 2, j // 2, j % 2, h, p))

        return 4 - self.gets * (1 - self.role)

    def copy(self, k):
        home = (self.layer, k // 2, k % 2, flip(self.at[3], self.role), self.at[4])
        return remote(
            self.piece(k), self.place(self.role, self.s), self.send.at[k], self.recv.at[self.role, self.s], home
        )

    def start(self):
        for k in range(4):

            @pl.when(self.is_me(k) == 0)
            def _(k=k):
                self.copy(k).start()

            @pl.when(self.is_me(k) == 1)
            def _(k=k):
                pltpu.make_async_copy(self.piece(k), self.place(0, k), self.local).start()

    def finish(self):
        for role in range(2):
            for j in range(4):
                dst = self.place(role, j)
                comes = self.gets if role else self.gets - self.is_me(j)

                @pl.when(comes == 1)
                def _(role=role, j=j, dst=dst):
                    remote(dst, dst, self.send.at[0], self.recv.at[role, j], self.at).wait_recv()

        for k in range(4):

            @pl.when(self.is_me(k) == 0)
            def _(k=k):
                self.copy(k).wait_send()

            @pl.when(self.is_me(k) == 1)
            def _(k=k):
                pltpu.make_async_copy(self.piece(k), self.place(0, k), self.local).wait()


class ToHome:
    def __init__(self, at, layer, block, place, sems):
        self.at, self.layer, self.block, self.place = at, layer, block, place
        self.send, self.recv, self.local = sems
        y, x, c, h, p = at
        self.gets = same(y, layer)
        self.role = far_role(at)
        self.is_me = self.gets * (1 - self.role)

    def holder(self, micro):
        y, x, c, h, p = self.at
        role = flip(h, micro)
        return (flip(role, c), x, c, micro, p), (1 - role) * self.is_me

    def greet(self):
        for micro in range(2):
            holder, is_me = self.holder(micro)

            @pl.when(self.gets - is_me == 1)
            def _(holder=holder):
                signal(holder)

        return 1 - self.is_me

    def copy(self):
        y, x, c, h, p = self.at
        home = (self.layer, x, c, flip(h, self.role), p)
        return remote(self.block, self.place(h), self.send, self.recv.at[h], home)

    def keep(self):
        return pltpu.make_async_copy(self.block, self.place(self.at[3]), self.local)

    def start(self):
        @pl.when(self.is_me == 0)
        def _():
            self.copy().start()

        @pl.when(self.is_me == 1)
        def _():
            self.keep().start()

    def finish(self):
        for micro in range(2):
            dst = self.place(micro)

            @pl.when(self.gets - self.holder(micro)[1] == 1)
            def _(micro=micro, dst=dst):
                remote(dst, dst, self.send, self.recv.at[micro], self.at).wait_recv()

        @pl.when(self.is_me == 0)
        def _():
            self.copy().wait_send()

        @pl.when(self.is_me == 1)
        def _():
            self.keep().wait()


def home_sems():
    dma = pltpu.SemaphoreType.DMA
    return (dma, dma((2,)), dma)


def head_sems():
    dma = pltpu.SemaphoreType.DMA
    return (dma((8,)), dma((4,)), dma)


def shard_sems():
    dma = pltpu.SemaphoreType.DMA
    return (dma((4,)), dma((2, 4)), dma)


def slices(ref, size):
    return lambda j: ref.at[:, pl.ds(j * size, size)]


def columns(ref):
    wide = ref.shape[-1] // 4

    def place(s):
        start = s * wide
        return ref.at[:, :, pl.ds(start if isinstance(s, int) else pl.multiple_of(start, wide), wide)]

    return place


def unit_of(values):
    inverse = lax.rsqrt(jnp.mean(values * values, axis=-1, keepdims=True) + EPSILON)
    return (values * inverse, inverse)


def back_of(grad_normed, values, gain_row):
    unit, inverse = unit_of(values)
    shaped = grad_normed * gain_row
    inner = jnp.mean(shaped * unit, axis=-1, keepdims=True)
    return (inverse * (shaped - unit * inner), jnp.sum(grad_normed * unit, axis=0, keepdims=True))


def span(b, rows):
    return pl.ds(pl.multiple_of(b * rows, rows), rows)


def turned(top, bottom, cosine, sine):
    return (top * cosine - bottom * sine, bottom * cosine + top * sine)


def project_block(b, buf, w_ref, cos_ref, sin_ref, mix_ref, qkv_ref):
    rows, half = buf.shape[1], HS // 2
    cols = span(b, rows)
    raw = dot(w_ref[...], buf[b], NT)
    cosine, sine = cos_ref[:, cols], sin_ref[:, cols]
    for first, scale in ((0, HS**-0.5), (HS, 1.0)):
        a, bb = turned(raw[first : first + half], raw[first + half : first + HS], cosine, sine)
        qkv_ref[first : first + half, cols] = (a.astype(LOW) * scale).astype(LOW)
        qkv_ref[first + half : first + HS, cols] = (bb.astype(LOW) * scale).astype(LOW)
    value = raw[2 * HS :]
    if mix_ref is not None:
        value = 0.5 * value + 0.5 * mix_ref[:, cols].astype(F32)
    qkv_ref[2 * HS :, cols] = value.astype(LOW)


def first_kernel(
    cos_ref, sin_ref, seg_ref, in_ref, a_ref, f_ref, gain_ref,
    qkv_ref, att_ref, flat_ref, lse_ref, x_ref, normed_ref, a0, a1, f0, f1, gains,
    buf, x_here, w_ref, gain_here, key_x, query_x, val_x, scores,
    ag_sems, block_sems, a0_sems, a1_sems, f0_sems, f1_sems, swap, gain_sems, loads,
):
    at = spot()
    y, x, c, h, p = at
    far = far_role(at)
    partner, above = (y, x, c, 1 - h, p), (1 - y, x, c, h, p)
    size = f_ref.shape[1] // 4
    a_pushes = [
        ToHeads(at, layer, slices(a_ref, HS), columns(into), sems)
        for layer, into, sems in ((0, a0, a0_sems), (1, a1, a1_sems))
    ]
    f_pushes = [
        ToHeads(at, layer, slices(f_ref, size), columns(into), sems)
        for layer, into, sems in ((0, f0, f0_sems), (1, f1, f1_sems))
    ]
    greet(at, *a_pushes, *f_pushes, peers=(above, partner))
    swapped = remote(in_ref.at[1 - h], x_here, swap.at[0], swap.at[1], partner)
    stays = pltpu.make_async_copy(in_ref.at[h], x_here, swap.at[2])

    @pl.when(far == 1)
    def _():
        swapped.start()

    @pl.when(far == 0)
    def _():
        stays.start()

    across = remote(gain_ref, gains.at[y], gain_sems.at[0], gain_sems.at[1], above)
    across.start()
    keeps = pltpu.make_async_copy(gain_ref, gains.at[y], gain_sems.at[2])
    keeps.start()
    for push in a_pushes:
        push.start()
    keeps.wait()
    across.wait_send()
    remote(gain_ref, gains.at[1 - y], gain_sems.at[0], gain_sems.at[1], above).wait_recv()
    gain_copy = pltpu.make_async_copy(gains.at[0], gain_here, loads.at[0])
    gain_copy.start()

    @pl.when(far == 1)
    def _():
        swapped.wait()

    @pl.when(far == 0)
    def _():
        stays.wait()

    gain_copy.wait()
    save = pltpu.make_async_copy(x_here, x_ref, loads.at[1])
    save.start()
    buf[block_of(at)] = (unit_of(x_here[...].astype(F32))[0] * gain_here[0:1]).astype(LOW)

    def ready():
        a_pushes[0].finish()
        copies = [pltpu.make_async_copy(a0.at[i], w_ref.at[pl.ds(i * HS, HS)], loads.at[2 + i]) for i in range(3)]
        for copy in copies:
            copy.start()
        for push in f_pushes:
            push.start()
        for copy in copies:
            copy.wait()

    keep = (normed_ref, block_sems)
    gather(at, buf, ag_sems, lambda b: project_block(b, buf, w_ref, cos_ref, sin_ref, None, qkv_ref), keep, ready)
    attend_body(qkv_ref, seg_ref, att_ref, flat_ref, lse_ref, key_x, query_x, val_x, scores)
    kept(buf, keep)
    save.wait()
    a_pushes[1].finish()
    for push in f_pushes:
        push.finish()


def up_block(b, buf, f_ref, hidden_ref, one_ref, two_ref):
    rows = span(b, buf.shape[1])
    x = buf[b]
    gate, up = dot(x, f_ref[0], NT), dot(x, f_ref[1], NT)
    sigmoid = 1.0 / (1.0 + jnp.exp(-gate))
    activated = gate * sigmoid
    hidden_ref[rows] = (activated * up).astype(LOW)
    one_ref[rows] = (up * sigmoid * (1.0 + gate * (1.0 - sigmoid))).astype(LOW)
    two_ref[rows] = activated.astype(LOW)


def middle_kernel(
    att_ref, x_ref, wo_ref, f_ref, gain_mid_ref, gain_in_ref, w_ref, cos_ref, sin_ref, mix_ref,
    middle_ref, out_ref, hidden_ref, one_ref, two_ref, qkv_ref, nmid_ref, normed_ref, home_ref,
    buf, total, out_c, in_c, rin, ag_sems, rs_sems, block_sems, homing,
):
    at = spot()
    rows = x_ref.shape[0]
    push = ToHome(at, 0, out_ref, lambda m: home_ref.at[m], homing)
    greet(at, push)
    boxes = (out_c, in_c, rin)
    scatter(at, total, boxes, rs_sems, lambda b: dot(att_ref[span(b, rows)], wo_ref[...]))
    middle = x_ref[...].astype(F32) + total[...]
    middle_ref[...] = middle
    buf[block_of(at)] = (unit_of(middle)[0] * gain_mid_ref[...]).astype(LOW)
    keep = (nmid_ref, block_sems)
    gather(at, buf, ag_sems, lambda b: up_block(b, buf, f_ref, hidden_ref, one_ref, two_ref), keep)
    scatter(
        at, total, boxes, rs_sems, lambda b: dot(hidden_ref[span(b, rows)], f_ref[2]), lambda: kept(buf, keep)
    )
    out = (middle_ref[...] + total[...]).astype(LOW)
    out_ref[...] = out
    push.start()
    buf[block_of(at)] = (unit_of(out.astype(F32))[0] * gain_in_ref[...]).astype(LOW)
    keep = (normed_ref, block_sems)
    gather(at, buf, ag_sems, lambda b: project_block(b, buf, w_ref, cos_ref, sin_ref, mix_ref, qkv_ref), keep)
    kept(buf, keep)
    push.finish()


def down_back(
    at, top, buf, nmid, total, boxes, ag_sems, rs_sems, f_ref, hidden_ref, one_ref, two_ref, wo_ref, att_ref,
    gain_ref, middle_ref, sums_ref, out_sum_ref,
    dmid_ref, gain_grad_ref, dout_ref, f_grad_ref, out_grad_ref,
):
    rows = buf.shape[1]
    buf[block_of(at)] = top.astype(LOW)
    sums_ref[...] = jnp.zeros_like(sums_ref)
    out_sum_ref[...] = jnp.zeros_like(out_sum_ref)

    def hidden_back(b):
        here = span(b, rows)
        grad = dot(buf[b], f_ref[2], NT)
        one_ref[here] = (grad * one_ref[here].astype(F32)).astype(LOW)
        two_ref[here] = (grad * two_ref[here].astype(F32)).astype(LOW)
        sums_ref[2] += dot(hidden_ref[here], buf[b], TN)

    gather(at, buf, ag_sems, hidden_back)

    def partial(b):
        here = span(b, rows)
        return dot(one_ref[here], f_ref[0]) + dot(two_ref[here], f_ref[1])

    scatter(at, total, boxes, rs_sems, partial)
    grad, gain_grad = back_of(total[...], middle_ref[...], gain_ref[...])
    gain_grad_ref[...] = gain_grad
    grad = grad + top
    dmid_ref[...] = grad
    buf[block_of(at)] = grad.astype(LOW)

    def out_back(b):
        here = span(b, rows)
        dout_ref[:, here] = dot(wo_ref[...], buf[b], NT).astype(LOW)
        out_sum_ref[...] += dot(att_ref[here], buf[b], TN)
        sums_ref[0] += dot(one_ref[here], nmid[b], TN)
        sums_ref[1] += dot(two_ref[here], nmid[b], TN)

    gather(at, buf, ag_sems, out_back)
    f_grad_ref[...] = sums_ref[...].astype(LOW)
    out_grad_ref[...] = out_sum_ref[...].astype(LOW)


def turn_kernel(
    att_ref, x_ref, wo_ref, f_ref, gain_ref, top_ref,
    dmid_ref, gain_grad_ref, dout_ref, f_grad_ref, out_grad_ref, home_ref,
    buf, nmid, out_ref, total, out_c, in_c, rin, middle_ref, hidden_ref, one_ref, two_ref, sums_ref,
    out_sum_ref, ag_sems, rs_sems, homing,
):
    at = spot()
    rows = x_ref.shape[0]
    push = ToHome(at, 1, out_ref, lambda m: home_ref.at[m], homing)
    greet(at, push)
    boxes = (out_c, in_c, rin)
    scatter(at, total, boxes, rs_sems, lambda b: dot(att_ref[span(b, rows)], wo_ref[...]))
    middle = x_ref[...].astype(F32) + total[...]
    middle_ref[...] = middle
    nmid[block_of(at)] = (unit_of(middle)[0] * gain_ref[...]).astype(LOW)
    gather(at, nmid, ag_sems, lambda b: up_block(b, nmid, f_ref, hidden_ref, one_ref, two_ref))
    scatter(at, total, boxes, rs_sems, lambda b: dot(hidden_ref[span(b, rows)], f_ref[2]))
    out_ref[...] = (middle_ref[...] + total[...]).astype(LOW)
    push.start()
    down_back(
        at, top_ref[...].astype(F32), buf, nmid, total, boxes, ag_sems, rs_sems, f_ref, hidden_ref, one_ref, two_ref,
        wo_ref, att_ref, gain_ref, middle_ref, sums_ref, out_sum_ref,
        dmid_ref, gain_grad_ref, dout_ref, f_grad_ref, out_grad_ref,
    )
    push.finish()


def input_back(
    at, dqkv_ref, w_ref, x_ref, gain_ref, dmid_ref, gain_grad_ref, total, boxes, rs_sems, normed, load, sum_ref, after=None
):
    rows = total.shape[0]

    def weight_sum():
        load.wait()
        sum_ref[...] = jnp.zeros_like(sum_ref)

        def one(b, none):
            sum_ref[...] += dot(dqkv_ref[:, span(b, rows)], normed[b])
            return none

        lax.fori_loop(0, 16, one, 0)
        if after is not None:
            after()

    scatter(
        at, total, boxes, rs_sems, lambda b: dot(dqkv_ref[:, span(b, rows)], w_ref[...], TN), weight_sum
    )
    grad, gain_grad = back_of(total[...], x_ref[...].astype(F32), gain_ref[...])
    gain_grad_ref[...] = gain_grad
    return grad + dmid_ref[...]


def lower_kernel(
    dqkv_ref, x_ref, w_ref, gain_in_ref, dmid_above_ref, f_ref, wo_ref, att_ref, gain_mid_ref, middle_ref,
    hidden_far, one_far, two_far, normed_far, nmid_far,
    gain_in_grad_ref, a_grad_ref, dmid_ref, gain_mid_grad_ref, dout_ref, f_grad_ref, out_grad_ref, home_ref,
    buf, nmid, grad_ref, low_ref, total, out_c, in_c, rin, hidden_ref, one_ref, two_ref, sums_ref, out_sum_ref,
    in_sum_ref, ag_sems, rs_sems, loads, homing,
):
    at = spot()
    push = ToHome(at, 1, low_ref, lambda m: home_ref.at[m], homing)
    copies = [
        pltpu.make_async_copy(far, near, loads.at[i])
        for i, (far, near) in enumerate(
            (
                (normed_far, buf),
                (hidden_far, hidden_ref),
                (one_far, one_ref),
                (two_far, two_ref),
                (nmid_far, nmid),
            )
        )
    ]
    for copy in copies:
        copy.start()
    greet(at, push)
    boxes = (out_c, in_c, rin)
    grad = input_back(
        at, dqkv_ref, w_ref, x_ref, gain_in_ref, dmid_above_ref, gain_in_grad_ref, total, boxes, rs_sems, buf,
        copies[0], in_sum_ref,
    )
    grad_ref[...] = grad
    low_ref[...] = grad.astype(LOW)
    push.start()
    a_grad_ref[...] = in_sum_ref[...].astype(LOW)
    for copy in copies[1:]:
        copy.wait()
    down_back(
        at, grad_ref[...], buf, nmid, total, boxes, ag_sems, rs_sems, f_ref, hidden_ref, one_ref, two_ref, wo_ref,
        att_ref, gain_mid_ref, middle_ref, sums_ref, out_sum_ref,
        dmid_ref, gain_mid_grad_ref, dout_ref, f_grad_ref, out_grad_ref,
    )
    push.finish()


def last_kernel(
    dqkv_ref, x_ref, w_ref, gain_ref, dmid_ref, out_grad_ref, gains_ref, normed_far,
    home_ref, a_in, gain_sum,
    buf, total, out_c, in_c, rin, in_sum_ref, a_grad_ref, low_ref, gain_grad_ref, heard, rs_sems, loads, homing,
    a_sems, gain_sems,
):
    at = spot()
    y, x, c, h, p = at
    copy = pltpu.make_async_copy(normed_far, buf, loads.at[0])
    copy.start()
    wide = a_grad_ref.shape[-1] // 4
    shards = ToShards(
        at, 0, lambda k: a_grad_ref.at[:, :, pl.ds(k * wide, wide)], lambda role, j: a_in.at[role, j], a_sems
    )
    push = ToHome(at, 0, low_ref, lambda m: home_ref.at[m], homing)
    peers = [moved(at, 0, 1), moved(at, 1), moved(at, 2), moved(at, 4), (y, x, c, 1 - h, p)]
    greet(at, push, shards, peers=peers[4:])
    boxes = (out_c, in_c, rin)

    def after():
        for i in range(3):
            a_grad_ref[i] = in_sum_ref[i * HS : (i + 1) * HS].astype(LOW)
        a_grad_ref[3] = out_grad_ref[...]
        shards.start()

    grad = input_back(
        at, dqkv_ref, w_ref, x_ref, gain_ref, dmid_ref, gain_grad_ref, total, boxes, rs_sems, buf, copy, in_sum_ref,
        after,
    )
    low_ref[...] = grad.astype(LOW)
    push.start()
    gain_sum[0, 0:1] = gain_grad_ref[...]
    gain_sum[0, 1:4] = gains_ref[...]
    for i, peer in enumerate(peers):
        copy = remote(gain_sum.at[i], heard.at[i], gain_sems.at[0, i], gain_sems.at[1, i], peer)
        copy.start()
        copy.wait()
        gain_sum[i + 1] = gain_sum[i] + heard[i]
    shards.finish()
    push.finish()


VMEM_SPEC = pl.BlockSpec(memory_space=pltpu.VMEM)
ANY_SPEC = pl.BlockSpec(memory_space=pl.ANY)


def links():
    dma = pltpu.SemaphoreType.DMA
    return (dma((3, 8)), dma((3, 8)), dma((8,)), dma((8,)))


def sum_boxes(rows, width):
    return [
        pltpu.VMEM((rows, width), F32),
        pltpu.VMEM((8, rows, width), LOW),
        pltpu.VMEM((8, rows, width), LOW),
        pltpu.VMEM((7, rows, width), LOW),
    ]


def reach(kernel, number, args, outs, scratch, name, far=()):
    return pl.pallas_call(
        kernel,
        out_shape=[jax.ShapeDtypeStruct(shape, dtype) for shape, dtype, _ in outs],
        in_specs=[VMEM_SPEC] * len(args) + [ANY_SPEC] * len(far),
        out_specs=[ANY_SPEC if stays else VMEM_SPEC for _, _, stays in outs],
        scratch_shapes=scratch,
        compiler_params=pltpu.CompilerParams(
            collective_id=number, has_side_effects=number is not None, vmem_limit_bytes=VMEM_BYTES
        ),
        name=name,
    )(*args, *far)


TILE = 512
MORE = 16
DOC_ROOM = 13
FLOOR = -1e20


def one_hot(seg_ref, part):
    rows = lax.broadcasted_iota(jnp.int32, (MORE, TILE), 0)
    return (rows, rows == seg_ref[:, part])


def tiles(length):
    return [slice(i * TILE, (i + 1) * TILE) for i in range(length // TILE)]


def causal():
    return lax.broadcasted_iota(jnp.int32, (TILE, 1), 0) <= lax.broadcasted_iota(jnp.int32, (1, TILE), 1)


def attend_body(qkv_ref, seg_ref, att_ref, flat_ref, lse_ref, key_x, query_x, val_x, scores):
    length = qkv_ref.shape[1]
    for part in tiles(length):
        rows, hot = one_hot(seg_ref, part)
        key = jnp.concatenate([qkv_ref[HS : 2 * HS, part].astype(F32), jnp.where(hot, 1.0, 0.0)])
        key_x[part] = key.T.astype(LOW)
        query_x[:HS, part] = qkv_ref[:HS, part]
        query_x[HS:, part] = jnp.where(hot | (rows >= DOC_ROOM), 0.0, NEGATIVE).astype(LOW)
        val_x[:HS, part] = qkv_ref[2 * HS :, part]
        val_x[HS:, part] = jnp.where(rows == 0, 1.0, 0.0).astype(LOW)

    def query_tile(qi):
        cols = slice(qi * TILE, (qi + 1) * TILE)
        query = query_x[:, cols]

        def ahead(slot, kb):
            scores[slot] = dot(key_x[span(kb, TILE)], query)

        def update(slot, kb, state, diagonal=False):
            largest, summed = state
            found = scores[slot]
            if diagonal:
                found = jnp.where(causal(), found, NEGATIVE)
            newest = jnp.maximum(largest, jnp.max(found, axis=0, keepdims=True))
            weights = jnp.exp(found - newest).astype(LOW)
            summed = summed * jnp.exp(largest - newest) + dot(val_x[:, span(kb, TILE)], weights)
            return (newest, summed)

        def pair(i, state):
            ahead(1, 2 * i + 1)
            state = update(0, 2 * i, state)
            ahead(0, 2 * i + 2)
            return update(1, 2 * i + 1, state)

        state = (jnp.full((1, TILE), FLOOR, F32), jnp.zeros((HS + MORE, TILE), F32))
        ahead(0, 0)
        state = lax.fori_loop(0, qi // 2, pair, state)
        if qi % 2:
            ahead(1, qi)
            state = update(0, qi - 1, state)
        largest, summed = update(qi % 2, qi, state, True)
        totals = summed[HS : HS + 1]
        attended = summed[:HS] / totals
        att_ref[:, cols] = attended
        flat_ref[cols] = attended.T.astype(LOW)
        lse_ref[:, cols] = largest + jnp.log(totals)

    for qi in range(length // TILE):
        query_tile(qi)


def attend_scratch(length):
    return [
        pltpu.VMEM((length, HS + MORE), LOW),
        pltpu.VMEM((HS + MORE, length), LOW),
        pltpu.VMEM((HS + MORE, length), LOW),
        pltpu.VMEM((2, TILE, TILE), F32),
    ]


def three(values):
    high = values.astype(LOW).astype(F32)
    mid = (values - high).astype(LOW).astype(F32)
    return (high, mid, values - high - mid)


def attend_back_body(
    qkv_ref, seg_ref, att_ref, lse_ref, dout_ref, cos_ref, sin_ref, extra_ref, dqkv_ref, send_ref,
    key_x, val_x, query_x, dout_x, dq, scores, along,
):
    length = qkv_ref.shape[1]
    half, count = HS // 2, length // TILE
    for part in tiles(length):
        rows, hot = one_hot(seg_ref, part)
        ones = jnp.where(rows >= DOC_ROOM, 1.0, 0.0)
        key = jnp.concatenate([qkv_ref[HS : 2 * HS, part].astype(F32), jnp.where(hot, 1.0, ones)])
        key_x[part] = key.T.astype(LOW)
        val_x[part] = jnp.concatenate([qkv_ref[2 * HS :, part].astype(F32), ones]).T.astype(LOW)

        def tail(values, rest, rows=rows):
            for i, piece in enumerate(three(values)):
                rest = jnp.where(rows == DOC_ROOM + i, piece, rest)
            return rest.astype(LOW)

        dout = dout_ref[:, part]
        delta = jnp.sum(dout.astype(F32) * att_ref[:, part], axis=0, keepdims=True)
        query_x[:HS, part] = qkv_ref[:HS, part]
        query_x[HS:, part] = tail(-lse_ref[:, part], jnp.where(hot, 0.0, NEGATIVE))
        dout_x[:HS, part] = dout
        dout_x[HS:, part] = tail(-delta, jnp.zeros((MORE, TILE), F32))
    dq[...] = jnp.zeros_like(dq)

    def key_tile(ki):
        here = slice(ki * TILE, (ki + 1) * TILE)
        rest = count - 1 - ki

        def ahead(slot, qb):
            cols = span(qb, TILE)
            scores[slot] = dot(key_x[here], query_x[:, cols])
            along[slot] = dot(val_x[here], dout_x[:, cols])

        def update(slot, qb, state, diagonal=False):
            dk, dv = state
            cols = span(qb, TILE)
            weights = jnp.exp(scores[slot])
            if diagonal:
                weights = jnp.where(causal(), weights, 0.0)
            ds = (weights * along[slot]).astype(LOW)
            dv = dv + dot(dout_x[:HS, cols], weights.astype(LOW), NT)
            dk = dk + dot(query_x[:HS, cols], ds, NT)
            dq[:, cols] += dot(qkv_ref[HS : 2 * HS, here], ds)
            return (dk, dv)

        def pair(i, state):
            qb = ki + 1 + 2 * i
            ahead(0, qb + 1)
            state = update(1, qb, state)
            ahead(1, qb + 2)
            return update(0, qb + 1, state)

        zero = jnp.zeros((HS, TILE), F32)
        ahead(0, ki)
        if rest:
            ahead(1, ki + 1)
        state = update(0, ki, (zero, zero), True)
        state = lax.fori_loop(0, max(0, (rest - 1) // 2), pair, state)
        if rest % 2:
            state = update(1, count - 1, state)
        elif rest:
            ahead(0, count - 1)
            state = update(1, count - 2, state)
            state = update(0, count - 1, state)
        dk, dv = state
        a, b = turned(dk[:half], dk[half:], cos_ref[:, here], -sin_ref[:, here])
        dqkv_ref[HS : HS + half, here] = a.astype(LOW)
        dqkv_ref[HS + half : 2 * HS, here] = b.astype(LOW)
        if send_ref is None:
            dqkv_ref[2 * HS :, here] = (dv + extra_ref[:, here]).astype(LOW)
        else:
            dqkv_ref[2 * HS :, here] = (0.5 * dv).astype(LOW)
            send_ref[:, here] = 0.5 * dv

    for ki in range(count):
        key_tile(ki)
    scale = HS**-0.5
    a, b = turned(dq[:half] * scale, dq[half:] * scale, cos_ref[...], -sin_ref[...])
    dqkv_ref[:half] = a.astype(LOW)
    dqkv_ref[half:HS] = b.astype(LOW)


def attend_back_scratch(length):
    wide = HS + MORE
    return [
        pltpu.VMEM((length, wide), LOW),
        pltpu.VMEM((length, wide), LOW),
        pltpu.VMEM((wide, length), LOW),
        pltpu.VMEM((wide, length), LOW),
        pltpu.VMEM((HS, length), F32),
        pltpu.VMEM((2, TILE, TILE), F32),
        pltpu.VMEM((2, TILE, TILE), F32),
    ]


def attend_back_upper(
    qkv_ref, seg_ref, att_ref, lse_ref, dout_ref, cos_ref, sin_ref, f_grad, dqkv_ref, send_ref, f_in, *rest
):
    *scratch, sems = rest
    at = spot()
    wide = f_grad.shape[-1] // 4
    push = ToShards(
        at, 1, lambda k: f_grad.at[:, :, pl.ds(k * wide, wide)], lambda role, j: f_in.at[role, j], sems
    )
    count = push.greet()
    pl.semaphore_wait(pltpu.get_barrier_semaphore(), count)
    push.start()
    attend_back_body(
        qkv_ref, seg_ref, att_ref, lse_ref, dout_ref, cos_ref, sin_ref, None, dqkv_ref, send_ref, *scratch
    )
    push.finish()


def attend_back_lower(
    qkv_ref, seg_ref, att_ref, lse_ref, dout_ref, cos_ref, sin_ref, extra_ref, f_grad, a_grad,
    dqkv_ref, f_in, a_in, *rest,
):
    *scratch, f_sems, a_sems = rest
    at = spot()
    wide = f_grad.shape[-1] // 4
    pushes = [
        ToShards(
            at,
            layer,
            lambda k, ref=ref: ref.at[:, :, pl.ds(k * wide, wide)],
            lambda role, j, into=into: into.at[role, j],
            sems,
        )
        for layer, ref, into, sems in ((0, f_grad, f_in, f_sems), (1, a_grad, a_in, a_sems))
    ]
    count = pushes[0].greet() + pushes[1].greet()
    pl.semaphore_wait(pltpu.get_barrier_semaphore(), count)
    for push in pushes:
        push.start()
    attend_back_body(
        qkv_ref, seg_ref, att_ref, lse_ref, dout_ref, cos_ref, sin_ref, extra_ref, dqkv_ref, None, *scratch
    )
    for push in pushes:
        push.finish()


def number_of(y, s, z):
    return (y * 4 + s) * 4 + z


def far_pairs():
    return [
        (number_of(y, s, z), number_of(y, s, (z + 2) % 4))
        for y in range(2)
        for s in range(4)
        for z in range(4)
        if (y + s) % 2
    ]


AXES = ("section", "seq", "tensor")


def on_grid(
    inputs, cotangent, lengths, w_query, w_key, w_value, w_out, w_gate, w_up, w_down, attn_gain, mlp_gain
):
    at = spot()
    y, x, c, half, p = at
    far = far_role(at) == 1
    rows, width = inputs.shape[1:]
    length = 16 * rows
    units = w_gate.shape[2] // 4
    length_row = lax.dynamic_index_in_dim(lengths, half, 0, keepdims=False)
    places = jnp.arange(length, dtype=jnp.int32)
    segment, within = doc_table(length_row, places)
    segment = segment[None]
    frequency = jnp.exp(jnp.arange(HS // 2, dtype=F32) * (-math.log(10000.0) / (HS // 2)))
    angles = within.astype(F32)[None, :] * frequency[:, None]
    tables = [jnp.cos(angles), jnp.sin(angles)]
    a_own = jnp.stack([w_query[0].T, w_key[0].T, w_value[0].T, w_out[0]])
    f_own = jnp.stack([w_gate[0].T, w_up[0].T, w_down[0]])
    buf = [pltpu.VMEM((16, rows, width), LOW)]
    boxes = sum_boxes(rows, width)
    dma = pltpu.SemaphoreType.DMA
    every = ((16, rows, width), LOW, True)
    turned_out = ((3 * HS, length), LOW, False)
    hidden_out = ((length, units), LOW, False)
    block_out = ((rows, width), F32, False)
    low_out = ((rows, width), LOW, False)
    gain_out = ((1, width), F32, False)
    dout_out = ((HS, length), LOW, False)
    head_out = ((HS, length), F32, False)
    flat_out = ((length, HS), LOW, False)
    lse_out = ((1, length), F32, False)
    f_out = ((3, units, width), LOW, False)
    wo_out = ((HS, width), LOW, False)
    f_far = ((3, units, width), LOW, True)
    a_far = ((4, HS, width), LOW, True)
    a_shards = ((2, 4, 4, HS, width // 4), LOW, True)
    f_shards = ((2, 4, 3, units, width // 4), LOW, True)
    hidden_scratch = pltpu.VMEM((length, units), LOW)
    f_sum = [pltpu.VMEM((3, units, width), F32), pltpu.VMEM((HS, width), F32)]
    in_sum = [pltpu.VMEM((3 * HS, width), F32)]

    home_out = ((2, rows, width), LOW, True)
    qkv0, att0, flat0, lse0, own_in, normed0, a0, a1, f0, f1, gains = reach(
        first_kernel,
        0,
        [*tables, segment],
        [turned_out, head_out, flat_out, lse_out, ((rows, width), LOW, True), every, a_far, a_far, f_far, f_far]
        + [((2, 2, width), F32, True)],
        buf
        + [pltpu.VMEM((rows, width), LOW), pltpu.VMEM((3 * HS, width), LOW), pltpu.VMEM((2, width), F32)]
        + attend_scratch(length)
        + [links(), dma((16,)), head_sems(), head_sems(), head_sems(), head_sems(), dma((3,)), dma((3,)), dma((5,))],
        "first",
        [inputs, a_own, f_own, jnp.concatenate([attn_gain, mlp_gain])],
    )
    both = lax.dynamic_index_in_dim(cotangent, 1 - half, 0, keepdims=False)
    own_top = jnp.where(
        far,
        lax.ppermute(both, AXES, far_pairs()),
        lax.dynamic_index_in_dim(cotangent, half, 0, keepdims=False),
    )
    gain_in, gain_mid = [gains[i, 0:1] for i in range(2)], [gains[i, 1:2] for i in range(2)]
    w_in = [a[:3].reshape(3 * HS, width) for a in (a0, a1)]
    w_back = [a[3] for a in (a0, a1)]

    mid0, out0, hid0, one0, two0, qkv1, nmid0, normed1, home_out0 = reach(
        middle_kernel,
        2,
        [flat0, own_in, w_back[0], f0, gain_mid[0], gain_in[1], w_in[1], *tables, qkv0[2 * HS :]],
        [block_out, low_out, hidden_out, hidden_out, hidden_out, turned_out, every, every, home_out],
        buf + boxes + [links(), links(), dma((16,)), home_sems()],
        "middle",
    )
    att1, flat1, lse1 = reach(
        attend_body, None, [qkv1, segment], [head_out, flat_out, lse_out], attend_scratch(length), "attend"
    )
    dmid1, gmid1, dout1, f_grad1, wo_grad1, home_out1 = reach(
        turn_kernel,
        3,
        [flat1, out0, w_back[1], f1, gain_mid[1], own_top],
        [block_out, gain_out, dout_out, f_out, wo_out, home_out],
        buf
        + buf
        + [pltpu.VMEM((rows, width), LOW)]
        + boxes
        + [pltpu.VMEM((rows, width), F32)]
        + [hidden_scratch] * 3
        + f_sum
        + [links(), links(), home_sems()],
        "turn",
    )
    dqkv1, extra, f_in1 = reach(
        attend_back_upper,
        9,
        [qkv1, segment, att1, lse1, dout1, *tables],
        [turned_out, head_out, f_shards],
        attend_back_scratch(length) + [shard_sems()],
        "attend_back",
        [f_grad1],
    )
    gin1, in_grad1, dmid0, gmid0, dout0, f_grad0, wo_grad0, home_grad1 = reach(
        lower_kernel,
        4,
        [dqkv1, out0, w_in[1], gain_in[1], dmid1, f0, w_back[0], flat0, gain_mid[0], mid0],
        [gain_out, ((3 * HS, width), LOW, False), block_out, gain_out, dout_out, f_out, wo_out, home_out],
        buf
        + buf
        + [pltpu.VMEM((rows, width), F32), pltpu.VMEM((rows, width), LOW)]
        + boxes
        + [hidden_scratch] * 3
        + f_sum
        + in_sum
        + [links(), links(), dma((5,)), home_sems()],
        "lower",
        [hid0, one0, two0, normed1, nmid0],
    )
    a_grad1 = jnp.concatenate([in_grad1, wo_grad1]).reshape(4, HS, width)
    dqkv0, f_in0, a_in1 = reach(
        attend_back_lower,
        10,
        [qkv0, segment, att0, lse0, dout0, *tables, extra],
        [turned_out, f_shards, a_shards],
        attend_back_scratch(length) + [shard_sems(), shard_sems()],
        "attend_back",
        [f_grad0, a_grad1],
    )
    home_grad0, a_in0, gain_sums = reach(
        last_kernel,
        5,
        [dqkv0, own_in, w_in[0], gain_in[0], dmid0, wo_grad0, jnp.concatenate([gin1, gmid0, gmid1])],
        [home_out, a_shards, ((6, 4, width), F32, False)],
        buf
        + boxes
        + in_sum
        + [pltpu.VMEM((4, HS, width), LOW), pltpu.VMEM((rows, width), LOW), pltpu.VMEM((1, width), F32)]
        + [pltpu.VMEM((5, 4, width), F32)]
        + [links(), dma((1,)), home_sems(), shard_sems(), dma((2, 5))],
        "last",
        [normed0],
    )
    on_first = y == 0
    a_sum = jnp.sum(jnp.where(on_first, a_in0, a_in1).astype(F32), axis=0)
    f_total = jnp.sum(jnp.where(on_first, f_in0, f_in1).astype(F32), axis=0)
    a_sum = jnp.transpose(a_sum, (1, 0, 2, 3)).reshape(4, 4 * HS, width // 4)
    f_total = jnp.transpose(f_total, (1, 0, 2, 3)).reshape(3, 4 * units, width // 4)
    layer_out = jnp.where(on_first, home_out0, home_out1)
    input_grad = jnp.where(on_first, home_grad0, home_grad1).astype(F32)
    share = width // 16
    first_col = (4 * (2 * x + c) + 2 * half + p) * share
    gain_share = lax.dynamic_slice_in_dim(gain_sums[5], first_col, share, 1)
    gain_in_share = jnp.where(on_first, gain_share[0:1], gain_share[1:2])
    gain_mid_share = jnp.where(on_first, gain_share[2:3], gain_share[3:4])
    return (
        layer_out[None],
        input_grad[None],
        a_sum[0].T[None],
        a_sum[1].T[None],
        a_sum[2].T[None],
        a_sum[3][None],
        f_total[0].T[None],
        f_total[1].T[None],
        f_total[2][None],
        gain_in_share,
        gain_mid_share,
    )


def solution(mesh):
    in_specs = (
        P(None, ("seq", "tensor"), None),
        P(None, ("seq", "tensor"), None),
        P(),
        P("section", "seq", "tensor"),
        P("section", "seq", "tensor"),
        P("section", "seq", "tensor"),
        P("section", "tensor", "seq"),
        P("section", "seq", "tensor"),
        P("section", "seq", "tensor"),
        P("section", "tensor", "seq"),
        P("section", None),
        P("section", None),
    )
    out_specs = (
        P("section", None, ("seq", "tensor"), None),
        P("section", None, ("seq", "tensor"), None),
        P("section", "seq", "tensor"),
        P("section", "seq", "tensor"),
        P("section", "seq", "tensor"),
        P("section", "tensor", "seq"),
        P("section", "seq", "tensor"),
        P("section", "seq", "tensor"),
        P("section", "tensor", "seq"),
        P("section", ("seq", "tensor")),
        P("section", ("seq", "tensor")),
    )
    grid = (mesh.shape["section"], mesh.shape["seq"], mesh.shape["tensor"]) == (2, 4, 4)
    return jax.shard_map(
        on_grid if grid else on_device, mesh=mesh, in_specs=in_specs, out_specs=out_specs, check_vma=False
    )
```

```python
import functools
import math

import jax
import jax.numpy as jnp
from jax import lax
from jax.experimental import pallas as pl
from jax.experimental.pallas import tpu as pltpu
from jax.sharding import PartitionSpec as P

HS = 64


EPSILON = 1e-05
NEGATIVE = -1e30


def shifted(shard, axis, by):
    peers = lax.axis_size(axis)
    pairs = [(i, i + by) for i in range(peers) if 0 <= i + by < peers]
    return lax.ppermute(shard, axis, pairs)


def product(left, right):
    return jnp.dot(left, right, preferred_element_type=jnp.float32)


def inner_rows(left, right):
    return lax.dot_general(
        left, right, (((0,), (0,)), ((), ())), preferred_element_type=jnp.float32
    )


def against(left, right):
    return lax.dot_general(
        left, right, (((1,), (1,)), ((), ())), preferred_element_type=jnp.float32
    )


def doc_table(length_row, places):
    doc_ends = jnp.cumsum(length_row)
    doc_starts = doc_ends - length_row
    segment = jnp.sum((places[:, None] >= doc_ends[None, :]).astype(jnp.int32), axis=1)
    member = segment[:, None] == jnp.arange(length_row.shape[0], dtype=jnp.int32)[None, :]
    offset = jnp.sum(jnp.where(member, doc_starts[None, :], 0), axis=1)
    return (segment, places - offset)


def rotate(matrix, within, direction):
    row_count = matrix.shape[0]
    head_count = matrix.shape[1] // HS
    half_size = HS // 2
    frequency = jnp.exp(jnp.arange(half_size, dtype=jnp.float32) * (-math.log(10000.0) / half_size))
    angles = within.astype(jnp.float32)[:, None] * frequency[None, :]
    cosine = jnp.cos(angles)[:, None, :]
    sine_part = direction * jnp.sin(angles)[:, None, :]
    paired = matrix.reshape(row_count, head_count, 2, half_size)
    former = paired[:, :, 0, :]
    latter = paired[:, :, 1, :]
    turned = jnp.stack(
        [former * cosine - latter * sine_part, latter * cosine + former * sine_part], axis=2
    )
    return turned.reshape(row_count, head_count * HS)


def norm_rows(values, gain_row):
    inverse = lax.rsqrt(jnp.mean(values * values, axis=-1, keepdims=True) + EPSILON)
    unit_rows = values * inverse
    return (unit_rows, inverse, (unit_rows * gain_row).astype(jnp.bfloat16))


def norm_back(grad_normed, unit_rows, inverse, gain_row):
    shaped = grad_normed * gain_row
    inner = jnp.mean(shaped * unit_rows, axis=-1, keepdims=True)
    return (inverse * (shaped - unit_rows * inner), jnp.sum(grad_normed * unit_rows, axis=0))


def spread(values):
    return lax.all_gather(values, "tensor", axis=0, tiled=True)


def fold_rows(values):
    return lax.psum_scatter(
        values.astype(jnp.bfloat16), "tensor", scatter_dimension=0, tiled=True
    ).astype(jnp.float32)


def allowed_mask(places, segment, key_places, key_segment):
    return (key_places[None, :] <= places[:, None]) & (key_segment[None, :] == segment[:, None])


def project(normed_all, matrices, within, mixin, on_first):
    query_rows = rotate(product(normed_all, matrices[0]), within, 1.0).astype(jnp.bfloat16)
    key_rows = rotate(product(normed_all, matrices[1]), within, 1.0).astype(jnp.bfloat16)
    value_raw = product(normed_all, matrices[2])
    value_rows = jnp.where(
        on_first, value_raw, 0.5 * value_raw + 0.5 * mixin.astype(jnp.float32)
    ).astype(jnp.bfloat16)
    return (query_rows, key_rows, value_rows)


def cycle_attend(query_rows, key_rows, value_rows, places, segment, length_row):
    row_count = query_rows.shape[0]
    head_count = query_rows.shape[1] // HS
    query_heads = query_rows.reshape(row_count, head_count, HS)
    largest = jnp.full((head_count, row_count), NEGATIVE, jnp.float32)
    piece_keys = lax.all_gather(key_rows, "seq", axis=0, tiled=True)
    piece_values = lax.all_gather(value_rows, "seq", axis=0, tiled=True)
    piece_rows = piece_keys.shape[0]
    key_places = jnp.arange(piece_rows, dtype=jnp.int32)
    key_segment = doc_table(length_row, key_places)[0]
    allowed = allowed_mask(places, segment, key_places, key_segment)
    scores = jnp.einsum(
        "qhd,khd->hqk",
        query_heads,
        piece_keys.reshape(piece_rows, head_count, HS),
        preferred_element_type=jnp.float32,
    ) * HS ** (-0.5)
    masked = jnp.where(allowed[None], scores, NEGATIVE)
    newest = jnp.maximum(largest, jnp.max(masked, axis=2))
    weights = jnp.where(allowed[None], jnp.exp(masked - newest[:, :, None]), 0.0)
    totals = jnp.sum(weights, axis=2)
    summed = jnp.einsum(
        "hqk,khd->hqd",
        weights.astype(jnp.bfloat16),
        piece_values.reshape(piece_rows, head_count, HS),
        preferred_element_type=jnp.float32,
    )
    largest, totals, summed = (newest, totals, summed)
    attended = summed / totals[:, :, None]
    return jnp.transpose(attended, (1, 0, 2)).reshape(row_count, head_count * HS)


def forward_layer(residual, mixin, on_first, matrices, gain_pair, places, length_row):
    segment, within = doc_table(length_row, places)
    normed_in = norm_rows(residual, gain_pair[0])[2]
    normed_all = spread(normed_in)
    query_rows, key_rows, value_rows = project(normed_all, matrices, within, mixin, on_first)
    attended = cycle_attend(query_rows, key_rows, value_rows, places, segment, length_row)
    middle = residual + fold_rows(product(attended.astype(jnp.bfloat16), matrices[3]))
    normed_mid = norm_rows(middle, gain_pair[1])[2]
    normed_mid_all = spread(normed_mid)
    gate_rows = product(normed_mid_all, matrices[4])
    up_rows = product(normed_mid_all, matrices[5])
    hidden = (jax.nn.silu(gate_rows) * up_rows).astype(jnp.bfloat16)
    return (middle + fold_rows(product(hidden, matrices[6])), value_rows)


def backward_layer(
    residual, mixin, grad_top, extra_values, on_first, matrices, gain_pair, places, length_row
):
    segment, within = doc_table(length_row, places)
    unit_in, inverse_in, normed_in = norm_rows(residual, gain_pair[0])
    normed_all = spread(normed_in)
    query_rows, key_rows, value_rows = project(normed_all, matrices, within, mixin, on_first)
    all_keys, all_values = (
        lax.all_gather(key_rows, "seq", axis=0, tiled=True),
        lax.all_gather(value_rows, "seq", axis=0, tiled=True),
    )
    row_count = query_rows.shape[0]
    head_count = query_rows.shape[1] // HS
    total_rows = all_keys.shape[0]
    block_count = total_rows // row_count
    query_heads = query_rows.reshape(row_count, head_count, HS)
    key_blocks = all_keys.reshape(block_count, row_count, head_count, HS)
    value_blocks = all_values.reshape(block_count, row_count, head_count, HS)
    block_numbers = jnp.arange(block_count, dtype=jnp.int32)

    def block_scores(block_number, block_keys):
        key_places = block_number * row_count + jnp.arange(row_count, dtype=jnp.int32)
        key_segment = doc_table(length_row, key_places)[0]
        allowed = allowed_mask(places, segment, key_places, key_segment)
        scores = jnp.einsum(
            "qhd,khd->hqk", query_heads, block_keys, preferred_element_type=jnp.float32
        ) * HS ** (-0.5)
        return (allowed, jnp.where(allowed[None], scores, NEGATIVE))

    def first_pass(running, block_item):
        largest, totals, summed = running
        block_number, block_keys, block_values = block_item
        allowed, masked = block_scores(block_number, block_keys)
        newest = jnp.maximum(largest, jnp.max(masked, axis=2))
        rescale = jnp.exp(largest - newest)
        weights = jnp.where(allowed[None], jnp.exp(masked - newest[:, :, None]), 0.0)
        totals = totals * rescale + jnp.sum(weights, axis=2)
        summed = summed * rescale[:, :, None] + jnp.einsum(
            "hqk,khd->hqd",
            weights.astype(jnp.bfloat16),
            block_values,
            preferred_element_type=jnp.float32,
        )
        return ((newest, totals, summed), None)

    start_state = (
        jnp.full((head_count, row_count), NEGATIVE, jnp.float32),
        jnp.zeros((head_count, row_count), jnp.float32),
        jnp.zeros((head_count, row_count, HS), jnp.float32),
    )
    (largest, totals, summed), _ = lax.scan(
        first_pass, start_state, (block_numbers, key_blocks, value_blocks)
    )
    attended = summed / totals[:, :, None]
    attended_low = (
        jnp.transpose(attended, (1, 0, 2)).reshape(row_count, head_count * HS).astype(jnp.bfloat16)
    )
    middle = residual + fold_rows(product(attended_low, matrices[3]))
    unit_mid, inverse_mid, normed_mid = norm_rows(middle, gain_pair[1])
    normed_mid_all = spread(normed_mid)
    gate_rows = product(normed_mid_all, matrices[4])
    up_rows = product(normed_mid_all, matrices[5])
    sigmoid_gate = jax.nn.sigmoid(gate_rows)
    activated = gate_rows * sigmoid_gate
    hidden = (activated * up_rows).astype(jnp.bfloat16)
    grad_top_all = spread(grad_top.astype(jnp.bfloat16))
    grad_w_down = inner_rows(hidden, grad_top_all)
    grad_hidden = against(grad_top_all, matrices[6])
    grad_gate = (
        grad_hidden * up_rows * sigmoid_gate * (1.0 + gate_rows * (1.0 - sigmoid_gate))
    ).astype(jnp.bfloat16)
    grad_up = (grad_hidden * activated).astype(jnp.bfloat16)
    grad_w_gate = inner_rows(normed_mid_all, grad_gate)
    grad_w_up = inner_rows(normed_mid_all, grad_up)
    grad_normed_mid = fold_rows(against(grad_gate, matrices[4]) + against(grad_up, matrices[5]))
    grad_middle, grad_gain_mid = norm_back(grad_normed_mid, unit_mid, inverse_mid, gain_pair[1])
    grad_middle = grad_middle + grad_top
    grad_middle_all = spread(grad_middle.astype(jnp.bfloat16))
    grad_w_out = inner_rows(attended_low, grad_middle_all)
    grad_attended = against(grad_middle_all, matrices[3]).astype(jnp.bfloat16)
    grad_heads = jnp.transpose(grad_attended.reshape(row_count, head_count, HS), (1, 0, 2))
    delta = jnp.sum(grad_heads.astype(jnp.float32) * attended, axis=2)
    scaled_grad = grad_heads.astype(jnp.float32) / totals[:, :, None]
    scaled_high = scaled_grad.astype(jnp.bfloat16)
    scaled_rest = (scaled_grad - scaled_high.astype(jnp.float32)).astype(jnp.bfloat16)
    inverse_totals = 1.0 / totals[:, :, None]

    def second_pass(grad_sum, block_item):
        block_number, block_keys, block_values = block_item
        allowed, masked = block_scores(block_number, block_keys)
        weights = jnp.where(allowed[None], jnp.exp(masked - largest[:, :, None]), 0.0)
        low_weights = weights.astype(jnp.bfloat16)
        along = jnp.einsum(
            "hqd,khd->hqk", grad_heads, block_values, preferred_element_type=jnp.float32
        )
        grad_scores = (weights * inverse_totals * (along - delta[:, :, None])).astype(jnp.bfloat16)
        grad_sum = grad_sum + jnp.einsum(
            "hqk,khd->qhd", grad_scores, block_keys, preferred_element_type=jnp.float32
        ) * HS ** (-0.5)
        block_key_grad = jnp.einsum(
            "hqk,qhd->khd", grad_scores, query_heads, preferred_element_type=jnp.float32
        ) * HS ** (-0.5)
        block_value_grad = jnp.einsum(
            "hqk,hqd->khd", low_weights, scaled_high, preferred_element_type=jnp.float32
        ) + jnp.einsum("hqk,hqd->khd", low_weights, scaled_rest, preferred_element_type=jnp.float32)
        return (grad_sum, (block_key_grad, block_value_grad))

    grad_queries, (grad_keys, grad_values) = lax.scan(
        second_pass,
        jnp.zeros((row_count, head_count, HS), jnp.float32),
        (block_numbers, key_blocks, value_blocks),
    )
    own_keys, own_values = (
        lax.psum_scatter(
            grad_keys.reshape(total_rows, head_count * HS).astype(jnp.bfloat16),
            "seq",
            scatter_dimension=0,
            tiled=True,
        ).astype(jnp.float32),
        lax.psum_scatter(
            grad_values.reshape(total_rows, head_count * HS).astype(jnp.bfloat16),
            "seq",
            scatter_dimension=0,
            tiled=True,
        ).astype(jnp.float32),
    )
    grad_value_raw = jnp.where(on_first, own_values + extra_values, 0.5 * own_values).astype(
        jnp.bfloat16
    )
    send_values = 0.5 * own_values
    grad_query_raw = rotate(grad_queries.reshape(row_count, head_count * HS), within, -1.0).astype(
        jnp.bfloat16
    )
    grad_key_raw = rotate(own_keys, within, -1.0).astype(jnp.bfloat16)
    grad_w_query = inner_rows(normed_all, grad_query_raw)
    grad_w_key = inner_rows(normed_all, grad_key_raw)
    grad_w_value = inner_rows(normed_all, grad_value_raw)
    grad_normed_in = fold_rows(
        against(grad_query_raw, matrices[0])
        + against(grad_key_raw, matrices[1])
        + against(grad_value_raw, matrices[2])
    )
    grad_in, grad_gain_in = norm_back(grad_normed_in, unit_in, inverse_in, gain_pair[0])
    weight_terms = (
        grad_w_query,
        grad_w_key,
        grad_w_value,
        grad_w_out,
        grad_w_gate,
        grad_w_up,
        grad_w_down,
    )
    return (grad_in + grad_middle, send_values, weight_terms, (grad_gain_in, grad_gain_mid))


def on_device(
    inputs,
    cotangent,
    lengths,
    w_query,
    w_key,
    w_value,
    w_out,
    w_gate,
    w_up,
    w_down,
    attn_gain,
    mlp_gain,
):
    section_index = lax.axis_index("section")
    on_first = section_index == 0
    micro_count = inputs.shape[0]
    local_rows = inputs.shape[1]
    model_width = inputs.shape[2]
    group_rows = local_rows * lax.axis_size("tensor")
    head_width = w_query.shape[2]
    row_values = local_rows * model_width
    places = lax.axis_index("seq") * group_rows + jnp.arange(group_rows, dtype=jnp.int32)
    gain_pair = (attn_gain[0], mlp_gain[0])
    gathered = (
        lax.all_gather(w_query[0], "seq", axis=0, tiled=True),
        lax.all_gather(w_key[0], "seq", axis=0, tiled=True),
        lax.all_gather(w_value[0], "seq", axis=0, tiled=True),
        lax.all_gather(w_out[0], "seq", axis=1, tiled=True),
        lax.all_gather(w_gate[0], "seq", axis=0, tiled=True),
        lax.all_gather(w_up[0], "seq", axis=0, tiled=True),
        lax.all_gather(w_down[0], "seq", axis=1, tiled=True),
    )
    recv_rows = jnp.zeros((local_rows, model_width), jnp.bfloat16)
    recv_values = jnp.zeros((group_rows, head_width), jnp.bfloat16)
    kept_inputs = jnp.zeros((micro_count, local_rows, model_width), jnp.bfloat16)
    kept_values = jnp.zeros((micro_count, group_rows, head_width), jnp.bfloat16)
    kept_outputs = jnp.zeros((micro_count, local_rows, model_width), jnp.bfloat16)
    for moment in range(micro_count + 1):
        which = moment - section_index
        usable = (which >= 0) & (which < micro_count)
        slot_index = jnp.clip(which, 0, micro_count - 1)
        own_rows = lax.dynamic_index_in_dim(inputs, slot_index, 0, keepdims=False)
        layer_in = jnp.where(on_first, own_rows, recv_rows)
        length_row = lax.dynamic_index_in_dim(lengths, slot_index, 0, keepdims=False)
        result, value_rows = forward_layer(
            layer_in.astype(jnp.float32),
            recv_values,
            on_first,
            gathered,
            gain_pair,
            places,
            length_row,
        )
        result_low = result.astype(jnp.bfloat16)
        kept_inputs = jnp.where(
            usable,
            lax.dynamic_update_index_in_dim(kept_inputs, layer_in, slot_index, 0),
            kept_inputs,
        )
        kept_values = jnp.where(
            usable,
            lax.dynamic_update_index_in_dim(kept_values, recv_values, slot_index, 0),
            kept_values,
        )
        kept_outputs = jnp.where(
            usable,
            lax.dynamic_update_index_in_dim(kept_outputs, result_low, slot_index, 0),
            kept_outputs,
        )
        if moment < micro_count:
            packed = jnp.concatenate([result_low.reshape(-1), value_rows.reshape(-1)])
            arrived = shifted(packed, "section", 1)
            recv_rows = arrived[:row_values].reshape(local_rows, model_width)
            recv_values = arrived[row_values:].reshape(group_rows, head_width)
    grad_rows_in = jnp.zeros((local_rows, model_width), jnp.float32)
    grad_values_in = jnp.zeros((group_rows, head_width), jnp.float32)
    grad_inputs = jnp.zeros((micro_count, local_rows, model_width), jnp.float32)
    weight_sums = tuple((jnp.zeros(matrix.shape, jnp.float32) for matrix in gathered))
    share_sums = (
        jnp.zeros(w_query[0].shape, jnp.float32),
        jnp.zeros(w_key[0].shape, jnp.float32),
        jnp.zeros(w_value[0].shape, jnp.float32),
        jnp.zeros(w_out[0].shape, jnp.float32),
        jnp.zeros(w_gate[0].shape, jnp.float32),
        jnp.zeros(w_up[0].shape, jnp.float32),
        jnp.zeros(w_down[0].shape, jnp.float32),
    )
    gain_sums = (jnp.zeros((model_width,), jnp.float32), jnp.zeros((model_width,), jnp.float32))
    for moment in range(micro_count + 1):
        which = moment - (1 - section_index)
        usable = (which >= 0) & (which < micro_count)
        slot_index = jnp.clip(which, 0, micro_count - 1)
        matrices = (
            lax.all_gather(w_query[0], "seq", axis=0, tiled=True),
            lax.all_gather(w_key[0], "seq", axis=0, tiled=True),
            lax.all_gather(w_value[0], "seq", axis=0, tiled=True),
            lax.all_gather(w_out[0], "seq", axis=1, tiled=True),
            lax.all_gather(w_gate[0], "seq", axis=0, tiled=True),
            lax.all_gather(w_up[0], "seq", axis=0, tiled=True),
            lax.all_gather(w_down[0], "seq", axis=1, tiled=True),
        )
        layer_in = lax.dynamic_index_in_dim(kept_inputs, slot_index, 0, keepdims=False).astype(
            jnp.float32
        )
        mixin = lax.dynamic_index_in_dim(kept_values, slot_index, 0, keepdims=False)
        length_row = lax.dynamic_index_in_dim(lengths, slot_index, 0, keepdims=False)
        own_grad = lax.dynamic_index_in_dim(cotangent, slot_index, 0, keepdims=False).astype(
            jnp.float32
        )
        grad_top = jnp.where(usable, jnp.where(on_first, grad_rows_in, own_grad), 0.0)
        extra_values = jnp.where(usable & on_first, grad_values_in, 0.0)
        grad_in, send_values, weight_terms, gain_terms = backward_layer(
            layer_in,
            mixin,
            grad_top,
            extra_values,
            on_first,
            matrices,
            gain_pair,
            places,
            length_row,
        )
        gain_sums = (gain_sums[0] + gain_terms[0], gain_sums[1] + gain_terms[1])
        weight_sums = tuple((total + term for total, term in zip(weight_sums, weight_terms)))
        grad_inputs = jnp.where(
            usable,
            lax.dynamic_update_index_in_dim(grad_inputs, grad_in, slot_index, 0),
            grad_inputs,
        )
        if moment < micro_count:
            packed = jnp.concatenate([grad_in.reshape(-1), send_values.reshape(-1)])
            arrived = shifted(packed.astype(jnp.bfloat16), "section", -1).astype(packed.dtype)
            grad_rows_in = arrived[:row_values].reshape(local_rows, model_width)
            grad_values_in = arrived[row_values:].reshape(group_rows, head_width)
    share_sums = (
        lax.psum_scatter(
            weight_sums[0].astype(jnp.bfloat16), "seq", scatter_dimension=0, tiled=True
        ).astype(jnp.float32),
        lax.psum_scatter(
            weight_sums[1].astype(jnp.bfloat16), "seq", scatter_dimension=0, tiled=True
        ).astype(jnp.float32),
        lax.psum_scatter(
            weight_sums[2].astype(jnp.bfloat16), "seq", scatter_dimension=0, tiled=True
        ).astype(jnp.float32),
        lax.psum_scatter(
            weight_sums[3].astype(jnp.bfloat16), "seq", scatter_dimension=1, tiled=True
        ).astype(jnp.float32),
        lax.psum_scatter(
            weight_sums[4].astype(jnp.bfloat16), "seq", scatter_dimension=0, tiled=True
        ).astype(jnp.float32),
        lax.psum_scatter(
            weight_sums[5].astype(jnp.bfloat16), "seq", scatter_dimension=0, tiled=True
        ).astype(jnp.float32),
        lax.psum_scatter(
            weight_sums[6].astype(jnp.bfloat16), "seq", scatter_dimension=1, tiled=True
        ).astype(jnp.float32),
    )
    gain_shares = (
        lax.psum_scatter(gain_sums[0], ("seq", "tensor"), scatter_dimension=0, tiled=True),
        lax.psum_scatter(gain_sums[1], ("seq", "tensor"), scatter_dimension=0, tiled=True),
    )
    return (
        kept_outputs[None],
        grad_inputs[None],
        share_sums[0][None],
        share_sums[1][None],
        share_sums[2][None],
        share_sums[3][None],
        share_sums[4][None],
        share_sums[5][None],
        share_sums[6][None],
        gain_shares[0][None],
        gain_shares[1][None],
    )


MESH_ID = pl.DeviceIdType.MESH
LOW = jnp.bfloat16
F32 = jnp.float32
ORDERS = ((1, 2, 4), (2, 4, 1), (4, 1, 2))
LEVELS = ((0,), (1, 2, 4), (3, 5, 6), (7,))
NT = (((1,), (1,)), ((), ()))
NN = (((1,), (0,)), ((), ()))
TN = (((0,), (0,)), ((), ()))
VMEM_BYTES = 53 * 2**20


def dot(left, right, dims=NN):
    return lax.dot_general(left, right, dims, preferred_element_type=F32)


def flip(value, bit):
    if isinstance(bit, int):
        return 1 - value if bit else value
    return value + bit - 2 * value * bit


def spot():
    y, s, z = lax.axis_index("section"), lax.axis_index("seq"), lax.axis_index("tensor")
    return (y, lax.div(s, 2), lax.rem(s, 2), lax.div(z, 2), lax.rem(z, 2))


def device(at):
    y, x, c, h, p = at
    return (y, 2 * x + c, 2 * h + p)


def moved(at, mask, core=0):
    y, x, c, h, p = at
    if isinstance(mask, int):
        bits = (mask & 1, (mask >> 1) & 1, mask >> 2)
    else:
        bits = (lax.rem(mask, 2), lax.rem(lax.div(mask, 2), 2), lax.div(mask, 4))
    return (flip(y, bits[1]), flip(x, bits[0]), flip(c, core), h, flip(p, bits[2]))


def far_role(at):
    return flip(at[0], at[2])


def lane_of(at):
    return 2 * flip(at[3], far_role(at)) + at[4]


def block_of(at):
    return (2 * at[1] + at[2]) * 4 + lane_of(at)


def level_mask(level, i):
    if level == 0:
        return 0 * i
    if level == 1:
        return 1 + i + lax.div(i, 2)
    if level == 2:
        return 3 + i + lax.div(i + 1, 2)
    return 0 * i + 7


def last_bit(k, mask):
    return [bit for bit in ORDERS[k] if bit & mask][-1]


def parts_of(rows):
    units = rows // 16
    small = units // 3
    sizes = (16 * (units - 2 * small), 16 * small, 16 * small)
    return ((0, sizes[0]), (sizes[0], sizes[1]), (sizes[0] + sizes[1], sizes[2]))


def remote(src, dst, send, recv, at):
    return pltpu.make_async_remote_copy(
        src_ref=src, dst_ref=dst, send_sem=send, recv_sem=recv, device_id=device(at), device_id_type=MESH_ID
    )


def others(at):
    return [moved(at, mask, core) for mask in range(8) for core in range(2) if mask + core]


def greet(at, *pushes, peers=()):
    met = others(at) + list(peers)
    count = len(met)
    for peer in met:
        signal(peer)
    for push in pushes:
        count = count + push.greet()
    pl.semaphore_wait(pltpu.get_barrier_semaphore(), count)


def run(steps):
    for _ in steps:
        pass


def gather(*args, **kwargs):
    run(gathering(*args, **kwargs))


def gathering(at, buf, sems, on_block=None, keep=None, ready=None):
    send, recv, csend, crecv = sems
    parts = parts_of(buf.shape[1])

    def rows(mask, k, core=0):
        return buf.at[block_of(moved(at, mask, core)), pl.ds(*parts[k])]

    def hop(k, target):
        bit = last_bit(k, target)
        ref = rows(target ^ bit, k)
        return remote(ref, ref, send.at[k, target], recv.at[k, target], moved(at, bit))

    def arrival(k, target):
        ref = rows(target, k)
        return remote(ref, ref, send.at[k, target], recv.at[k, target], moved(at, last_bit(k, target)))

    def across(mask, core=0):
        ref = buf.at[block_of(moved(at, mask, core))]
        return remote(ref, ref, csend.at[mask], crecv.at[mask], moved(at, 0, 1))

    def visit(level, core):
        if on_block is None and keep is None:
            return

        def one(i, none):
            b = block_of(moved(at, level_mask(level, i), core))
            if keep is not None:
                pltpu.make_async_copy(buf.at[b], keep[0].at[b], keep[1].at[b]).start()
            if on_block is not None:
                on_block(b)
            return none

        lax.fori_loop(0, len(LEVELS[level]), one, 0)

    for i in range(2):
        for k in range(3):
            hop(k, ORDERS[k][i]).start()
        if i == 0:
            across(0).start()
    if ready is not None:
        ready()
    visit(0, 0)
    across(0, 1).wait_recv()
    visit(0, 1)
    yield
    for k in range(3):
        first, second, third = ORDERS[k]
        arrival(k, first).wait_recv()
        hop(k, first | second).start()
    for k in range(3):
        first, second, third = ORDERS[k]
        hop(k, third).start()
        hop(k, first | third).start()
    yield
    for k in range(3):
        first, second, third = ORDERS[k]
        arrival(k, second).wait_recv()
        hop(k, second | third).start()
    yield
    for k in range(3):
        first, second, third = ORDERS[k]
        arrival(k, first | second).wait_recv()
        hop(k, 7).start()
    yield
    for level in (1, 2, 3):
        for mask in LEVELS[level]:
            for k in range(3):
                first, second, third = ORDERS[k]
                if mask not in (first, second, first | second):
                    arrival(k, mask).wait_recv()
            across(mask).start()
        visit(level, 0)
        for mask in LEVELS[level]:
            across(mask, 1).wait_recv()
        visit(level, 1)
        yield
    for k in range(3):
        for target in range(1, 8):
            hop(k, target).wait_send()
    for mask in range(8):
        across(mask).wait_send()


def kept(buf, keep):
    for b in range(16):
        pltpu.make_async_copy(buf.at[b], keep[0].at[b], keep[1].at[b]).wait()


def scatter(*args, **kwargs):
    run(scattering(*args, **kwargs))


def scattering(at, total, boxes, sems, partial, before_last=None):
    out_c, in_c, rin = boxes
    send, recv, csend, crecv = sems
    parts = parts_of(total.shape[0])

    def hop(k, target):
        rows = pl.ds(*parts[k])
        return remote(
            in_c.at[target, rows],
            rin.at[target - 1, rows],
            send.at[k, target],
            recv.at[k, target],
            moved(at, last_bit(k, target)),
        )

    def across(mask):
        slot = 0 if mask in (0, 7) else 1 + (LEVELS[1] + LEVELS[2]).index(mask) % 3
        return remote(out_c.at[slot], in_c.at[mask], csend.at[mask], crecv.at[mask], moved(at, 0, 1))

    def emit(level):
        if level < 2:
            for mask in LEVELS[3 - level]:
                across(mask).wait_send()

        def one(i, none):
            slot = 1 + i if level in (1, 2) else 0
            out_c[slot] = partial(block_of(moved(at, level_mask(level, i), 1))).astype(LOW)
            return none

        lax.fori_loop(0, len(LEVELS[level]), one, 0)
        for mask in LEVELS[level]:
            across(mask).start()

    def settle(level):
        for mask in LEVELS[level]:
            across(mask).wait_recv()

        def one(i, none):
            mask = level_mask(level, i)
            mine = partial(block_of(moved(at, mask))) + in_c[mask].astype(F32)
            if level == 0:
                total[...] = mine
            else:
                in_c[mask] = mine.astype(LOW)
            return none

        lax.fori_loop(0, len(LEVELS[level]), one, 0)
        for mask in LEVELS[level]:
            for k in range(3):
                if mask & ORDERS[k][2]:
                    hop(k, mask).start()

    def arrived(k, target):
        hop(k, target).wait_recv()
        return rin[target - 1, pl.ds(*parts[k])].astype(F32)

    emit(3)
    emit(2)
    yield
    settle(3)
    settle(2)
    emit(1)
    yield
    settle(1)
    if before_last is not None:
        before_last()
    emit(0)
    settle(0)
    yield
    for mask_of in (lambda a, b: a | b, lambda a, b: b):
        for k in range(3):
            first, second, third = ORDERS[k]
            mask, rows = mask_of(first, second), pl.ds(*parts[k])
            in_c[mask, rows] = (in_c[mask, rows].astype(F32) + arrived(k, mask | third)).astype(LOW)
            hop(k, mask).start()
        yield
    for k in range(3):
        first, second, third = ORDERS[k]
        rows = pl.ds(*parts[k])
        in_c[first, rows] = (
            in_c[first, rows].astype(F32) + arrived(k, first | third) + arrived(k, first | second)
        ).astype(LOW)
        hop(k, first).start()
    yield
    for k in range(3):
        first, second, third = ORDERS[k]
        rows = pl.ds(*parts[k])
        total[rows] = total[rows] + arrived(k, third) + arrived(k, second) + arrived(k, first)
    for k in range(3):
        for target in range(1, 8):
            hop(k, target).wait_send()
    for mask in LEVELS[0] + LEVELS[1]:
        across(mask).wait_send()


class ToRows:
    def __init__(self, at, block, place, sems):
        self.at, self.block, self.place = at, block, place
        self.send, self.recv, self.local = sems
        self.mine = block_of(at)

    def copy(self, b):
        lane, (y, x, c, h, p) = b % 4, self.at
        x, c = b // 8, (b // 4) % 2
        home = (flip(flip(h, lane // 2), c), x, c, h, lane % 2)
        return remote(self.block(b), self.place(self.mine), self.send.at[b], self.recv.at[self.mine], home)

    def start(self, b):
        @pl.when(same(b, self.mine) == 0)
        def _():
            self.copy(b).start()

        @pl.when(same(b, self.mine) == 1)
        def _():
            pltpu.make_async_copy(self.block(b), self.place(b), self.local).start()

    def finish(self):
        for b in range(16):

            @pl.when(same(b, self.mine) == 0)
            def _(b=b):
                dst = self.place(b)
                remote(dst, dst, self.send.at[b], self.recv.at[b], self.at).wait_recv()
                self.copy(b).wait_send()

            @pl.when(same(b, self.mine) == 1)
            def _(b=b):
                pltpu.make_async_copy(self.block(b), self.place(b), self.local).wait()


def row_sems():
    dma = pltpu.SemaphoreType.DMA
    return (dma((16,)), dma((16,)), dma)


def same(a, b):
    return 1 - jnp.minimum(jnp.abs(a - b), 1)


def signal(at):
    pl.semaphore_signal(pltpu.get_barrier_semaphore(), inc=1, device_id=device(at), device_id_type=MESH_ID)


class ToHeads:
    def __init__(self, at, layer, piece, place, relay, sems):
        self.at, self.layer, self.piece, self.place, self.relay = at, layer, piece, place, relay
        self.send, self.recv, self.local, self.relay_send, self.relay_recv = sems
        y, x, c, h, p = at
        self.s = 2 * x + c
        self.sends = same(y, layer)
        self.near = 1 - far_role(at)

    def is_me(self, j):
        return self.sends * self.near * same(self.s, j)

    def greet(self):
        y, x, c, h, p = self.at
        source = self.near * self.layer + (1 - self.near) * y
        for k in range(4):

            @pl.when(self.is_me(k) == 0)
            def _(k=k):
                signal((source, k // 2, k % 2, flip(h, 1 - self.near), p))

        return 2 + self.sends * (4 - self.near)

    def near_copy(self, j):
        h, p = self.at[3], self.at[4]
        home = (j % 2, j // 2, j % 2, h, p)
        return remote(self.piece(j), self.place(self.s), self.send.at[j], self.recv.at[self.s], home)

    def far_copy(self, src, i, j):
        h, p = self.at[3], self.at[4]
        home = (1 - j % 2, j // 2, j % 2, 1 - h, p)
        return remote(src, self.place(self.s), self.send.at[4 + i], self.recv.at[self.s], home)

    def direct(self, i):
        j = 2 * i + 1 - self.layer
        return self.far_copy(self.piece(j), i, j)

    def relayed(self, i):
        return self.far_copy(self.relay.at[i], i, 2 * i + self.layer)

    def to_twin(self, i):
        y, x, c, h, p = self.at
        return remote(
            self.piece(2 * i + self.layer),
            self.relay.at[i],
            self.relay_send.at[i],
            self.relay_recv.at[i],
            (1 - self.layer, x, c, h, p),
        )

    def start_relay(self):
        @pl.when(self.sends == 1)
        def _():
            for i in range(2):
                self.to_twin(i).start()

    def start(self):
        @pl.when(self.sends == 1)
        def _():
            for i in range(2):
                self.direct(i).start()

        for j in range(4):

            @pl.when(self.sends - self.is_me(j) == 1)
            def _(j=j):
                self.near_copy(j).start()

            @pl.when(self.is_me(j) == 1)
            def _(j=j):
                pltpu.make_async_copy(self.piece(j), self.place(j), self.local).start()

    def forward(self):
        @pl.when(self.sends == 0)
        def _():
            for i in range(2):
                self.to_twin(i).wait_recv()
                self.relayed(i).start()

    def finish(self):
        for k in range(4):
            dst = self.place(k)

            @pl.when(self.is_me(k) == 0)
            def _(k=k, dst=dst):
                remote(dst, dst, self.send.at[0], self.recv.at[k], self.at).wait_recv()

            @pl.when(self.is_me(k) == 1)
            def _(k=k, dst=dst):
                pltpu.make_async_copy(self.piece(k), dst, self.local).wait()

        @pl.when(self.sends == 0)
        def _():
            for i in range(2):
                self.relayed(i).wait_send()

        @pl.when(self.sends == 1)
        def _():
            for i in range(2):
                self.direct(i).wait_send()
                self.to_twin(i).wait_send()

        for j in range(4):

            @pl.when(self.sends - self.is_me(j) == 1)
            def _(j=j):
                self.near_copy(j).wait_send()


class ToShards:
    def __init__(self, at, layer, piece, place, sems, roles=(0, 1)):
        self.at, self.layer, self.piece, self.place, self.roles = at, layer, piece, place, roles
        self.send, self.recv, self.local = sems
        y, x, c, h, p = at
        self.s = 2 * x + c
        self.gets = same(y, layer)
        self.role = far_role(at)
        self.active = {(0, 1): 1, (0,): 1 - self.role, (1,): self.role}[roles]

    def is_me(self, k):
        return self.gets * (1 - self.role) * same(self.s, k) if 0 in self.roles else 0 * self.gets

    def greet(self):
        h, p = self.at[3], self.at[4]
        for j in range(4):
            if 1 in self.roles:

                @pl.when(self.gets == 1)
                def _(j=j):
                    signal((1 - j % 2, j // 2, j % 2, 1 - h, p))

            if 0 in self.roles:

                @pl.when(self.gets - self.is_me(j) == 1)
                def _(j=j):
                    signal((j % 2, j // 2, j % 2, h, p))

        return self.active * (4 - self.gets * (1 - self.role))

    def copy(self, k):
        home = (self.layer, k // 2, k % 2, flip(self.at[3], self.role), self.at[4])
        return remote(
            self.piece(k), self.place(self.role, self.s), self.send.at[k], self.recv.at[self.role, self.s], home
        )

    def start(self):
        for k in range(4):

            @pl.when(self.active - self.is_me(k) == 1)
            def _(k=k):
                self.copy(k).start()

            @pl.when(self.is_me(k) == 1)
            def _(k=k):
                pltpu.make_async_copy(self.piece(k), self.place(0, k), self.local).start()

    def finish(self):
        for role in self.roles:
            for j in range(4):
                dst = self.place(role, j)
                comes = self.gets if role else self.gets - self.is_me(j)

                @pl.when(comes == 1)
                def _(role=role, j=j, dst=dst):
                    remote(dst, dst, self.send.at[0], self.recv.at[role, j], self.at).wait_recv()

        for k in range(4):

            @pl.when(self.active - self.is_me(k) == 1)
            def _(k=k):
                self.copy(k).wait_send()

            @pl.when(self.is_me(k) == 1)
            def _(k=k):
                pltpu.make_async_copy(self.piece(k), self.place(0, k), self.local).wait()


class ToHome:
    def __init__(self, at, layer, block, place, sems):
        self.at, self.layer, self.block, self.place = at, layer, block, place
        self.send, self.recv, self.local = sems
        y, x, c, h, p = at
        self.gets = same(y, layer)
        self.role = far_role(at)
        self.is_me = self.gets * (1 - self.role)

    def holder(self, micro):
        y, x, c, h, p = self.at
        role = flip(h, micro)
        return (flip(role, c), x, c, micro, p), (1 - role) * self.is_me

    def greet(self):
        for micro in range(2):
            holder, is_me = self.holder(micro)

            @pl.when(self.gets - is_me == 1)
            def _(holder=holder):
                signal(holder)

        return 1 - self.is_me

    def copy(self):
        y, x, c, h, p = self.at
        home = (self.layer, x, c, flip(h, self.role), p)
        return remote(self.block, self.place(h), self.send, self.recv.at[h], home)

    def keep(self):
        return pltpu.make_async_copy(self.block, self.place(self.at[3]), self.local)

    def start(self):
        @pl.when(self.is_me == 0)
        def _():
            self.copy().start()

        @pl.when(self.is_me == 1)
        def _():
            self.keep().start()

    def finish(self):
        for micro in range(2):
            dst = self.place(micro)

            @pl.when(self.gets - self.holder(micro)[1] == 1)
            def _(micro=micro, dst=dst):
                remote(dst, dst, self.send, self.recv.at[micro], self.at).wait_recv()

        @pl.when(self.is_me == 0)
        def _():
            self.copy().wait_send()

        @pl.when(self.is_me == 1)
        def _():
            self.keep().wait()


def home_sems():
    dma = pltpu.SemaphoreType.DMA
    return (dma, dma((2,)), dma)


def head_sems():
    dma = pltpu.SemaphoreType.DMA
    return (dma((6,)), dma((4,)), dma, dma((2,)), dma((2,)))


def shard_sems():
    dma = pltpu.SemaphoreType.DMA
    return (dma((4,)), dma((2, 4)), dma)


def slices(ref, size):
    return lambda j: ref.at[:, pl.ds(j * size, size)]


def columns(ref):
    wide = ref.shape[-1] // 4

    def place(s):
        start = s * wide
        return ref.at[:, :, pl.ds(start if isinstance(s, int) else pl.multiple_of(start, wide), wide)]

    return place


def unit_of(values):
    inverse = lax.rsqrt(jnp.mean(values * values, axis=-1, keepdims=True) + EPSILON)
    return (values * inverse, inverse)


def back_of(grad_normed, values, gain_row):
    unit, inverse = unit_of(values)
    shaped = grad_normed * gain_row
    inner = jnp.mean(shaped * unit, axis=-1, keepdims=True)
    return (inverse * (shaped - unit * inner), jnp.sum(grad_normed * unit, axis=0, keepdims=True))


def span(b, rows):
    return pl.ds(pl.multiple_of(b * rows, rows), rows)


def turned(top, bottom, cosine, sine):
    return (top * cosine - bottom * sine, bottom * cosine + top * sine)


def project_block(b, buf, w_ref, cos_ref, sin_ref, mix_ref, qkv_ref):
    rows, half = buf.shape[1], HS // 2
    cols = span(b, rows)
    raw = dot(w_ref[:3].reshape(3 * HS, buf.shape[2]), buf[b], NT)
    cosine, sine = cos_ref[:, cols], sin_ref[:, cols]
    for first, scale in ((0, HS**-0.5), (HS, 1.0)):
        a, bb = turned(raw[first : first + half], raw[first + half : first + HS], cosine, sine)
        qkv_ref[first : first + half, cols] = (a.astype(LOW) * scale).astype(LOW)
        qkv_ref[first + half : first + HS, cols] = (bb.astype(LOW) * scale).astype(LOW)
    value = raw[2 * HS :]
    if mix_ref is not None:
        value = 0.5 * value + 0.5 * mix_ref[:, cols].astype(F32)
    qkv_ref[2 * HS :, cols] = value.astype(LOW)


def up_block(b, buf, f_ref, hidden_ref, one_ref, two_ref):
    rows = span(b, buf.shape[1])
    x = buf[b]
    gate, up = dot(x, f_ref[0], NT), dot(x, f_ref[1], NT)
    sigmoid = 1.0 / (1.0 + jnp.exp(-gate))
    activated = gate * sigmoid
    hidden_ref[rows] = (activated * up).astype(LOW)
    one_ref[rows] = (up * sigmoid * (1.0 + gate * (1.0 - sigmoid))).astype(LOW)
    two_ref[rows] = activated.astype(LOW)


def held(buf):
    def blocks(use):
        def one(b, none):
            use(b, buf[b])
            return none

        lax.fori_loop(0, buf.shape[0], one, 0)

    return blocks


def streamed(far, ring, sems):
    half = ring.shape[0]

    def copy(b, slot):
        return pltpu.make_async_copy(far.at[b], ring.at[slot], sems.at[slot])

    for slot in range(half):
        copy(slot, slot).start()

    def blocks(use):
        def first(b, none):
            copy(b, b).wait()
            use(b, ring[b])
            copy(b + half, b).start()
            return none

        def second(b, none):
            copy(b + half, b).wait()
            use(b + half, ring[b])
            return none

        lax.fori_loop(0, half, first, 0)
        lax.fori_loop(0, half, second, 0)

    return blocks


class Stage:
    def __init__(self, sems):
        self.sems, self.count = sems, 0

    def copy(self, src, dst):
        copy = pltpu.make_async_copy(src, dst, self.sems.at[self.count])
        self.count += 1
        copy.start()
        return copy


def taking_turns(*steps):
    steps = list(steps)
    while steps:
        for one in list(steps):
            if next(one, True):
                steps.remove(one)
        yield


def feed_scratch(length, f_ref):
    return [pltpu.VMEM((length, f_ref.shape[1]), LOW)] * 3 + [pltpu.VMEM(f_ref.shape, F32)]


def out_project(at, push, att_in, wo_all, x_ref):
    push.finish()
    heads = att_in.shape[0] * HS
    summed = dot(att_in[...].reshape(heads, -1), wo_all[...].reshape(heads, -1), TN)
    return x_ref[...].astype(F32) + summed


def attend_and_share(at, steps, push, before, *refs):
    def after(qi):
        if qi == 0 and before is not None:
            before()
        each = TILE * 16 // refs[0].shape[1]
        for b in range(qi * each, (qi + 1) * each):
            push.start(b)
        next(steps, None)

    attend_body(*refs, after)
    run(steps)


def hidden_back(b, buf, f_ref, hidden_ref, one_ref, two_ref, sums_ref):
    here = span(b, buf.shape[1])
    grad = dot(buf[b], f_ref[2], NT)
    one_ref[here] = (grad * one_ref[here].astype(F32)).astype(LOW)
    two_ref[here] = (grad * two_ref[here].astype(F32)).astype(LOW)
    sums_ref[2] += dot(hidden_ref[here], buf[b], TN)


def down_back(
    at, top, ready, buf, blocks, total, boxes, ag_sems, rs_sems, f_ref, hidden_ref, one_ref, two_ref,
    gain_ref, middle_ref, sums_ref, wo_all, dout_block, push, dmid_ref, gain_grad_ref,
):
    rows = buf.shape[1]
    if not ready:
        sums_ref[...] = jnp.zeros_like(sums_ref)
        buf[block_of(at)] = top().astype(LOW)
        gather(at, buf, ag_sems, lambda b: hidden_back(b, buf, f_ref, hidden_ref, one_ref, two_ref, sums_ref))

    def partial(b):
        here = span(b, rows)
        return dot(one_ref[here], f_ref[0]) + dot(two_ref[here], f_ref[1])

    scatter(at, total, boxes, rs_sems, partial)
    grad, gain_grad = back_of(total[...], middle_ref[...], gain_ref[...])
    gain_grad_ref[...] = gain_grad
    grad = grad + top()
    dmid_ref[...] = grad
    heads = wo_all.shape[0] * HS
    found = dot(wo_all[...].reshape(heads, -1), grad.astype(LOW), NT).astype(LOW)
    dout_block[...] = found.reshape(dout_block.shape)
    for b in range(16):
        push.start(b)

    def gate_up(b, normed):
        here = span(b, rows)
        sums_ref[0] += dot(one_ref[here], normed, TN)
        sums_ref[1] += dot(two_ref[here], normed, TN)

    blocks(gate_up)
    push.finish()


def first_kernel(
    cos_ref, sin_ref, seg_ref, in_ref, a_ref, f_ref, gain_ref,
    qkv0_ref, att_ref, lse_ref, att_in, wo_all, x_here, middle_ref, out_ref, qkv1_ref,
    normed0_far, nmid_far, normed1_far, hidden_far, one_far, two_far, home_ref, a0, a1, f0, f1, gains, a0_relay, a1_relay, f0_relay, f1_relay,
    buf, low_ref, a_here, f_here, gain_here, hidden_ref, one_ref, two_ref,
    key_x, query_x, val_x, scores, total, out_c, in_c, rin,
    ag_sems, wo_sems, rs_sems, share_sems, block_sems, a0_sems, a1_sems, f0_sems, f1_sems, swap, gain_sems, loads,
    homing,
):
    at = spot()
    y, x, c, h, p = at
    rows = x_here.shape[0]
    far = far_role(at)
    stage = Stage(loads)
    partner, above = (y, x, c, 1 - h, p), (1 - y, x, c, h, p)
    size = f_ref.shape[1] // 4
    a_pushes = [
        ToHeads(at, layer, slices(a_ref, HS), columns(into), relay, sems)
        for layer, into, relay, sems in ((0, a0, a0_relay, a0_sems), (1, a1, a1_relay, a1_sems))
    ]
    f_pushes = [
        ToHeads(at, layer, slices(f_ref, size), columns(into), relay, sems)
        for layer, into, relay, sems in ((0, f0, f0_relay, f0_sems), (1, f1, f1_relay, f1_sems))
    ]
    home = ToHome(at, 0, out_ref, lambda m: home_ref.at[m], homing)
    share = ToRows(at, lambda b: low_ref.at[:, pl.ds(b * rows, rows)], lambda b: att_in.at[b], share_sems)
    greet(at, *a_pushes, *f_pushes, home, peers=(partner,))
    swapped = remote(in_ref.at[1 - h], x_here, swap.at[0], swap.at[1], partner)
    stays = pltpu.make_async_copy(in_ref.at[h], x_here, swap.at[2])

    @pl.when(far == 1)
    def _():
        swapped.start()

    @pl.when(far == 0)
    def _():
        stays.start()

    across = remote(gain_ref, gains.at[y], gain_sems.at[0], gain_sems.at[1], above)
    across.start()
    keeps = pltpu.make_async_copy(gain_ref, gains.at[y], gain_sems.at[2])
    keeps.start()
    for push in a_pushes:
        push.start_relay()
    a_pushes[0].start()
    for push in f_pushes:
        push.start_relay()
    a_pushes[0].forward()
    keeps.wait()
    across.wait_send()
    remote(gain_ref, gains.at[1 - y], gain_sems.at[0], gain_sems.at[1], above).wait_recv()
    gain_copy = stage.copy(gains, gain_here)

    @pl.when(far == 1)
    def _():
        swapped.wait()

    @pl.when(far == 0)
    def _():
        stays.wait()

    gain_copy.wait()
    buf[block_of(at)] = (unit_of(x_here[...].astype(F32))[0] * gain_here[0, 0:1]).astype(LOW)

    def ready():
        a_pushes[0].finish()
        copy = stage.copy(a0, a_here)
        for push in (a_pushes[1], f_pushes[0]):
            push.start()
            push.forward()
        copy.wait()

    keep = (normed0_far, block_sems)
    gather(at, buf, ag_sems, lambda b: project_block(b, buf, a_here, cos_ref, sin_ref, None, qkv0_ref), keep, ready)
    wo_all[block_of(at)] = a_here[3]
    attend_and_share(
        at, gathering(at, wo_all, wo_sems), share, lambda: kept(buf, keep),
        qkv0_ref, seg_ref, att_ref, low_ref, lse_ref, key_x, query_x, val_x, scores,
    )
    middle = out_project(at, share, att_in, wo_all, x_here)
    middle_ref[...] = middle
    buf[block_of(at)] = (unit_of(middle)[0] * gain_here[0, 1:2]).astype(LOW)
    keep = (nmid_far, block_sems)

    def more():
        f_pushes[0].finish()
        copy = stage.copy(f0, f_here)
        f_pushes[1].start()
        f_pushes[1].forward()
        copy.wait()

    gather(at, buf, ag_sems, lambda b: up_block(b, buf, f_here, hidden_ref, one_ref, two_ref), keep, more)
    saves = [stage.copy(*pair) for pair in ((hidden_ref, hidden_far), (one_ref, one_far), (two_ref, two_far))]
    boxes = (out_c, in_c, rin)
    scatter(
        at, total, boxes, rs_sems, lambda b: dot(hidden_ref[span(b, rows)], f_here[2]), lambda: kept(buf, keep)
    )
    out = (middle_ref[...] + total[...]).astype(LOW)
    out_ref[...] = out
    home.start()
    buf[block_of(at)] = (unit_of(out.astype(F32))[0] * gain_here[1, 0:1]).astype(LOW)
    keep = (normed1_far, block_sems)

    def last():
        a_pushes[1].finish()
        stage.copy(a1, a_here).wait()

    mix_ref = qkv0_ref.at[pl.ds(2 * HS, HS)]
    gather(
        at, buf, ag_sems, lambda b: project_block(b, buf, a_here, cos_ref, sin_ref, mix_ref, qkv1_ref), keep, last
    )
    kept(buf, keep)
    for save in saves:
        save.wait()
    home.finish()
    f_pushes[1].finish()


def turn_kernel(
    qkv_ref, seg_ref, a_ref, f_ref, gain_ref, x_ref, top_ref,
    att_ref, lse_ref, att_in, dmid_ref, gain_grad_ref, dout_ref, f_grad_ref, middle_ref, hidden_far,
    buf, nmid, wo_all, low_ref, dout_block, total, out_c, in_c, rin,
    ag_sems, wo_sems, rs_sems, share_sems, back_sems, loads,
):
    at = spot()
    rows = x_ref.shape[0]
    share = ToRows(at, lambda b: low_ref.at[:, pl.ds(b * rows, rows)], lambda b: att_in.at[b], share_sems)

    def column(b):
        start = b * rows
        return dout_ref.at[:, pl.ds(start if isinstance(b, int) else pl.multiple_of(start, rows), rows)]

    back = ToRows(at, lambda b: dout_block.at[b], column, back_sems)
    greet(at)
    wo_all[block_of(at)] = a_ref[3]
    buf[block_of(at)] = top_ref[...]
    steps = taking_turns(gathering(at, wo_all, wo_sems), gathering(at, buf, ag_sems))
    pl.run_scoped(
        functools.partial(attend_and_share, at, steps, share, None, qkv_ref, seg_ref, att_ref, low_ref, lse_ref),
        *attend_scratch(qkv_ref.shape[1]),
    )
    middle = out_project(at, share, att_in, wo_all, x_ref)
    middle_ref[...] = middle
    nmid[block_of(at)] = (unit_of(middle)[0] * gain_ref[...]).astype(LOW)

    def rest(hidden_ref, one_ref, two_ref, sums_ref):
        sums_ref[...] = jnp.zeros_like(sums_ref)

        def both_ways(b):
            up_block(b, nmid, f_ref, hidden_ref, one_ref, two_ref)
            hidden_back(b, buf, f_ref, hidden_ref, one_ref, two_ref, sums_ref)

        gather(at, nmid, ag_sems, both_ways)
        save = Stage(loads).copy(hidden_ref, hidden_far)
        boxes = (out_c, in_c, rin)
        down_back(
            at, lambda: top_ref[...].astype(F32), True, buf, held(nmid), total, boxes, ag_sems, rs_sems, f_ref, hidden_ref, one_ref,
            two_ref, gain_ref, middle_ref, sums_ref, wo_all, dout_block, back, dmid_ref, gain_grad_ref,
        )
        f_grad_ref[...] = sums_ref[...].astype(LOW)
        save.wait()

    pl.run_scoped(rest, *feed_scratch(qkv_ref.shape[1], f_ref))


def input_back(
    at, dqkv_ref, a_ref, x_ref, gain_ref, dmid_ref, gain_grad_ref, total, boxes, rs_sems, normed, load, sum_ref, after
):
    rows, width = total.shape

    def weight_sum():
        load.wait()
        sum_ref[...] = jnp.zeros_like(sum_ref)

        def one(b, none):
            sum_ref[...] += dot(dqkv_ref[:, span(b, rows)], normed[b])
            return none

        lax.fori_loop(0, 16, one, 0)
        after()

    def partial(b):
        return dot(dqkv_ref[:, span(b, rows)], a_ref[:3].reshape(3 * HS, width), TN)

    scatter(at, total, boxes, rs_sems, partial, weight_sum)
    grad, gain_grad = back_of(total[...], x_ref[...].astype(F32), gain_ref[...])
    gain_grad_ref[...] = gain_grad
    return grad + dmid_ref[...]


def staged_scratch(refs):
    return [pltpu.VMEM(ref.shape, ref.dtype) for ref in refs]


def attend_back_staged(stage, far, outs, steps, early, *refs):
    near, scratch = refs[: len(far)], refs[len(far) :]
    copies = [stage.copy(*pair) for pair in zip(far, near)]
    for _ in range(early):
        next(steps, None)
    for copy in copies:
        copy.wait()
    attend_back_body(*near, *outs, *scratch, lambda ki: next(steps, None))
    run(steps)


def out_weight_steps(at, total, boxes, sems, att_in, dmid_ref, low_ref):
    low_ref[...] = dmid_ref[...].astype(LOW)
    return scattering(at, total, boxes, sems, lambda b: dot(att_in[b], low_ref[...]))


def put_grads(a_grad_ref, in_sum_ref, out_total):
    for i in range(3):
        a_grad_ref[i] = in_sum_ref[i * HS : (i + 1) * HS].astype(LOW)
    a_grad_ref[3] = out_total[...].astype(LOW)


def by_columns(ref):
    wide = ref.shape[-1] // 4
    return lambda k: ref.at[:, :, pl.ds(k * wide, wide)]


def lower_kernel(
    a_ref, gain_in_ref, dmid_above, att_in, gain_mid_ref,
    x_far, f_far, middle_far, qkv_far, seg_far, att_far, lse_far, dout_far, cos_far, sin_far,
    hidden_far, one_far, two_far, normed_far, nmid_far, wo_far, hidden_above, middle_above, f_above, f_grad_above,
    send_ref, gain_in_grad_ref, dmid_ref, gain_mid_grad_ref, dout_ref, f_grad_ref, a_grad_ref, home_ref, out_home, f_in_far,
    buf, wo_all, dqkv_ref, low_ref, out_ref, in_sum_ref, dout_block,
    total, out_c, in_c, rin, out_total, out_c2, in_c2, rin2,
    ag_sems, rs_sems, rs2_sems, back_sems, f_sems, homing, out_homing, loads, ring_sems,
):
    at = spot()
    rows = low_ref.shape[0]
    stage = Stage(loads)
    normed_copy = stage.copy(normed_far, buf)
    wo_copy = stage.copy(wo_far, wo_all)
    length = dqkv_ref.shape[1]
    home = ToHome(at, 1, low_ref, lambda m: home_ref.at[m], homing)
    out = ToHome(at, 1, out_ref, lambda m: out_home.at[m], out_homing)

    def column(b):
        start = b * rows
        return dout_ref.at[:, pl.ds(start if isinstance(b, int) else pl.multiple_of(start, rows), rows)]

    back = ToRows(at, lambda b: dout_block.at[b], column, back_sems)
    push = ToShards(at, 1, by_columns(f_grad_above), lambda role, j: f_in_far.at[j], f_sems, (1,))
    greet(at, home, out, push)
    push.start()
    boxes = (out_c, in_c, rin)

    def out_steps(hidden_ref, down_ref):
        yield from scattering(
            at, total, boxes, rs_sems, lambda b: dot(hidden_ref[span(b, rows)], down_ref[...])
        )
        out_ref[...] = (dmid_ref[...] + total[...]).astype(LOW)
        out.start()

    def weight_steps():
        for _ in range(5):
            yield
        yield from out_weight_steps(at, out_total, (out_c2, in_c2, rin2), rs2_sems, att_in, dmid_above, low_ref)

    def attention(hidden_ref, down_ref, *refs):
        copies = [
            stage.copy(*pair)
            for pair in ((hidden_above, hidden_ref), (f_above.at[2], down_ref), (middle_above, dmid_ref))
        ]
        for copy in copies:
            copy.wait()
        steps = taking_turns(out_steps(hidden_ref, down_ref), weight_steps())
        attend_back_staged(
            stage, (qkv_far, seg_far, att_far, lse_far, dout_far, cos_far, sin_far), (None, dqkv_ref, send_ref),
            steps, 3, *refs,
        )

    pl.run_scoped(
        attention,
        pltpu.VMEM(hidden_above.shape, LOW),
        pltpu.VMEM(f_above.shape[1:], LOW),
        *staged_scratch((qkv_far, seg_far, att_far, lse_far, dout_far, cos_far, sin_far)),
        *attend_back_scratch(length),
    )

    def after():
        put_grads(a_grad_ref, in_sum_ref, out_total)

    def rest(hidden_ref, one_ref, two_ref, sums_ref, x_ref, f_ref, middle_ref, ring):
        blocks = streamed(nmid_far, ring, ring_sems)
        pairs = (
            (x_far, x_ref),
            (f_far, f_ref),
            (middle_far, middle_ref),
            (hidden_far, hidden_ref),
            (one_far, one_ref),
            (two_far, two_ref),
        )
        copies = [stage.copy(*pair) for pair in pairs]
        copies.pop(0).wait()
        grad = input_back(
            at, dqkv_ref, a_ref, x_ref, gain_in_ref, dmid_above, gain_in_grad_ref, total, boxes, rs_sems, buf,
            normed_copy, in_sum_ref, after,
        )
        dmid_ref[...] = grad
        low_ref[...] = grad.astype(LOW)
        home.start()
        for copy in copies + [wo_copy]:
            copy.wait()
        down_back(
            at, lambda: dmid_ref[...], False, buf, blocks, total, boxes, ag_sems, rs_sems, f_ref, hidden_ref, one_ref, two_ref,
            gain_mid_ref, middle_ref, sums_ref, wo_all, dout_block, back, dmid_ref, gain_mid_grad_ref,
        )
        f_grad_ref[...] = sums_ref[...].astype(LOW)

    ring_type = pltpu.VMEM((8, *nmid_far.shape[1:]), LOW)
    pl.run_scoped(rest, *feed_scratch(length, f_far), *staged_scratch((x_far, f_far, middle_far)), ring_type)
    home.finish()
    out.finish()
    push.finish()


def last_kernel(
    qkv_ref, seg_ref, att_ref, lse_ref, dout_in, cos_ref, sin_ref, extra_ref, x_ref, a_ref, gain_ref, dmid_ref,
    att_in, gains_ref, f_grad, f_above, a_above, normed_far,
    home_ref, f_in, f_in_above, a_in, a_in_above, gain_sum,
    buf, dqkv_ref, low_ref, in_sum_ref, a_grad_ref, gain_grad_ref, heard,
    key_x, val_x, query_x, dout_x, dq, scores, along,
    total, out_c, in_c, rin, out_total, out_c2, in_c2, rin2,
    rs_sems, rs2_sems, f_sems, f1_sems, a_sems, a1_sems, homing, gain_sems, loads,
):
    at = spot()
    y, x, c, h, p = at
    copy = Stage(loads).copy(normed_far, buf)
    home = ToHome(at, 0, low_ref, lambda m: home_ref.at[m], homing)
    early = [
        ToShards(at, layer, by_columns(ref), place, sems, roles)
        for layer, ref, place, sems, roles in (
            (1, f_above, lambda role, j: f_in_above.at[j], f1_sems, (0,)),
            (0, f_grad, lambda role, j: f_in.at[role, j], f_sems, (0, 1)),
            (1, a_above, lambda role, j: a_in_above.at[role, j], a1_sems, (0, 1)),
        )
    ]
    a_push = ToShards(at, 0, by_columns(a_grad_ref), lambda role, j: a_in.at[role, j], a_sems)
    peers = [moved(at, 0, 1), moved(at, 1), moved(at, 2), moved(at, 4), (y, x, c, 1 - h, p)]
    greet(at, home, a_push, *early, peers=peers[4:])
    for push in early:
        push.start()
    steps = out_weight_steps(at, out_total, (out_c2, in_c2, rin2), rs2_sems, att_in, dmid_ref, low_ref)
    attend_back_body(
        qkv_ref, seg_ref, att_ref, lse_ref, dout_in, cos_ref, sin_ref, extra_ref, dqkv_ref, None,
        key_x, val_x, query_x, dout_x, dq, scores, along, lambda ki: next(steps, None),
    )
    run(steps)

    def after():
        put_grads(a_grad_ref, in_sum_ref, out_total)
        a_push.start()

    grad = input_back(
        at, dqkv_ref, a_ref, x_ref, gain_ref, dmid_ref, gain_grad_ref, total, (out_c, in_c, rin), rs_sems, buf, copy,
        in_sum_ref, after,
    )
    low_ref[...] = grad.astype(LOW)
    home.start()
    gain_sum[0, 0:1] = gain_grad_ref[...]
    gain_sum[0, 1:4] = gains_ref[...]
    for i, peer in enumerate(peers):
        copy = remote(gain_sum.at[i], heard.at[i], gain_sems.at[0, i], gain_sems.at[1, i], peer)
        copy.start()
        copy.wait()
        gain_sum[i + 1] = gain_sum[i] + heard[i]
    for push in early:
        push.finish()
    a_push.finish()
    home.finish()


VMEM_SPEC = pl.BlockSpec(memory_space=pltpu.VMEM)
ANY_SPEC = pl.BlockSpec(memory_space=pl.ANY)


def links():
    dma = pltpu.SemaphoreType.DMA
    return (dma((3, 8)), dma((3, 8)), dma((8,)), dma((8,)))


def sum_boxes(rows, width):
    return [
        pltpu.VMEM((rows, width), F32),
        pltpu.VMEM((4, rows, width), LOW),
        pltpu.VMEM((8, rows, width), LOW),
        pltpu.VMEM((7, rows, width), LOW),
    ]


def reach(kernel, number, args, outs, scratch, name, far=()):
    return pl.pallas_call(
        kernel,
        out_shape=[jax.ShapeDtypeStruct(shape, dtype) for shape, dtype, _ in outs],
        in_specs=[VMEM_SPEC] * len(args) + [ANY_SPEC] * len(far),
        out_specs=[ANY_SPEC if stays else VMEM_SPEC for _, _, stays in outs],
        scratch_shapes=scratch,
        compiler_params=pltpu.CompilerParams(
            collective_id=number, has_side_effects=number is not None, vmem_limit_bytes=VMEM_BYTES
        ),
        name=name,
    )(*args, *far)


TILE = 512
MORE = 16
DOC_ROOM = 13
FLOOR = -1e20


def one_hot(seg_ref, part):
    rows = lax.broadcasted_iota(jnp.int32, (MORE, TILE), 0)
    return (rows, rows == seg_ref[:, part])


def tiles(length):
    return [slice(i * TILE, (i + 1) * TILE) for i in range(length // TILE)]


def causal():
    return lax.broadcasted_iota(jnp.int32, (TILE, 1), 0) <= lax.broadcasted_iota(jnp.int32, (1, TILE), 1)


def attend_body(qkv_ref, seg_ref, att_ref, low_ref, lse_ref, key_x, query_x, val_x, scores, after):
    length = qkv_ref.shape[1]
    for part in tiles(length):
        rows, hot = one_hot(seg_ref, part)
        key = jnp.concatenate([qkv_ref[HS : 2 * HS, part].astype(F32), jnp.where(hot, 1.0, 0.0)])
        key_x[part] = key.T.astype(LOW)
        query_x[:HS, part] = qkv_ref[:HS, part]
        query_x[HS:, part] = jnp.where(hot | (rows >= DOC_ROOM), 0.0, NEGATIVE).astype(LOW)
        val_x[:HS, part] = qkv_ref[2 * HS :, part]
        val_x[HS:, part] = jnp.where(rows == 0, 1.0, 0.0).astype(LOW)

    def query_tile(qi):
        cols = slice(qi * TILE, (qi + 1) * TILE)
        query = query_x[:, cols]

        def ahead(slot, kb):
            scores[slot] = dot(key_x[span(kb, TILE)], query)

        def update(slot, kb, state, diagonal=False):
            largest, summed = state
            found = scores[slot]
            if diagonal:
                found = jnp.where(causal(), found, NEGATIVE)
            newest = jnp.maximum(largest, jnp.max(found, axis=0, keepdims=True))
            weights = jnp.exp(found - newest).astype(LOW)
            summed = summed * jnp.exp(largest - newest) + dot(val_x[:, span(kb, TILE)], weights)
            return (newest, summed)

        def pair(i, state):
            ahead(1, 2 * i + 1)
            state = update(0, 2 * i, state)
            ahead(0, 2 * i + 2)
            return update(1, 2 * i + 1, state)

        state = (jnp.full((1, TILE), FLOOR, F32), jnp.zeros((HS + MORE, TILE), F32))
        ahead(0, 0)
        state = lax.fori_loop(0, qi // 2, pair, state)
        if qi % 2:
            ahead(1, qi)
            state = update(0, qi - 1, state)
        largest, summed = update(qi % 2, qi, state, True)
        totals = summed[HS : HS + 1]
        attended = summed[:HS] / totals
        att_ref[:, cols] = attended
        low_ref[:, cols] = attended.astype(LOW)
        lse_ref[:, cols] = largest + jnp.log(totals)

    for qi in range(length // TILE):
        query_tile(qi)
        after(qi)


def attend_scratch(length):
    return [
        pltpu.VMEM((length, HS + MORE), LOW),
        pltpu.VMEM((HS + MORE, length), LOW),
        pltpu.VMEM((HS + MORE, length), LOW),
        pltpu.VMEM((2, TILE, TILE), F32),
    ]


def three(values):
    high = values.astype(LOW).astype(F32)
    mid = (values - high).astype(LOW).astype(F32)
    return (high, mid, values - high - mid)


def attend_back_body(
    qkv_ref, seg_ref, att_ref, lse_ref, dout_ref, cos_ref, sin_ref, extra_ref, dqkv_ref, send_ref,
    key_x, val_x, query_x, dout_x, dq, scores, along, after,
):
    length = qkv_ref.shape[1]
    half, count = HS // 2, length // TILE
    for part in tiles(length):
        rows, hot = one_hot(seg_ref, part)
        ones = jnp.where(rows >= DOC_ROOM, 1.0, 0.0)
        key = jnp.concatenate([qkv_ref[HS : 2 * HS, part].astype(F32), jnp.where(hot, 1.0, ones)])
        key_x[part] = key.T.astype(LOW)
        val_x[part] = jnp.concatenate([qkv_ref[2 * HS :, part].astype(F32), ones]).T.astype(LOW)

        def tail(values, rest, rows=rows):
            for i, piece in enumerate(three(values)):
                rest = jnp.where(rows == DOC_ROOM + i, piece, rest)
            return rest.astype(LOW)

        dout = dout_ref[:, part]
        delta = jnp.sum(dout.astype(F32) * att_ref[:, part], axis=0, keepdims=True)
        query_x[:HS, part] = qkv_ref[:HS, part]
        query_x[HS:, part] = tail(-lse_ref[:, part], jnp.where(hot, 0.0, NEGATIVE))
        dout_x[:HS, part] = dout
        dout_x[HS:, part] = tail(-delta, jnp.zeros((MORE, TILE), F32))
    dq[...] = jnp.zeros_like(dq)

    def key_tile(ki):
        here = slice(ki * TILE, (ki + 1) * TILE)
        rest = count - 1 - ki

        def ahead(slot, qb):
            cols = span(qb, TILE)
            scores[slot] = dot(key_x[here], query_x[:, cols])
            along[slot] = dot(val_x[here], dout_x[:, cols])

        def update(slot, qb, state, diagonal=False):
            dk, dv = state
            cols = span(qb, TILE)
            weights = jnp.exp(scores[slot])
            if diagonal:
                weights = jnp.where(causal(), weights, 0.0)
            ds = (weights * along[slot]).astype(LOW)
            dv = dv + dot(dout_x[:HS, cols], weights.astype(LOW), NT)
            dk = dk + dot(query_x[:HS, cols], ds, NT)
            dq[:, cols] += dot(qkv_ref[HS : 2 * HS, here], ds)
            return (dk, dv)

        def pair(i, state):
            qb = ki + 1 + 2 * i
            ahead(0, qb + 1)
            state = update(1, qb, state)
            ahead(1, qb + 2)
            return update(0, qb + 1, state)

        zero = jnp.zeros((HS, TILE), F32)
        ahead(0, ki)
        if rest:
            ahead(1, ki + 1)
        state = update(0, ki, (zero, zero), True)
        state = lax.fori_loop(0, max(0, (rest - 1) // 2), pair, state)
        if rest % 2:
            state = update(1, count - 1, state)
        elif rest:
            ahead(0, count - 1)
            state = update(1, count - 2, state)
            state = update(0, count - 1, state)
        dk, dv = state
        a, b = turned(dk[:half], dk[half:], cos_ref[:, here], -sin_ref[:, here])
        dqkv_ref[HS : HS + half, here] = a.astype(LOW)
        dqkv_ref[HS + half : 2 * HS, here] = b.astype(LOW)
        if send_ref is None:
            dqkv_ref[2 * HS :, here] = (dv + extra_ref[:, here]).astype(LOW)
        else:
            dqkv_ref[2 * HS :, here] = (0.5 * dv).astype(LOW)
            send_ref[:, here] = 0.5 * dv

    for ki in range(count):
        key_tile(ki)
        after(ki)
    scale = HS**-0.5
    a, b = turned(dq[:half] * scale, dq[half:] * scale, cos_ref[...], -sin_ref[...])
    dqkv_ref[:half] = a.astype(LOW)
    dqkv_ref[half:HS] = b.astype(LOW)


def attend_back_scratch(length):
    wide = HS + MORE
    return [
        pltpu.VMEM((length, wide), LOW),
        pltpu.VMEM((length, wide), LOW),
        pltpu.VMEM((wide, length), LOW),
        pltpu.VMEM((wide, length), LOW),
        pltpu.VMEM((HS, length), F32),
        pltpu.VMEM((2, TILE, TILE), F32),
        pltpu.VMEM((2, TILE, TILE), F32),
    ]


def number_of(y, s, z):
    return (y * 4 + s) * 4 + z


def far_pairs():
    return [
        (number_of(y, s, z), number_of(y, s, (z + 2) % 4))
        for y in range(2)
        for s in range(4)
        for z in range(4)
        if (y + s) % 2
    ]


AXES = ("section", "seq", "tensor")


def on_grid(
    inputs, cotangent, lengths, w_query, w_key, w_value, w_out, w_gate, w_up, w_down, attn_gain, mlp_gain
):
    at = spot()
    y, x, c, half, p = at
    far = far_role(at) == 1
    rows, width = inputs.shape[1:]
    length = 16 * rows
    units = w_gate.shape[2] // 4
    length_row = lax.dynamic_index_in_dim(lengths, half, 0, keepdims=False)
    places = jnp.arange(length, dtype=jnp.int32)
    segment, within = doc_table(length_row, places)
    segment = segment[None]
    frequency = jnp.exp(jnp.arange(HS // 2, dtype=F32) * (-math.log(10000.0) / (HS // 2)))
    angles = within.astype(F32)[None, :] * frequency[:, None]
    tables = [jnp.cos(angles), jnp.sin(angles)]
    a_own = jnp.stack([w_query[0].T, w_key[0].T, w_value[0].T, w_out[0]])
    f_own = jnp.stack([w_gate[0].T, w_up[0].T, w_down[0]])
    dma = pltpu.SemaphoreType.DMA

    def vmem(*shape, dtype=LOW):
        return pltpu.VMEM(shape, dtype)

    def near(*shape, dtype=LOW):
        return (shape, dtype, False)

    def stays(*shape, dtype=LOW):
        return (shape, dtype, True)

    buf = [vmem(16, rows, width)]
    boxes = sum_boxes(rows, width)
    small_boxes = sum_boxes(HS, width)
    wo_buf = [vmem(16, HS, width)]
    low_head = [vmem(HS, length)]
    block, low_block = [vmem(rows, width, dtype=F32)], [vmem(rows, width)]
    hidden = [vmem(length, units)] * 3
    dout_block = [vmem(16, HS, rows)]
    in_sum = [vmem(3 * HS, width, dtype=F32), vmem(4, HS, width)]
    turned_out, head_out, lse_out = near(3 * HS, length), near(HS, length, dtype=F32), near(1, length, dtype=F32)
    att_in_out, every = near(16, HS, rows), stays(16, rows, width)
    block_out, low_out, gain_out = near(rows, width, dtype=F32), near(rows, width), near(1, width, dtype=F32)
    dout_out, f_out = near(HS, length), near(3, units, width)
    hidden_far, home_out = stays(length, units), stays(2, rows, width)
    a_far, f_far = stays(4, HS, width), stays(3, units, width)
    f_half = stays(4, 3, units, width // 4)
    a_shards, f_shards = stays(2, 4, 4, HS, width // 4), stays(2, 4, 3, units, width // 4)

    both = lax.dynamic_index_in_dim(cotangent, 1 - half, 0, keepdims=False)
    own_top = jnp.where(
        far,
        lax.ppermute(both, AXES, far_pairs()),
        lax.dynamic_index_in_dim(cotangent, half, 0, keepdims=False),
    )
    (
        qkv0, att0, lse0, att_in0, wo_all0, own_in, mid0, out0, qkv1,
        normed0, nmid0, normed1, hid0, one0, two0, home_out0, a0, a1, f0, f1, gains, *_,
    ) = reach(
        first_kernel,
        0,
        [*tables, segment],
        [turned_out, head_out, lse_out, att_in_out, near(16, HS, width), low_out, block_out, low_out, turned_out]
        + [every] * 3
        + [hidden_far] * 3
        + [home_out, a_far, a_far, f_far, f_far, stays(2, 2, width, dtype=F32)]
        + [stays(2, 4, HS, width // 4)] * 2
        + [stays(2, 3, units, width // 4)] * 2,
        buf
        + low_head
        + [vmem(4, HS, width), vmem(3, units, width), vmem(2, 2, width, dtype=F32)]
        + hidden
        + attend_scratch(length)
        + boxes
        + [links(), links(), links(), row_sems(), dma((16,))]
        + [head_sems()] * 4
        + [dma((3,)), dma((3,)), dma((7,)), home_sems()],
        "first",
        [inputs, a_own, f_own, jnp.concatenate([attn_gain, mlp_gain])],
    )
    gain_in, gain_mid = [gains[i, 0:1] for i in range(2)], [gains[i, 1:2] for i in range(2)]
    att1, lse1, att_in1, dmid1, gmid1, dout1, f_grad1, mid1, hid1 = reach(
        turn_kernel,
        1,
        [qkv1, segment, a1, f1, gain_mid[1], out0, own_top],
        [head_out, lse_out, att_in_out, block_out, gain_out, dout_out, f_out, block_out, hidden_far],
        buf
        + buf
        + wo_buf
        + low_head
        + dout_block
        + boxes
        + [links(), links(), links(), row_sems(), row_sems(), dma((1,))],
        "turn",
    )
    extra, gin1, dmid0, gmid0, dout0, f_grad0, a_grad1, home_grad1, home_out1, f_far1 = reach(
        lower_kernel,
        2,
        [a1, gain_in[1], dmid1, att_in1, gain_mid[0]],
        [head_out, gain_out, block_out, gain_out, dout_out, f_out, near(4, HS, width), home_out, home_out, f_half],
        buf
        + wo_buf
        + [vmem(3 * HS, length)]
        + low_block
        + low_block
        + in_sum[:1]
        + dout_block
        + boxes
        + small_boxes
        + [links(), links(), links(), row_sems(), shard_sems(), home_sems(), home_sems()]
        + [dma((18,)), dma((8,))],
        "lower",
        [out0, f0, mid0, qkv1, segment, att1, lse1, dout1, *tables, hid0, one0, two0, normed1, nmid0, wo_all0]
        + [hid1, mid1, f1, f_grad1],
    )
    home_grad0, f_in0, f_near1, a_in0, a_in1, gain_sums = reach(
        last_kernel,
        3,
        [qkv0, segment, att0, lse0, dout0, *tables, extra, own_in, a0, gain_in[0], dmid0, att_in0]
        + [jnp.concatenate([gin1, gmid0, gmid1])],
        [home_out, f_shards, f_half, a_shards, a_shards, near(6, 4, width, dtype=F32)],
        buf
        + [vmem(3 * HS, length)]
        + low_block
        + in_sum
        + [vmem(1, width, dtype=F32), vmem(5, 4, width, dtype=F32)]
        + attend_back_scratch(length)
        + boxes
        + small_boxes
        + [links(), links()]
        + [shard_sems()] * 4
        + [home_sems(), dma((2, 5)), dma((1,))],
        "last",
        [f_grad0, f_grad1, a_grad1, normed0],
    )
    on_first = y == 0
    a_sum = jnp.sum(jnp.where(on_first, a_in0, a_in1).astype(F32), axis=0)
    f_total = jnp.where(on_first, f_in0[0], f_near1).astype(F32) + jnp.where(on_first, f_in0[1], f_far1).astype(F32)
    a_sum = jnp.transpose(a_sum, (1, 0, 2, 3)).reshape(4, 4 * HS, width // 4)
    f_total = jnp.transpose(f_total, (1, 0, 2, 3)).reshape(3, 4 * units, width // 4)
    layer_out = jnp.where(on_first, home_out0, home_out1)
    input_grad = jnp.where(on_first, home_grad0, home_grad1).astype(F32)
    share = width // 16
    first_col = (4 * (2 * x + c) + 2 * half + p) * share
    gain_share = lax.dynamic_slice_in_dim(gain_sums[5], first_col, share, 1)
    gain_in_share = jnp.where(on_first, gain_share[0:1], gain_share[1:2])
    gain_mid_share = jnp.where(on_first, gain_share[2:3], gain_share[3:4])
    return (
        layer_out[None],
        input_grad[None],
        a_sum[0].T[None],
        a_sum[1].T[None],
        a_sum[2].T[None],
        a_sum[3][None],
        f_total[0].T[None],
        f_total[1].T[None],
        f_total[2][None],
        gain_in_share,
        gain_mid_share,
    )


def solution(mesh):
    in_specs = (
        P(None, ("seq", "tensor"), None),
        P(None, ("seq", "tensor"), None),
        P(),
        P("section", "seq", "tensor"),
        P("section", "seq", "tensor"),
        P("section", "seq", "tensor"),
        P("section", "tensor", "seq"),
        P("section", "seq", "tensor"),
        P("section", "seq", "tensor"),
        P("section", "tensor", "seq"),
        P("section", None),
        P("section", None),
    )
    out_specs = (
        P("section", None, ("seq", "tensor"), None),
        P("section", None, ("seq", "tensor"), None),
        P("section", "seq", "tensor"),
        P("section", "seq", "tensor"),
        P("section", "seq", "tensor"),
        P("section", "tensor", "seq"),
        P("section", "seq", "tensor"),
        P("section", "seq", "tensor"),
        P("section", "tensor", "seq"),
        P("section", ("seq", "tensor")),
        P("section", ("seq", "tensor")),
    )
    grid = (mesh.shape["section"], mesh.shape["seq"], mesh.shape["tensor"]) == (2, 4, 4)
    return jax.shard_map(
        on_grid if grid else on_device, mesh=mesh, in_specs=in_specs, out_specs=out_specs, check_vma=False
    )
```

```python
import functools
import math

import jax
import jax.numpy as jnp
from jax import lax
from jax.experimental import pallas as pl
from jax.experimental.pallas import tpu as pltpu
from jax.sharding import PartitionSpec as P

HS = 64


EPSILON = 1e-05
NEGATIVE = -1e30


def shifted(shard, axis, by):
    peers = lax.axis_size(axis)
    pairs = [(i, i + by) for i in range(peers) if 0 <= i + by < peers]
    return lax.ppermute(shard, axis, pairs)


def product(left, right):
    return jnp.dot(left, right, preferred_element_type=jnp.float32)


def inner_rows(left, right):
    return lax.dot_general(
        left, right, (((0,), (0,)), ((), ())), preferred_element_type=jnp.float32
    )


def against(left, right):
    return lax.dot_general(
        left, right, (((1,), (1,)), ((), ())), preferred_element_type=jnp.float32
    )


def doc_table(length_row, places):
    doc_ends = jnp.cumsum(length_row)
    doc_starts = doc_ends - length_row
    segment = jnp.sum((places[:, None] >= doc_ends[None, :]).astype(jnp.int32), axis=1)
    member = segment[:, None] == jnp.arange(length_row.shape[0], dtype=jnp.int32)[None, :]
    offset = jnp.sum(jnp.where(member, doc_starts[None, :], 0), axis=1)
    return (segment, places - offset)


def rotate(matrix, within, direction):
    row_count = matrix.shape[0]
    head_count = matrix.shape[1] // HS
    half_size = HS // 2
    frequency = jnp.exp(jnp.arange(half_size, dtype=jnp.float32) * (-math.log(10000.0) / half_size))
    angles = within.astype(jnp.float32)[:, None] * frequency[None, :]
    cosine = jnp.cos(angles)[:, None, :]
    sine_part = direction * jnp.sin(angles)[:, None, :]
    paired = matrix.reshape(row_count, head_count, 2, half_size)
    former = paired[:, :, 0, :]
    latter = paired[:, :, 1, :]
    turned = jnp.stack(
        [former * cosine - latter * sine_part, latter * cosine + former * sine_part], axis=2
    )
    return turned.reshape(row_count, head_count * HS)


def norm_rows(values, gain_row):
    inverse = lax.rsqrt(jnp.mean(values * values, axis=-1, keepdims=True) + EPSILON)
    unit_rows = values * inverse
    return (unit_rows, inverse, (unit_rows * gain_row).astype(jnp.bfloat16))


def norm_back(grad_normed, unit_rows, inverse, gain_row):
    shaped = grad_normed * gain_row
    inner = jnp.mean(shaped * unit_rows, axis=-1, keepdims=True)
    return (inverse * (shaped - unit_rows * inner), jnp.sum(grad_normed * unit_rows, axis=0))


def spread(values):
    return lax.all_gather(values, "tensor", axis=0, tiled=True)


def fold_rows(values):
    return lax.psum_scatter(
        values.astype(jnp.bfloat16), "tensor", scatter_dimension=0, tiled=True
    ).astype(jnp.float32)


def allowed_mask(places, segment, key_places, key_segment):
    return (key_places[None, :] <= places[:, None]) & (key_segment[None, :] == segment[:, None])


def project(normed_all, matrices, within, mixin, on_first):
    query_rows = rotate(product(normed_all, matrices[0]), within, 1.0).astype(jnp.bfloat16)
    key_rows = rotate(product(normed_all, matrices[1]), within, 1.0).astype(jnp.bfloat16)
    value_raw = product(normed_all, matrices[2])
    value_rows = jnp.where(
        on_first, value_raw, 0.5 * value_raw + 0.5 * mixin.astype(jnp.float32)
    ).astype(jnp.bfloat16)
    return (query_rows, key_rows, value_rows)


def cycle_attend(query_rows, key_rows, value_rows, places, segment, length_row):
    row_count = query_rows.shape[0]
    head_count = query_rows.shape[1] // HS
    query_heads = query_rows.reshape(row_count, head_count, HS)
    largest = jnp.full((head_count, row_count), NEGATIVE, jnp.float32)
    piece_keys = lax.all_gather(key_rows, "seq", axis=0, tiled=True)
    piece_values = lax.all_gather(value_rows, "seq", axis=0, tiled=True)
    piece_rows = piece_keys.shape[0]
    key_places = jnp.arange(piece_rows, dtype=jnp.int32)
    key_segment = doc_table(length_row, key_places)[0]
    allowed = allowed_mask(places, segment, key_places, key_segment)
    scores = jnp.einsum(
        "qhd,khd->hqk",
        query_heads,
        piece_keys.reshape(piece_rows, head_count, HS),
        preferred_element_type=jnp.float32,
    ) * HS ** (-0.5)
    masked = jnp.where(allowed[None], scores, NEGATIVE)
    newest = jnp.maximum(largest, jnp.max(masked, axis=2))
    weights = jnp.where(allowed[None], jnp.exp(masked - newest[:, :, None]), 0.0)
    totals = jnp.sum(weights, axis=2)
    summed = jnp.einsum(
        "hqk,khd->hqd",
        weights.astype(jnp.bfloat16),
        piece_values.reshape(piece_rows, head_count, HS),
        preferred_element_type=jnp.float32,
    )
    largest, totals, summed = (newest, totals, summed)
    attended = summed / totals[:, :, None]
    return jnp.transpose(attended, (1, 0, 2)).reshape(row_count, head_count * HS)


def forward_layer(residual, mixin, on_first, matrices, gain_pair, places, length_row):
    segment, within = doc_table(length_row, places)
    normed_in = norm_rows(residual, gain_pair[0])[2]
    normed_all = spread(normed_in)
    query_rows, key_rows, value_rows = project(normed_all, matrices, within, mixin, on_first)
    attended = cycle_attend(query_rows, key_rows, value_rows, places, segment, length_row)
    middle = residual + fold_rows(product(attended.astype(jnp.bfloat16), matrices[3]))
    normed_mid = norm_rows(middle, gain_pair[1])[2]
    normed_mid_all = spread(normed_mid)
    gate_rows = product(normed_mid_all, matrices[4])
    up_rows = product(normed_mid_all, matrices[5])
    hidden = (jax.nn.silu(gate_rows) * up_rows).astype(jnp.bfloat16)
    return (middle + fold_rows(product(hidden, matrices[6])), value_rows)


def backward_layer(
    residual, mixin, grad_top, extra_values, on_first, matrices, gain_pair, places, length_row
):
    segment, within = doc_table(length_row, places)
    unit_in, inverse_in, normed_in = norm_rows(residual, gain_pair[0])
    normed_all = spread(normed_in)
    query_rows, key_rows, value_rows = project(normed_all, matrices, within, mixin, on_first)
    all_keys, all_values = (
        lax.all_gather(key_rows, "seq", axis=0, tiled=True),
        lax.all_gather(value_rows, "seq", axis=0, tiled=True),
    )
    row_count = query_rows.shape[0]
    head_count = query_rows.shape[1] // HS
    total_rows = all_keys.shape[0]
    block_count = total_rows // row_count
    query_heads = query_rows.reshape(row_count, head_count, HS)
    key_blocks = all_keys.reshape(block_count, row_count, head_count, HS)
    value_blocks = all_values.reshape(block_count, row_count, head_count, HS)
    block_numbers = jnp.arange(block_count, dtype=jnp.int32)

    def block_scores(block_number, block_keys):
        key_places = block_number * row_count + jnp.arange(row_count, dtype=jnp.int32)
        key_segment = doc_table(length_row, key_places)[0]
        allowed = allowed_mask(places, segment, key_places, key_segment)
        scores = jnp.einsum(
            "qhd,khd->hqk", query_heads, block_keys, preferred_element_type=jnp.float32
        ) * HS ** (-0.5)
        return (allowed, jnp.where(allowed[None], scores, NEGATIVE))

    def first_pass(running, block_item):
        largest, totals, summed = running
        block_number, block_keys, block_values = block_item
        allowed, masked = block_scores(block_number, block_keys)
        newest = jnp.maximum(largest, jnp.max(masked, axis=2))
        rescale = jnp.exp(largest - newest)
        weights = jnp.where(allowed[None], jnp.exp(masked - newest[:, :, None]), 0.0)
        totals = totals * rescale + jnp.sum(weights, axis=2)
        summed = summed * rescale[:, :, None] + jnp.einsum(
            "hqk,khd->hqd",
            weights.astype(jnp.bfloat16),
            block_values,
            preferred_element_type=jnp.float32,
        )
        return ((newest, totals, summed), None)

    start_state = (
        jnp.full((head_count, row_count), NEGATIVE, jnp.float32),
        jnp.zeros((head_count, row_count), jnp.float32),
        jnp.zeros((head_count, row_count, HS), jnp.float32),
    )
    (largest, totals, summed), _ = lax.scan(
        first_pass, start_state, (block_numbers, key_blocks, value_blocks)
    )
    attended = summed / totals[:, :, None]
    attended_low = (
        jnp.transpose(attended, (1, 0, 2)).reshape(row_count, head_count * HS).astype(jnp.bfloat16)
    )
    middle = residual + fold_rows(product(attended_low, matrices[3]))
    unit_mid, inverse_mid, normed_mid = norm_rows(middle, gain_pair[1])
    normed_mid_all = spread(normed_mid)
    gate_rows = product(normed_mid_all, matrices[4])
    up_rows = product(normed_mid_all, matrices[5])
    sigmoid_gate = jax.nn.sigmoid(gate_rows)
    activated = gate_rows * sigmoid_gate
    hidden = (activated * up_rows).astype(jnp.bfloat16)
    grad_top_all = spread(grad_top.astype(jnp.bfloat16))
    grad_w_down = inner_rows(hidden, grad_top_all)
    grad_hidden = against(grad_top_all, matrices[6])
    grad_gate = (
        grad_hidden * up_rows * sigmoid_gate * (1.0 + gate_rows * (1.0 - sigmoid_gate))
    ).astype(jnp.bfloat16)
    grad_up = (grad_hidden * activated).astype(jnp.bfloat16)
    grad_w_gate = inner_rows(normed_mid_all, grad_gate)
    grad_w_up = inner_rows(normed_mid_all, grad_up)
    grad_normed_mid = fold_rows(against(grad_gate, matrices[4]) + against(grad_up, matrices[5]))
    grad_middle, grad_gain_mid = norm_back(grad_normed_mid, unit_mid, inverse_mid, gain_pair[1])
    grad_middle = grad_middle + grad_top
    grad_middle_all = spread(grad_middle.astype(jnp.bfloat16))
    grad_w_out = inner_rows(attended_low, grad_middle_all)
    grad_attended = against(grad_middle_all, matrices[3]).astype(jnp.bfloat16)
    grad_heads = jnp.transpose(grad_attended.reshape(row_count, head_count, HS), (1, 0, 2))
    delta = jnp.sum(grad_heads.astype(jnp.float32) * attended, axis=2)
    scaled_grad = grad_heads.astype(jnp.float32) / totals[:, :, None]
    scaled_high = scaled_grad.astype(jnp.bfloat16)
    scaled_rest = (scaled_grad - scaled_high.astype(jnp.float32)).astype(jnp.bfloat16)
    inverse_totals = 1.0 / totals[:, :, None]

    def second_pass(grad_sum, block_item):
        block_number, block_keys, block_values = block_item
        allowed, masked = block_scores(block_number, block_keys)
        weights = jnp.where(allowed[None], jnp.exp(masked - largest[:, :, None]), 0.0)
        low_weights = weights.astype(jnp.bfloat16)
        along = jnp.einsum(
            "hqd,khd->hqk", grad_heads, block_values, preferred_element_type=jnp.float32
        )
        grad_scores = (weights * inverse_totals * (along - delta[:, :, None])).astype(jnp.bfloat16)
        grad_sum = grad_sum + jnp.einsum(
            "hqk,khd->qhd", grad_scores, block_keys, preferred_element_type=jnp.float32
        ) * HS ** (-0.5)
        block_key_grad = jnp.einsum(
            "hqk,qhd->khd", grad_scores, query_heads, preferred_element_type=jnp.float32
        ) * HS ** (-0.5)
        block_value_grad = jnp.einsum(
            "hqk,hqd->khd", low_weights, scaled_high, preferred_element_type=jnp.float32
        ) + jnp.einsum("hqk,hqd->khd", low_weights, scaled_rest, preferred_element_type=jnp.float32)
        return (grad_sum, (block_key_grad, block_value_grad))

    grad_queries, (grad_keys, grad_values) = lax.scan(
        second_pass,
        jnp.zeros((row_count, head_count, HS), jnp.float32),
        (block_numbers, key_blocks, value_blocks),
    )
    own_keys, own_values = (
        lax.psum_scatter(
            grad_keys.reshape(total_rows, head_count * HS).astype(jnp.bfloat16),
            "seq",
            scatter_dimension=0,
            tiled=True,
        ).astype(jnp.float32),
        lax.psum_scatter(
            grad_values.reshape(total_rows, head_count * HS).astype(jnp.bfloat16),
            "seq",
            scatter_dimension=0,
            tiled=True,
        ).astype(jnp.float32),
    )
    grad_value_raw = jnp.where(on_first, own_values + extra_values, 0.5 * own_values).astype(
        jnp.bfloat16
    )
    send_values = 0.5 * own_values
    grad_query_raw = rotate(grad_queries.reshape(row_count, head_count * HS), within, -1.0).astype(
        jnp.bfloat16
    )
    grad_key_raw = rotate(own_keys, within, -1.0).astype(jnp.bfloat16)
    grad_w_query = inner_rows(normed_all, grad_query_raw)
    grad_w_key = inner_rows(normed_all, grad_key_raw)
    grad_w_value = inner_rows(normed_all, grad_value_raw)
    grad_normed_in = fold_rows(
        against(grad_query_raw, matrices[0])
        + against(grad_key_raw, matrices[1])
        + against(grad_value_raw, matrices[2])
    )
    grad_in, grad_gain_in = norm_back(grad_normed_in, unit_in, inverse_in, gain_pair[0])
    weight_terms = (
        grad_w_query,
        grad_w_key,
        grad_w_value,
        grad_w_out,
        grad_w_gate,
        grad_w_up,
        grad_w_down,
    )
    return (grad_in + grad_middle, send_values, weight_terms, (grad_gain_in, grad_gain_mid))


def on_device(
    inputs,
    cotangent,
    lengths,
    w_query,
    w_key,
    w_value,
    w_out,
    w_gate,
    w_up,
    w_down,
    attn_gain,
    mlp_gain,
):
    section_index = lax.axis_index("section")
    on_first = section_index == 0
    micro_count = inputs.shape[0]
    local_rows = inputs.shape[1]
    model_width = inputs.shape[2]
    group_rows = local_rows * lax.axis_size("tensor")
    head_width = w_query.shape[2]
    row_values = local_rows * model_width
    places = lax.axis_index("seq") * group_rows + jnp.arange(group_rows, dtype=jnp.int32)
    gain_pair = (attn_gain[0], mlp_gain[0])
    gathered = (
        lax.all_gather(w_query[0], "seq", axis=0, tiled=True),
        lax.all_gather(w_key[0], "seq", axis=0, tiled=True),
        lax.all_gather(w_value[0], "seq", axis=0, tiled=True),
        lax.all_gather(w_out[0], "seq", axis=1, tiled=True),
        lax.all_gather(w_gate[0], "seq", axis=0, tiled=True),
        lax.all_gather(w_up[0], "seq", axis=0, tiled=True),
        lax.all_gather(w_down[0], "seq", axis=1, tiled=True),
    )
    recv_rows = jnp.zeros((local_rows, model_width), jnp.bfloat16)
    recv_values = jnp.zeros((group_rows, head_width), jnp.bfloat16)
    kept_inputs = jnp.zeros((micro_count, local_rows, model_width), jnp.bfloat16)
    kept_values = jnp.zeros((micro_count, group_rows, head_width), jnp.bfloat16)
    kept_outputs = jnp.zeros((micro_count, local_rows, model_width), jnp.bfloat16)
    for moment in range(micro_count + 1):
        which = moment - section_index
        usable = (which >= 0) & (which < micro_count)
        slot_index = jnp.clip(which, 0, micro_count - 1)
        own_rows = lax.dynamic_index_in_dim(inputs, slot_index, 0, keepdims=False)
        layer_in = jnp.where(on_first, own_rows, recv_rows)
        length_row = lax.dynamic_index_in_dim(lengths, slot_index, 0, keepdims=False)
        result, value_rows = forward_layer(
            layer_in.astype(jnp.float32),
            recv_values,
            on_first,
            gathered,
            gain_pair,
            places,
            length_row,
        )
        result_low = result.astype(jnp.bfloat16)
        kept_inputs = jnp.where(
            usable,
            lax.dynamic_update_index_in_dim(kept_inputs, layer_in, slot_index, 0),
            kept_inputs,
        )
        kept_values = jnp.where(
            usable,
            lax.dynamic_update_index_in_dim(kept_values, recv_values, slot_index, 0),
            kept_values,
        )
        kept_outputs = jnp.where(
            usable,
            lax.dynamic_update_index_in_dim(kept_outputs, result_low, slot_index, 0),
            kept_outputs,
        )
        if moment < micro_count:
            packed = jnp.concatenate([result_low.reshape(-1), value_rows.reshape(-1)])
            arrived = shifted(packed, "section", 1)
            recv_rows = arrived[:row_values].reshape(local_rows, model_width)
            recv_values = arrived[row_values:].reshape(group_rows, head_width)
    grad_rows_in = jnp.zeros((local_rows, model_width), jnp.float32)
    grad_values_in = jnp.zeros((group_rows, head_width), jnp.float32)
    grad_inputs = jnp.zeros((micro_count, local_rows, model_width), jnp.float32)
    weight_sums = tuple((jnp.zeros(matrix.shape, jnp.float32) for matrix in gathered))
    share_sums = (
        jnp.zeros(w_query[0].shape, jnp.float32),
        jnp.zeros(w_key[0].shape, jnp.float32),
        jnp.zeros(w_value[0].shape, jnp.float32),
        jnp.zeros(w_out[0].shape, jnp.float32),
        jnp.zeros(w_gate[0].shape, jnp.float32),
        jnp.zeros(w_up[0].shape, jnp.float32),
        jnp.zeros(w_down[0].shape, jnp.float32),
    )
    gain_sums = (jnp.zeros((model_width,), jnp.float32), jnp.zeros((model_width,), jnp.float32))
    for moment in range(micro_count + 1):
        which = moment - (1 - section_index)
        usable = (which >= 0) & (which < micro_count)
        slot_index = jnp.clip(which, 0, micro_count - 1)
        matrices = (
            lax.all_gather(w_query[0], "seq", axis=0, tiled=True),
            lax.all_gather(w_key[0], "seq", axis=0, tiled=True),
            lax.all_gather(w_value[0], "seq", axis=0, tiled=True),
            lax.all_gather(w_out[0], "seq", axis=1, tiled=True),
            lax.all_gather(w_gate[0], "seq", axis=0, tiled=True),
            lax.all_gather(w_up[0], "seq", axis=0, tiled=True),
            lax.all_gather(w_down[0], "seq", axis=1, tiled=True),
        )
        layer_in = lax.dynamic_index_in_dim(kept_inputs, slot_index, 0, keepdims=False).astype(
            jnp.float32
        )
        mixin = lax.dynamic_index_in_dim(kept_values, slot_index, 0, keepdims=False)
        length_row = lax.dynamic_index_in_dim(lengths, slot_index, 0, keepdims=False)
        own_grad = lax.dynamic_index_in_dim(cotangent, slot_index, 0, keepdims=False).astype(
            jnp.float32
        )
        grad_top = jnp.where(usable, jnp.where(on_first, grad_rows_in, own_grad), 0.0)
        extra_values = jnp.where(usable & on_first, grad_values_in, 0.0)
        grad_in, send_values, weight_terms, gain_terms = backward_layer(
            layer_in,
            mixin,
            grad_top,
            extra_values,
            on_first,
            matrices,
            gain_pair,
            places,
            length_row,
        )
        gain_sums = (gain_sums[0] + gain_terms[0], gain_sums[1] + gain_terms[1])
        weight_sums = tuple((total + term for total, term in zip(weight_sums, weight_terms)))
        grad_inputs = jnp.where(
            usable,
            lax.dynamic_update_index_in_dim(grad_inputs, grad_in, slot_index, 0),
            grad_inputs,
        )
        if moment < micro_count:
            packed = jnp.concatenate([grad_in.reshape(-1), send_values.reshape(-1)])
            arrived = shifted(packed.astype(jnp.bfloat16), "section", -1).astype(packed.dtype)
            grad_rows_in = arrived[:row_values].reshape(local_rows, model_width)
            grad_values_in = arrived[row_values:].reshape(group_rows, head_width)
    share_sums = (
        lax.psum_scatter(
            weight_sums[0].astype(jnp.bfloat16), "seq", scatter_dimension=0, tiled=True
        ).astype(jnp.float32),
        lax.psum_scatter(
            weight_sums[1].astype(jnp.bfloat16), "seq", scatter_dimension=0, tiled=True
        ).astype(jnp.float32),
        lax.psum_scatter(
            weight_sums[2].astype(jnp.bfloat16), "seq", scatter_dimension=0, tiled=True
        ).astype(jnp.float32),
        lax.psum_scatter(
            weight_sums[3].astype(jnp.bfloat16), "seq", scatter_dimension=1, tiled=True
        ).astype(jnp.float32),
        lax.psum_scatter(
            weight_sums[4].astype(jnp.bfloat16), "seq", scatter_dimension=0, tiled=True
        ).astype(jnp.float32),
        lax.psum_scatter(
            weight_sums[5].astype(jnp.bfloat16), "seq", scatter_dimension=0, tiled=True
        ).astype(jnp.float32),
        lax.psum_scatter(
            weight_sums[6].astype(jnp.bfloat16), "seq", scatter_dimension=1, tiled=True
        ).astype(jnp.float32),
    )
    gain_shares = (
        lax.psum_scatter(gain_sums[0], ("seq", "tensor"), scatter_dimension=0, tiled=True),
        lax.psum_scatter(gain_sums[1], ("seq", "tensor"), scatter_dimension=0, tiled=True),
    )
    return (
        kept_outputs[None],
        grad_inputs[None],
        share_sums[0][None],
        share_sums[1][None],
        share_sums[2][None],
        share_sums[3][None],
        share_sums[4][None],
        share_sums[5][None],
        share_sums[6][None],
        gain_shares[0][None],
        gain_shares[1][None],
    )


MESH_ID = pl.DeviceIdType.MESH
LOW = jnp.bfloat16
F32 = jnp.float32
ORDERS = ((1, 2, 4), (2, 4, 1), (4, 1, 2))
LEVELS = ((0,), (1, 2, 4), (3, 5, 6), (7,))
NT = (((1,), (1,)), ((), ()))
NN = (((1,), (0,)), ((), ()))
TN = (((0,), (0,)), ((), ()))
VMEM_BYTES = 53 * 2**20


def dot(left, right, dims=NN):
    return lax.dot_general(left, right, dims, preferred_element_type=F32)


def flip(value, bit):
    if isinstance(bit, int):
        return 1 - value if bit else value
    return value + bit - 2 * value * bit


def spot():
    y, s, z = lax.axis_index("section"), lax.axis_index("seq"), lax.axis_index("tensor")
    return (y, lax.div(s, 2), lax.rem(s, 2), lax.div(z, 2), lax.rem(z, 2))


def device(at):
    y, x, c, h, p = at
    return (y, 2 * x + c, 2 * h + p)


def moved(at, mask, core=0):
    y, x, c, h, p = at
    if isinstance(mask, int):
        bits = (mask & 1, (mask >> 1) & 1, mask >> 2)
    else:
        bits = (lax.rem(mask, 2), lax.rem(lax.div(mask, 2), 2), lax.div(mask, 4))
    return (flip(y, bits[1]), flip(x, bits[0]), flip(c, core), h, flip(p, bits[2]))


def far_role(at):
    return flip(flip(at[0], at[2]), at[3])


def partner_of(at):
    y, x, c, h, p = at
    return (y, x, c, 1 - h, p)


def lane_of(at):
    return 2 * flip(at[3], far_role(at)) + at[4]


def block_of(at):
    return (2 * at[1] + at[2]) * 4 + lane_of(at)


def level_mask(level, i):
    if level == 0:
        return 0 * i
    if level == 1:
        return 1 + i + lax.div(i, 2)
    if level == 2:
        return 3 + i + lax.div(i + 1, 2)
    return 0 * i + 7


def last_bit(k, mask):
    return [bit for bit in ORDERS[k] if bit & mask][-1]


def parts_of(rows):
    units = rows // 16
    small = units // 3
    sizes = (16 * (units - 2 * small), 16 * small, 16 * small)
    return ((0, sizes[0]), (sizes[0], sizes[1]), (sizes[0] + sizes[1], sizes[2]))


def remote(src, dst, send, recv, at):
    return pltpu.make_async_remote_copy(
        src_ref=src, dst_ref=dst, send_sem=send, recv_sem=recv, device_id=device(at), device_id_type=MESH_ID
    )


def others(at):
    return [moved(at, mask, core) for mask in range(8) for core in range(2) if mask + core]


def greet(at, *pushes, peers=()):
    met = others(at) + list(peers)
    count = len(met)
    for peer in met:
        signal(peer)
    for push in pushes:
        count = count + push.greet()
    pl.semaphore_wait(pltpu.get_barrier_semaphore(), count)


def run(steps):
    for _ in steps:
        pass


def gather(*args, **kwargs):
    run(gathering(*args, **kwargs))


def gathering(at, buf, sems, on_block=None, keep=None, ready=None):
    send, recv, csend, crecv = sems
    parts = parts_of(buf.shape[1])

    def rows(mask, k, core=0):
        return buf.at[block_of(moved(at, mask, core)), pl.ds(*parts[k])]

    def hop(k, target):
        bit = last_bit(k, target)
        ref = rows(target ^ bit, k)
        return remote(ref, ref, send.at[k, target], recv.at[k, target], moved(at, bit))

    def arrival(k, target):
        ref = rows(target, k)
        return remote(ref, ref, send.at[k, target], recv.at[k, target], moved(at, last_bit(k, target)))

    def across(mask, core=0):
        ref = buf.at[block_of(moved(at, mask, core))]
        return remote(ref, ref, csend.at[mask], crecv.at[mask], moved(at, 0, 1))

    def visit(level, core):
        if on_block is None and keep is None:
            return

        def one(i, none):
            b = block_of(moved(at, level_mask(level, i), core))
            if keep is not None:
                pltpu.make_async_copy(buf.at[b], keep[0].at[b], keep[1].at[b]).start()
            if on_block is not None:
                on_block(b)
            return none

        lax.fori_loop(0, len(LEVELS[level]), one, 0)

    for i in range(2):
        for k in range(3):
            hop(k, ORDERS[k][i]).start()
        if i == 0:
            across(0).start()
    if ready is not None:
        ready()
    visit(0, 0)
    across(0, 1).wait_recv()
    visit(0, 1)
    yield
    for k in range(3):
        first, second, third = ORDERS[k]
        arrival(k, first).wait_recv()
        hop(k, first | second).start()
    for k in range(3):
        first, second, third = ORDERS[k]
        hop(k, third).start()
        hop(k, first | third).start()
    yield
    for k in range(3):
        first, second, third = ORDERS[k]
        arrival(k, second).wait_recv()
        hop(k, second | third).start()
    yield
    for k in range(3):
        first, second, third = ORDERS[k]
        arrival(k, first | second).wait_recv()
        hop(k, 7).start()
    yield
    for level in (1, 2, 3):
        for mask in LEVELS[level]:
            for k in range(3):
                first, second, third = ORDERS[k]
                if mask not in (first, second, first | second):
                    arrival(k, mask).wait_recv()
            across(mask).start()
        visit(level, 0)
        for mask in LEVELS[level]:
            across(mask, 1).wait_recv()
        visit(level, 1)
        yield
    for k in range(3):
        for target in range(1, 8):
            hop(k, target).wait_send()
    for mask in range(8):
        across(mask).wait_send()


def kept(buf, keep):
    for b in range(16):
        pltpu.make_async_copy(buf.at[b], keep[0].at[b], keep[1].at[b]).wait()


def scatter(*args, **kwargs):
    run(scattering(*args, **kwargs))


def scattering(at, total, boxes, sems, partial, before_last=None):
    out_c, in_c, rin = boxes
    send, recv, csend, crecv = sems
    parts = parts_of(total.shape[0])

    def hop(k, target):
        rows = pl.ds(*parts[k])
        return remote(
            in_c.at[target, rows],
            rin.at[target - 1, rows],
            send.at[k, target],
            recv.at[k, target],
            moved(at, last_bit(k, target)),
        )

    def across(mask):
        slot = 0 if mask in (0, 7) else 1 + (LEVELS[1] + LEVELS[2]).index(mask) % 3
        return remote(out_c.at[slot], in_c.at[mask], csend.at[mask], crecv.at[mask], moved(at, 0, 1))

    def emit(level):
        if level < 2:
            for mask in LEVELS[3 - level]:
                across(mask).wait_send()

        def one(i, none):
            slot = 1 + i if level in (1, 2) else 0
            out_c[slot] = partial(block_of(moved(at, level_mask(level, i), 1))).astype(LOW)
            return none

        lax.fori_loop(0, len(LEVELS[level]), one, 0)
        for mask in LEVELS[level]:
            across(mask).start()

    def settle(level):
        for mask in LEVELS[level]:
            across(mask).wait_recv()

        def one(i, none):
            mask = level_mask(level, i)
            mine = partial(block_of(moved(at, mask))) + in_c[mask].astype(F32)
            if level == 0:
                total[...] = mine
            else:
                in_c[mask] = mine.astype(LOW)
            return none

        lax.fori_loop(0, len(LEVELS[level]), one, 0)
        for mask in LEVELS[level]:
            for k in range(3):
                if mask & ORDERS[k][2]:
                    hop(k, mask).start()

    def arrived(k, target):
        hop(k, target).wait_recv()
        return rin[target - 1, pl.ds(*parts[k])].astype(F32)

    emit(3)
    emit(2)
    yield
    settle(3)
    settle(2)
    emit(1)
    yield
    settle(1)
    if before_last is not None:
        before_last()
    emit(0)
    settle(0)
    yield
    for mask_of in (lambda a, b: a | b, lambda a, b: b):
        for k in range(3):
            first, second, third = ORDERS[k]
            mask, rows = mask_of(first, second), pl.ds(*parts[k])
            in_c[mask, rows] = (in_c[mask, rows].astype(F32) + arrived(k, mask | third)).astype(LOW)
            hop(k, mask).start()
        yield
    for k in range(3):
        first, second, third = ORDERS[k]
        rows = pl.ds(*parts[k])
        in_c[first, rows] = (
            in_c[first, rows].astype(F32) + arrived(k, first | third) + arrived(k, first | second)
        ).astype(LOW)
        hop(k, first).start()
    yield
    for k in range(3):
        first, second, third = ORDERS[k]
        rows = pl.ds(*parts[k])
        total[rows] = total[rows] + arrived(k, third) + arrived(k, second) + arrived(k, first)
    for k in range(3):
        for target in range(1, 8):
            hop(k, target).wait_send()
    for mask in LEVELS[0] + LEVELS[1]:
        across(mask).wait_send()


class ToRows:
    def __init__(self, at, block, place, sems):
        self.at, self.block, self.place = at, block, place
        self.send, self.recv, self.local = sems
        self.mine = block_of(at)

    def copy(self, b):
        lane, (y, x, c, h, p) = b % 4, self.at
        x, c = b // 8, (b // 4) % 2
        home = ((c + lane // 2) % 2, x, c, h, lane % 2)
        return remote(self.block(b), self.place(self.mine), self.send.at[b], self.recv.at[self.mine], home)

    def start(self, b):
        @pl.when(same(b, self.mine) == 0)
        def _():
            self.copy(b).start()

        @pl.when(same(b, self.mine) == 1)
        def _():
            pltpu.make_async_copy(self.block(b), self.place(b), self.local).start()

    def finish(self):
        for b in range(16):

            @pl.when(same(b, self.mine) == 0)
            def _(b=b):
                dst = self.place(b)
                remote(dst, dst, self.send.at[b], self.recv.at[b], self.at).wait_recv()
                self.copy(b).wait_send()

            @pl.when(same(b, self.mine) == 1)
            def _(b=b):
                pltpu.make_async_copy(self.block(b), self.place(b), self.local).wait()


def row_sems():
    dma = pltpu.SemaphoreType.DMA
    return (dma((16,)), dma((16,)), dma)


def same(a, b):
    return 1 - jnp.minimum(jnp.abs(a - b), 1)


def signal(at):
    pl.semaphore_signal(pltpu.get_barrier_semaphore(), inc=1, device_id=device(at), device_id_type=MESH_ID)


class ToHeads:
    def __init__(self, at, layer, piece, place, sems):
        self.at, self.layer, self.piece, self.place = at, layer, piece, place
        self.send, self.recv, self.local, self.forth = sems
        y, x, c, h, p = at
        self.s = 2 * x + c
        self.sends = same(y, layer)
        self.near = 1 - far_role(at)

    def is_me(self, j):
        return self.sends * self.near * same(self.s, j)

    def greet(self):
        h, p = self.at[3], self.at[4]
        for k in range(4):

            @pl.when(self.near - self.is_me(k) == 1)
            def _(k=k):
                signal((self.layer, k // 2, k % 2, h, p))

        return self.sends * (4 - self.near)

    def copy(self, j):
        h, p = self.at[3], self.at[4]
        home = (flip(h, j % 2), j // 2, j % 2, h, p)
        return remote(self.piece(j), self.place(self.s), self.send.at[j], self.recv.at[self.s], home)

    def on(self, k):
        return remote(self.place(k), self.place(k), self.forth.at[k], self.recv.at[k], partner_of(self.at))

    def start(self):
        for j in range(4):

            @pl.when(self.sends - self.is_me(j) == 1)
            def _(j=j):
                self.copy(j).start()

            @pl.when(self.is_me(j) == 1)
            def _(j=j):
                pltpu.make_async_copy(self.piece(j), self.place(j), self.local).start()

    def forward(self):
        for k in range(4):

            @pl.when(self.near - self.is_me(k) == 1)
            def _(k=k):
                self.on(k).wait_recv()

            @pl.when(self.is_me(k) == 1)
            def _(k=k):
                pltpu.make_async_copy(self.piece(k), self.place(k), self.local).wait()

            @pl.when(self.near == 1)
            def _(k=k):
                self.on(k).start()

    def finish(self):
        for k in range(4):

            @pl.when(self.near == 0)
            def _(k=k):
                self.on(k).wait_recv()

            @pl.when(self.near == 1)
            def _(k=k):
                self.on(k).wait_send()

            @pl.when(self.sends - self.is_me(k) == 1)
            def _(k=k):
                self.copy(k).wait_send()


class ToShards:
    def __init__(self, at, layer, piece, place, sems, roles=(0, 1)):
        self.at, self.layer, self.piece, self.place, self.roles = at, layer, piece, place, roles
        self.send, self.recv, self.local = sems
        y, x, c, h, p = at
        self.s = 2 * x + c
        self.gets = same(y, layer)
        self.role = far_role(at)
        self.active = {(0, 1): 1, (0,): 1 - self.role, (1,): self.role}[roles]

    def is_me(self, k):
        return self.gets * (1 - self.role) * same(self.s, k) if 0 in self.roles else 0 * self.gets

    def greet(self):
        h, p = self.at[3], self.at[4]
        for j in range(4):
            if 1 in self.roles:

                @pl.when(self.gets == 1)
                def _(j=j):
                    signal((flip(h, j % 2), j // 2, j % 2, 1 - h, p))

            if 0 in self.roles:

                @pl.when(self.gets - self.is_me(j) == 1)
                def _(j=j):
                    signal((flip(h, j % 2), j // 2, j % 2, h, p))

        return self.active * (4 - self.gets * (1 - self.role))

    def copy(self, k):
        home = (self.layer, k // 2, k % 2, flip(self.at[3], self.role), self.at[4])
        return remote(
            self.piece(k), self.place(self.role, self.s), self.send.at[k], self.recv.at[self.role, self.s], home
        )

    def start(self):
        for k in range(4):

            @pl.when(self.active - self.is_me(k) == 1)
            def _(k=k):
                self.copy(k).start()

            @pl.when(self.is_me(k) == 1)
            def _(k=k):
                pltpu.make_async_copy(self.piece(k), self.place(0, k), self.local).start()

    def finish(self):
        for role in self.roles:
            for j in range(4):
                dst = self.place(role, j)
                comes = self.gets if role else self.gets - self.is_me(j)

                @pl.when(comes == 1)
                def _(role=role, j=j, dst=dst):
                    remote(dst, dst, self.send.at[0], self.recv.at[role, j], self.at).wait_recv()

        for k in range(4):

            @pl.when(self.active - self.is_me(k) == 1)
            def _(k=k):
                self.copy(k).wait_send()

            @pl.when(self.is_me(k) == 1)
            def _(k=k):
                pltpu.make_async_copy(self.piece(k), self.place(0, k), self.local).wait()


class ToHome:
    def __init__(self, at, layer, block, place, sems):
        self.at, self.layer, self.block, self.place = at, layer, block, place
        self.send, self.recv, self.local = sems
        y, x, c, h, p = at
        self.gets = same(y, layer)
        self.role = far_role(at)
        self.is_me = self.gets * (1 - self.role)

    def holder(self, micro):
        y, x, c, h, p = self.at
        return (flip(h, c), x, c, micro, p), (1 - flip(h, micro)) * self.is_me

    def greet(self):
        for micro in range(2):
            holder, is_me = self.holder(micro)

            @pl.when(self.gets - is_me == 1)
            def _(holder=holder):
                signal(holder)

        return 1 - self.is_me

    def copy(self):
        y, x, c, h, p = self.at
        home = (self.layer, x, c, flip(h, self.role), p)
        return remote(self.block, self.place(h), self.send, self.recv.at[h], home)

    def keep(self):
        return pltpu.make_async_copy(self.block, self.place(self.at[3]), self.local)

    def start(self):
        @pl.when(self.is_me == 0)
        def _():
            self.copy().start()

        @pl.when(self.is_me == 1)
        def _():
            self.keep().start()

    def finish(self):
        for micro in range(2):
            dst = self.place(micro)

            @pl.when(self.gets - self.holder(micro)[1] == 1)
            def _(micro=micro, dst=dst):
                remote(dst, dst, self.send, self.recv.at[micro], self.at).wait_recv()

        @pl.when(self.is_me == 0)
        def _():
            self.copy().wait_send()

        @pl.when(self.is_me == 1)
        def _():
            self.keep().wait()


def home_sems():
    dma = pltpu.SemaphoreType.DMA
    return (dma, dma((2,)), dma)


def head_sems():
    dma = pltpu.SemaphoreType.DMA
    return (dma((4,)), dma((4,)), dma, dma((4,)))


def shard_sems():
    dma = pltpu.SemaphoreType.DMA
    return (dma((4,)), dma((2, 4)), dma)


def slices(ref, size):
    return lambda j: ref.at[:, pl.ds(j * size, size)]


def columns(ref):
    wide = ref.shape[-1] // 4

    def place(s):
        start = s * wide
        return ref.at[:, :, pl.ds(start if isinstance(s, int) else pl.multiple_of(start, wide), wide)]

    return place


def unit_of(values):
    inverse = lax.rsqrt(jnp.mean(values * values, axis=-1, keepdims=True) + EPSILON)
    return (values * inverse, inverse)


def back_of(grad_normed, values, gain_row):
    unit, inverse = unit_of(values)
    shaped = grad_normed * gain_row
    inner = jnp.mean(shaped * unit, axis=-1, keepdims=True)
    return (inverse * (shaped - unit * inner), jnp.sum(grad_normed * unit, axis=0, keepdims=True))


def span(b, rows):
    return pl.ds(pl.multiple_of(b * rows, rows), rows)


def turned(top, bottom, cosine, sine):
    return (top * cosine - bottom * sine, bottom * cosine + top * sine)


def project_block(b, buf, w_ref, cos_ref, sin_ref, mix_ref, qkv_ref):
    rows, half = buf.shape[1], HS // 2
    cols = span(b, rows)
    raw = dot(w_ref[:3].reshape(3 * HS, buf.shape[2]), buf[b], NT)
    cosine, sine = cos_ref[:, cols], sin_ref[:, cols]
    for first, scale in ((0, HS**-0.5), (HS, 1.0)):
        a, bb = turned(raw[first : first + half], raw[first + half : first + HS], cosine, sine)
        qkv_ref[first : first + half, cols] = (a.astype(LOW) * scale).astype(LOW)
        qkv_ref[first + half : first + HS, cols] = (bb.astype(LOW) * scale).astype(LOW)
    value = raw[2 * HS :]
    if mix_ref is not None:
        value = 0.5 * value + 0.5 * mix_ref[:, cols].astype(F32)
    qkv_ref[2 * HS :, cols] = value.astype(LOW)


def up_block(b, buf, f_ref, hidden_ref, one_ref, two_ref):
    rows = span(b, buf.shape[1])
    x = buf[b]
    gate, up = dot(x, f_ref[0], NT), dot(x, f_ref[1], NT)
    sigmoid = 1.0 / (1.0 + jnp.exp(-gate))
    activated = gate * sigmoid
    hidden_ref[rows] = (activated * up).astype(LOW)
    one_ref[rows] = (up * sigmoid * (1.0 + gate * (1.0 - sigmoid))).astype(LOW)
    two_ref[rows] = activated.astype(LOW)


def held(buf):
    def blocks(use):
        def one(b, none):
            use(b, buf[b])
            return none

        lax.fori_loop(0, buf.shape[0], one, 0)

    return blocks


def streamed(far, ring, sems):
    half = ring.shape[0]

    def copy(b, slot):
        return pltpu.make_async_copy(far.at[b], ring.at[slot], sems.at[slot])

    for slot in range(half):
        copy(slot, slot).start()

    def blocks(use):
        def first(b, none):
            copy(b, b).wait()
            use(b, ring[b])
            copy(b + half, b).start()
            return none

        def second(b, none):
            copy(b + half, b).wait()
            use(b + half, ring[b])
            return none

        lax.fori_loop(0, half, first, 0)
        lax.fori_loop(0, half, second, 0)

    return blocks


class Stage:
    def __init__(self, sems):
        self.sems, self.count = sems, 0

    def copy(self, src, dst):
        copy = pltpu.make_async_copy(src, dst, self.sems.at[self.count])
        self.count += 1
        copy.start()
        return copy


def taking_turns(*steps):
    steps = list(steps)
    while steps:
        for one in list(steps):
            if next(one, True):
                steps.remove(one)
        yield


def feed_scratch(length, f_ref):
    return [pltpu.VMEM((length, f_ref.shape[1]), LOW)] * 3 + [pltpu.VMEM(f_ref.shape, F32)]


def out_project(at, push, att_in, wo_all, x_ref):
    push.finish()
    heads = att_in.shape[0] * HS
    summed = dot(att_in[...].reshape(heads, -1), wo_all[...].reshape(heads, -1), TN)
    return x_ref[...].astype(F32) + summed


def attend_and_share(at, steps, push, before, *refs):
    def after(qi):
        if qi == 0 and before is not None:
            before()
        each = TILE * 16 // refs[0].shape[1]
        for b in range(qi * each, (qi + 1) * each):
            push.start(b)
        next(steps, None)

    attend_body(*refs, after)
    run(steps)


def hidden_back(b, buf, f_ref, hidden_ref, one_ref, two_ref, sums_ref):
    here = span(b, buf.shape[1])
    grad = dot(buf[b], f_ref[2], NT)
    one_ref[here] = (grad * one_ref[here].astype(F32)).astype(LOW)
    two_ref[here] = (grad * two_ref[here].astype(F32)).astype(LOW)
    sums_ref[2] += dot(hidden_ref[here], buf[b], TN)


def down_back(
    at, top, ready, buf, blocks, total, boxes, ag_sems, rs_sems, f_ref, hidden_ref, one_ref, two_ref,
    gain_ref, middle_ref, sums_ref, wo_all, dout_block, push, dmid_ref, gain_grad_ref,
):
    rows = buf.shape[1]
    if not ready:
        sums_ref[...] = jnp.zeros_like(sums_ref)
        buf[block_of(at)] = top().astype(LOW)
        gather(at, buf, ag_sems, lambda b: hidden_back(b, buf, f_ref, hidden_ref, one_ref, two_ref, sums_ref))

    def partial(b):
        here = span(b, rows)
        return dot(one_ref[here], f_ref[0]) + dot(two_ref[here], f_ref[1])

    scatter(at, total, boxes, rs_sems, partial)
    grad, gain_grad = back_of(total[...], middle_ref[...], gain_ref[...])
    gain_grad_ref[...] = gain_grad
    grad = grad + top()
    dmid_ref[...] = grad
    heads = wo_all.shape[0] * HS
    found = dot(wo_all[...].reshape(heads, -1), grad.astype(LOW), NT).astype(LOW)
    dout_block[...] = found.reshape(dout_block.shape)
    for b in range(16):
        push.start(b)

    def gate_up(b, normed):
        here = span(b, rows)
        sums_ref[0] += dot(one_ref[here], normed, TN)
        sums_ref[1] += dot(two_ref[here], normed, TN)

    blocks(gate_up)
    push.finish()


def first_kernel(
    cos_ref, sin_ref, seg_ref, in_ref, a_ref, f_ref, gain_ref,
    qkv0_ref, att_ref, lse_ref, att_in, wo_all, x_here, middle_ref, out_ref, qkv1_ref,
    normed0_far, nmid_far, normed1_far, hidden_far, one_far, two_far, a0, a1, f0, f1, gains,
    buf, low_ref, a_here, f_here, gain_here, hidden_ref, one_ref, two_ref,
    key_x, query_x, val_x, scores, total, out_c, in_c, rin,
    ag_sems, wo_sems, rs_sems, share_sems, block_sems, a0_sems, a1_sems, f0_sems, f1_sems, swap, gain_sems, loads,
):
    at = spot()
    y, x, c, h, p = at
    rows = x_here.shape[0]
    far = far_role(at)
    stage = Stage(loads)
    partner, above = partner_of(at), (1 - y, x, c, h, p)
    size = f_ref.shape[1] // 4
    a_pushes = [
        ToHeads(at, layer, slices(a_ref, HS), columns(into), sems)
        for layer, into, sems in ((0, a0, a0_sems), (1, a1, a1_sems))
    ]
    f_pushes = [
        ToHeads(at, layer, slices(f_ref, size), columns(into), sems)
        for layer, into, sems in ((0, f0, f0_sems), (1, f1, f1_sems))
    ]
    share = ToRows(at, lambda b: low_ref.at[:, pl.ds(b * rows, rows)], lambda b: att_in.at[b], share_sems)
    greet(at, *a_pushes, *f_pushes, peers=(partner,))
    swapped = remote(in_ref.at[1 - h], x_here, swap.at[0], swap.at[1], partner)
    stays = pltpu.make_async_copy(in_ref.at[h], x_here, swap.at[2])

    @pl.when(far == 0)
    def _():
        swapped.start()
        stays.start()

    across = remote(gain_ref, gains.at[y], gain_sems.at[0], gain_sems.at[1], above)
    across.start()
    keeps = pltpu.make_async_copy(gain_ref, gains.at[y], gain_sems.at[2])
    keeps.start()
    for push in (a_pushes[0], f_pushes[0], a_pushes[1], f_pushes[1]):
        push.start()
    a_pushes[0].forward()
    keeps.wait()
    across.wait_send()
    remote(gain_ref, gains.at[1 - y], gain_sems.at[0], gain_sems.at[1], above).wait_recv()
    gain_copy = stage.copy(gains, gain_here)

    @pl.when(far == 1)
    def _():
        swapped.wait_recv()

    @pl.when(far == 0)
    def _():
        stays.wait()
        swapped.wait_send()

    gain_copy.wait()
    buf[block_of(at)] = (unit_of(x_here[...].astype(F32))[0] * gain_here[0, 0:1]).astype(LOW)

    def ready():
        a_pushes[0].finish()
        copy = stage.copy(a0, a_here)
        copy.wait()

    keep = (normed0_far, block_sems)
    gather(at, buf, ag_sems, lambda b: project_block(b, buf, a_here, cos_ref, sin_ref, None, qkv0_ref), keep, ready)
    wo_all[block_of(at)] = a_here[3]
    f_pushes[0].forward()
    attend_and_share(
        at, gathering(at, wo_all, wo_sems), share, lambda: kept(buf, keep),
        qkv0_ref, seg_ref, att_ref, low_ref, lse_ref, key_x, query_x, val_x, scores,
    )
    middle = out_project(at, share, att_in, wo_all, x_here)
    middle_ref[...] = middle
    buf[block_of(at)] = (unit_of(middle)[0] * gain_here[0, 1:2]).astype(LOW)
    keep = (nmid_far, block_sems)

    def more():
        f_pushes[0].finish()
        copy = stage.copy(f0, f_here)
        a_pushes[1].forward()
        f_pushes[1].forward()
        copy.wait()

    gather(at, buf, ag_sems, lambda b: up_block(b, buf, f_here, hidden_ref, one_ref, two_ref), keep, more)
    saves = [stage.copy(*pair) for pair in ((hidden_ref, hidden_far), (one_ref, one_far), (two_ref, two_far))]
    boxes = (out_c, in_c, rin)
    scatter(
        at, total, boxes, rs_sems, lambda b: dot(hidden_ref[span(b, rows)], f_here[2]), lambda: kept(buf, keep)
    )
    out = (middle_ref[...] + total[...]).astype(LOW)
    out_ref[...] = out
    buf[block_of(at)] = (unit_of(out.astype(F32))[0] * gain_here[1, 0:1]).astype(LOW)
    keep = (normed1_far, block_sems)

    def last():
        a_pushes[1].finish()
        stage.copy(a1, a_here).wait()

    mix_ref = qkv0_ref.at[pl.ds(2 * HS, HS)]
    gather(
        at, buf, ag_sems, lambda b: project_block(b, buf, a_here, cos_ref, sin_ref, mix_ref, qkv1_ref), keep, last
    )
    kept(buf, keep)
    for save in saves:
        save.wait()
    f_pushes[1].finish()


def turn_kernel(
    qkv_ref, seg_ref, a_ref, f_ref, gain_ref, x_ref, top_ref,
    att_ref, lse_ref, att_in, dmid_ref, gain_grad_ref, dout_ref, f_grad_ref, middle_ref, hidden_far,
    buf, nmid, wo_all, low_ref, dout_block, total, out_c, in_c, rin,
    ag_sems, wo_sems, rs_sems, share_sems, back_sems, loads,
):
    at = spot()
    rows = x_ref.shape[0]
    share = ToRows(at, lambda b: low_ref.at[:, pl.ds(b * rows, rows)], lambda b: att_in.at[b], share_sems)

    def column(b):
        start = b * rows
        return dout_ref.at[:, pl.ds(start if isinstance(b, int) else pl.multiple_of(start, rows), rows)]

    back = ToRows(at, lambda b: dout_block.at[b], column, back_sems)
    greet(at)
    wo_all[block_of(at)] = a_ref[3]
    buf[block_of(at)] = top_ref[...]
    steps = taking_turns(gathering(at, wo_all, wo_sems), gathering(at, buf, ag_sems))
    pl.run_scoped(
        functools.partial(attend_and_share, at, steps, share, None, qkv_ref, seg_ref, att_ref, low_ref, lse_ref),
        *attend_scratch(qkv_ref.shape[1]),
    )
    middle = out_project(at, share, att_in, wo_all, x_ref)
    middle_ref[...] = middle
    nmid[block_of(at)] = (unit_of(middle)[0] * gain_ref[...]).astype(LOW)

    def rest(hidden_ref, one_ref, two_ref, sums_ref):
        sums_ref[...] = jnp.zeros_like(sums_ref)

        def both_ways(b):
            up_block(b, nmid, f_ref, hidden_ref, one_ref, two_ref)
            hidden_back(b, buf, f_ref, hidden_ref, one_ref, two_ref, sums_ref)

        gather(at, nmid, ag_sems, both_ways)
        save = Stage(loads).copy(hidden_ref, hidden_far)
        boxes = (out_c, in_c, rin)
        down_back(
            at, lambda: top_ref[...].astype(F32), True, buf, held(nmid), total, boxes, ag_sems, rs_sems, f_ref, hidden_ref, one_ref,
            two_ref, gain_ref, middle_ref, sums_ref, wo_all, dout_block, back, dmid_ref, gain_grad_ref,
        )
        f_grad_ref[...] = sums_ref[...].astype(LOW)
        save.wait()

    pl.run_scoped(rest, *feed_scratch(qkv_ref.shape[1], f_ref))


def input_back(
    at, dqkv_ref, a_ref, x_ref, gain_ref, dmid_ref, gain_grad_ref, total, boxes, rs_sems, normed, load, sum_ref, after
):
    rows, width = total.shape

    def weight_sum():
        load.wait()
        sum_ref[...] = jnp.zeros_like(sum_ref)

        def one(b, none):
            sum_ref[...] += dot(dqkv_ref[:, span(b, rows)], normed[b])
            return none

        lax.fori_loop(0, 16, one, 0)
        if after is not None:
            after()

    def partial(b):
        return dot(dqkv_ref[:, span(b, rows)], a_ref[:3].reshape(3 * HS, width), TN)

    scatter(at, total, boxes, rs_sems, partial, weight_sum)
    grad, gain_grad = back_of(total[...], x_ref[...].astype(F32), gain_ref[...])
    gain_grad_ref[...] = gain_grad
    return grad + dmid_ref[...]


def staged_scratch(refs):
    return [pltpu.VMEM(ref.shape, ref.dtype) for ref in refs]


def attend_back_staged(stage, far, outs, steps, early, *refs):
    near, scratch = refs[: len(far)], refs[len(far) :]
    copies = [stage.copy(*pair) for pair in zip(far, near)]
    for _ in range(early):
        next(steps, None)
    for copy in copies:
        copy.wait()
    attend_back_body(*near, *outs, *scratch, lambda ki: next(steps, None))
    run(steps)


def meet(at, sem):
    for mask, core in ((1, 0), (2, 0), (4, 0), (0, 1)):
        peer = device(moved(at, mask, core))
        pl.semaphore_signal(sem, inc=1, device_id=peer, device_id_type=MESH_ID)
    pl.semaphore_wait(sem, 4)


def put_grads(a_grad_ref, in_sum_ref, out_total):
    for i in range(3):
        a_grad_ref[i] = in_sum_ref[i * HS : (i + 1) * HS].astype(LOW)
    a_grad_ref[3] = out_total.astype(LOW)


def by_columns(ref):
    wide = ref.shape[-1] // 4
    return lambda k: ref.at[:, :, pl.ds(k * wide, wide)]


def lower_kernel(
    a_ref, gain_in_ref, dmid_above, gain_mid_ref,
    x_far, f_far, middle_far, qkv_far, seg_far, att_far, lse_far, dout_far, cos_far, sin_far,
    hidden_far, one_far, two_far, normed_far, nmid_far, wo_far, hidden_above, middle_above, f_above, f_grad_above,
    out_below,
    send_ref, gain_in_grad_ref, dmid_ref, gain_mid_grad_ref, dout_ref, f_grad_ref, in_grad_ref, low_ref, out_ref, out_home, f_heard,
    buf, wo_all, dqkv_ref, in_sum_ref, dout_block,
    total, out_c, in_c, rin,
    ag_sems, rs_sems, back_sems, heard_sems, out_homing, loads, ring_sems, meeting,
):
    at = spot()
    rows = low_ref.shape[0]
    stage = Stage(loads)
    normed_copy = stage.copy(normed_far, buf)
    wo_copy = stage.copy(wo_far, wo_all)
    length = dqkv_ref.shape[1]
    home = ToHome(at, 0, out_below, lambda m: out_home.at[m], out_homing)
    far = far_role(at)
    push = remote(f_grad_above, f_heard, heard_sems.at[0], heard_sems.at[1], partner_of(at))

    def column(b):
        start = b * rows
        return dout_ref.at[:, pl.ds(start if isinstance(b, int) else pl.multiple_of(start, rows), rows)]

    back = ToRows(at, lambda b: dout_block.at[b], column, back_sems)
    greet(at, home, peers=(partner_of(at),))

    @pl.when(far == 1)
    def _():
        push.start()

    home.start()
    boxes = (out_c, in_c, rin)

    def out_steps(hidden_ref, down_ref):
        yield from scattering(
            at, total, boxes, rs_sems, lambda b: dot(hidden_ref[span(b, rows)], down_ref[...])
        )
        out_ref[...] = (dmid_ref[...] + total[...]).astype(LOW)

    def attention(hidden_ref, down_ref, *refs):
        copies = [
            stage.copy(*pair)
            for pair in ((hidden_above, hidden_ref), (f_above.at[2], down_ref), (middle_above, dmid_ref))
        ]
        for copy in copies:
            copy.wait()
        steps = out_steps(hidden_ref, down_ref)
        attend_back_staged(
            stage, (qkv_far, seg_far, att_far, lse_far, dout_far, cos_far, sin_far), (None, dqkv_ref, send_ref),
            steps, 3, *refs,
        )

    pl.run_scoped(
        attention,
        pltpu.VMEM(hidden_above.shape, LOW),
        pltpu.VMEM(f_above.shape[1:], LOW),
        *staged_scratch((qkv_far, seg_far, att_far, lse_far, dout_far, cos_far, sin_far)),
        *attend_back_scratch(length),
    )

    meet(at, meeting)

    def rest(hidden_ref, one_ref, two_ref, sums_ref, x_ref, f_ref, middle_ref, ring):
        blocks = streamed(nmid_far, ring, ring_sems)
        pairs = (
            (x_far, x_ref),
            (f_far, f_ref),
            (middle_far, middle_ref),
            (hidden_far, hidden_ref),
            (one_far, one_ref),
            (two_far, two_ref),
        )
        copies = [stage.copy(*pair) for pair in pairs]
        copies.pop(0).wait()
        grad = input_back(
            at, dqkv_ref, a_ref, x_ref, gain_in_ref, dmid_above, gain_in_grad_ref, total, boxes, rs_sems, buf,
            normed_copy, in_sum_ref, None,
        )
        dmid_ref[...] = grad
        low_ref[...] = grad.astype(LOW)
        in_grad_ref[...] = in_sum_ref[...].astype(LOW)
        for copy in copies + [wo_copy]:
            copy.wait()
        down_back(
            at, lambda: dmid_ref[...], False, buf, blocks, total, boxes, ag_sems, rs_sems, f_ref, hidden_ref, one_ref, two_ref,
            gain_mid_ref, middle_ref, sums_ref, wo_all, dout_block, back, dmid_ref, gain_mid_grad_ref,
        )
        f_grad_ref[...] = sums_ref[...].astype(LOW)

    ring_type = pltpu.VMEM((8, *nmid_far.shape[1:]), LOW)
    pl.run_scoped(rest, *feed_scratch(length, f_far), *staged_scratch((x_far, f_far, middle_far)), ring_type)
    home.finish()

    @pl.when(far == 1)
    def _():
        push.wait_send()

    @pl.when(far == 0)
    def _():
        push.wait_recv()


def last_kernel(
    qkv_ref, seg_ref, att_ref, lse_ref, dout_in, cos_ref, sin_ref, extra_ref, x_ref, a_ref, gain_ref, dmid_ref,
    att_in, att_in_above, dmid_above, in_grad_above, gains_ref, f_grad, f_above, f_heard, out_above, grad_above, normed_far,
    home_ref, out_home, grad_home, f_in, f_in_above, a_in, a_in_above, gain_sum,
    buf, dqkv_ref, low_ref, two_low, in_sum_ref, a_grad_ref, a_above, gain_grad_ref, heard, f_sum, f_sum_above, f_got,
    key_x, val_x, query_x, dout_x, dq, scores, along,
    total, out_c, in_c, rin, out_total, out_c2, in_c2, rin2,
    rs_sems, rs2_sems, f_sems, f1_sems, a_sems, a1_sems, homing, out_homing, grad_homing, gain_sems, got_sems, loads,
):
    at = spot()
    y, x, c, h, p = at
    stage = Stage(loads)
    far = far_role(at)
    copy = stage.copy(normed_far, buf)
    home = ToHome(at, 0, low_ref, lambda m: home_ref.at[m], homing)
    homes = [
        ToHome(at, 1, ref, lambda m, into=into: into.at[m], sems)
        for ref, into, sems in ((out_above, out_home, out_homing), (grad_above, grad_home, grad_homing))
    ]
    f_push, f_push_above = (
        ToShards(at, layer, by_columns(ref), lambda role, j, into=into: into.at[j], sems, (0,))
        for layer, ref, into, sems in ((0, f_sum, f_in, f_sems), (1, f_sum_above, f_in_above, f1_sems))
    )
    a_push, a_push_above = (
        ToShards(at, layer, by_columns(ref), lambda role, j, into=into: into.at[role, j], sems)
        for layer, ref, into, sems in ((0, a_grad_ref, a_in, a_sems), (1, a_above, a_in_above, a1_sems))
    )
    peers = [moved(at, 0, 1), moved(at, 1), moved(at, 2), moved(at, 4), partner_of(at)]
    greet(at, home, *homes, f_push, f_push_above, a_push, a_push_above, peers=peers[4:])
    give = remote(f_grad, f_got, got_sems.at[0], got_sems.at[1], partner_of(at))

    @pl.when(far == 1)
    def _():
        give.start()

    @pl.when(far == 0)
    def _():
        pairs = ((f_above, f_sum_above), (f_heard, f_sum))
        copies = [pltpu.make_async_copy(*pair, got_sems.at[2 + i]) for i, pair in enumerate(pairs)]
        for one in copies:
            one.start()
        for one in copies:
            one.wait()
        f_sum_above[...] = (f_sum_above[...].astype(F32) + f_sum[...].astype(F32)).astype(LOW)
        pltpu.make_async_copy(f_grad, f_sum, got_sems.at[2]).start()

    f_push_above.start()
    for one in homes:
        one.start()
    two_low[0] = dmid_ref[...].astype(LOW)
    two_low[1] = dmid_above[...].astype(LOW)

    def two_layers(b):
        return jnp.concatenate([dot(att_in[b], two_low[0]), dot(att_in_above[b], two_low[1])])

    steps = scattering(at, out_total, (out_c2, in_c2, rin2), rs2_sems, two_layers)
    attend_back_body(
        qkv_ref, seg_ref, att_ref, lse_ref, dout_in, cos_ref, sin_ref, extra_ref, dqkv_ref, None,
        key_x, val_x, query_x, dout_x, dq, scores, along, lambda ki: next(steps, None),
    )
    run(steps)

    for i in range(3):
        a_above[i] = in_grad_above[i * HS : (i + 1) * HS]
    a_above[3] = out_total[HS:].astype(LOW)
    a_push_above.start()

    @pl.when(far == 0)
    def _():
        pltpu.make_async_copy(f_grad, f_sum, got_sems.at[2]).wait()
        give.wait_recv()
        f_sum[...] = (f_sum[...].astype(F32) + f_got[...].astype(F32)).astype(LOW)

    f_push.start()

    def after():
        put_grads(a_grad_ref, in_sum_ref, out_total[:HS])
        a_push.start()

    grad = input_back(
        at, dqkv_ref, a_ref, x_ref, gain_ref, dmid_ref, gain_grad_ref, total, (out_c, in_c, rin), rs_sems, buf, copy,
        in_sum_ref, after,
    )
    low_ref[...] = grad.astype(LOW)
    home.start()
    gain_sum[0, 0:1] = gain_grad_ref[...]
    gain_sum[0, 1:4] = gains_ref[...]
    for i, peer in enumerate(peers):
        copy = remote(gain_sum.at[i], heard.at[i], gain_sems.at[0, i], gain_sems.at[1, i], peer)
        copy.start()
        copy.wait()
        gain_sum[i + 1] = gain_sum[i] + heard[i]

    @pl.when(far == 1)
    def _():
        give.wait_send()

    for push in (*homes, f_push_above, f_push, a_push_above, a_push, home):
        push.finish()


VMEM_SPEC = pl.BlockSpec(memory_space=pltpu.VMEM)
ANY_SPEC = pl.BlockSpec(memory_space=pl.ANY)


def links():
    dma = pltpu.SemaphoreType.DMA
    return (dma((3, 8)), dma((3, 8)), dma((8,)), dma((8,)))


def sum_boxes(rows, width):
    return [
        pltpu.VMEM((rows, width), F32),
        pltpu.VMEM((4, rows, width), LOW),
        pltpu.VMEM((8, rows, width), LOW),
        pltpu.VMEM((7, rows, width), LOW),
    ]


def reach(kernel, number, args, outs, scratch, name, far=()):
    return pl.pallas_call(
        kernel,
        out_shape=[jax.ShapeDtypeStruct(shape, dtype) for shape, dtype, _ in outs],
        in_specs=[VMEM_SPEC] * len(args) + [ANY_SPEC] * len(far),
        out_specs=[ANY_SPEC if stays else VMEM_SPEC for _, _, stays in outs],
        scratch_shapes=scratch,
        compiler_params=pltpu.CompilerParams(
            collective_id=number, has_side_effects=number is not None, vmem_limit_bytes=VMEM_BYTES
        ),
        name=name,
    )(*args, *far)


TILE = 512
MORE = 16
DOC_ROOM = 13
FLOOR = -1e20


def one_hot(seg_ref, part):
    rows = lax.broadcasted_iota(jnp.int32, (MORE, TILE), 0)
    return (rows, rows == seg_ref[:, part])


def tiles(length):
    return [slice(i * TILE, (i + 1) * TILE) for i in range(length // TILE)]


def causal():
    return lax.broadcasted_iota(jnp.int32, (TILE, 1), 0) <= lax.broadcasted_iota(jnp.int32, (1, TILE), 1)


def attend_body(qkv_ref, seg_ref, att_ref, low_ref, lse_ref, key_x, query_x, val_x, scores, after):
    length = qkv_ref.shape[1]
    for part in tiles(length):
        rows, hot = one_hot(seg_ref, part)
        key = jnp.concatenate([qkv_ref[HS : 2 * HS, part].astype(F32), jnp.where(hot, 1.0, 0.0)])
        key_x[part] = key.T.astype(LOW)
        query_x[:HS, part] = qkv_ref[:HS, part]
        query_x[HS:, part] = jnp.where(hot | (rows >= DOC_ROOM), 0.0, NEGATIVE).astype(LOW)
        val_x[:HS, part] = qkv_ref[2 * HS :, part]
        val_x[HS:, part] = jnp.where(rows == 0, 1.0, 0.0).astype(LOW)

    def query_tile(qi):
        cols = slice(qi * TILE, (qi + 1) * TILE)
        query = query_x[:, cols]

        def ahead(slot, kb):
            scores[slot] = dot(key_x[span(kb, TILE)], query)

        def update(slot, kb, state, diagonal=False):
            largest, summed = state
            found = scores[slot]
            if diagonal:
                found = jnp.where(causal(), found, NEGATIVE)
            newest = jnp.maximum(largest, jnp.max(found, axis=0, keepdims=True))
            weights = jnp.exp(found - newest).astype(LOW)
            summed = summed * jnp.exp(largest - newest) + dot(val_x[:, span(kb, TILE)], weights)
            return (newest, summed)

        def pair(i, state):
            ahead(1, 2 * i + 1)
            state = update(0, 2 * i, state)
            ahead(0, 2 * i + 2)
            return update(1, 2 * i + 1, state)

        state = (jnp.full((1, TILE), FLOOR, F32), jnp.zeros((HS + MORE, TILE), F32))
        ahead(0, 0)
        state = lax.fori_loop(0, qi // 2, pair, state)
        if qi % 2:
            ahead(1, qi)
            state = update(0, qi - 1, state)
        largest, summed = update(qi % 2, qi, state, True)
        totals = summed[HS : HS + 1]
        attended = summed[:HS] / totals
        att_ref[:, cols] = attended
        low_ref[:, cols] = attended.astype(LOW)
        lse_ref[:, cols] = largest + jnp.log(totals)

    for qi in range(length // TILE):
        query_tile(qi)
        after(qi)


def attend_scratch(length):
    return [
        pltpu.VMEM((length, HS + MORE), LOW),
        pltpu.VMEM((HS + MORE, length), LOW),
        pltpu.VMEM((HS + MORE, length), LOW),
        pltpu.VMEM((2, TILE, TILE), F32),
    ]


def three(values):
    high = values.astype(LOW).astype(F32)
    mid = (values - high).astype(LOW).astype(F32)
    return (high, mid, values - high - mid)


def attend_back_body(
    qkv_ref, seg_ref, att_ref, lse_ref, dout_ref, cos_ref, sin_ref, extra_ref, dqkv_ref, send_ref,
    key_x, val_x, query_x, dout_x, dq, scores, along, after,
):
    length = qkv_ref.shape[1]
    half, count = HS // 2, length // TILE
    for part in tiles(length):
        rows, hot = one_hot(seg_ref, part)
        ones = jnp.where(rows >= DOC_ROOM, 1.0, 0.0)
        key = jnp.concatenate([qkv_ref[HS : 2 * HS, part].astype(F32), jnp.where(hot, 1.0, ones)])
        key_x[part] = key.T.astype(LOW)
        val_x[part] = jnp.concatenate([qkv_ref[2 * HS :, part].astype(F32), ones]).T.astype(LOW)

        def tail(values, rest, rows=rows):
            for i, piece in enumerate(three(values)):
                rest = jnp.where(rows == DOC_ROOM + i, piece, rest)
            return rest.astype(LOW)

        dout = dout_ref[:, part]
        delta = jnp.sum(dout.astype(F32) * att_ref[:, part], axis=0, keepdims=True)
        query_x[:HS, part] = qkv_ref[:HS, part]
        query_x[HS:, part] = tail(-lse_ref[:, part], jnp.where(hot, 0.0, NEGATIVE))
        dout_x[:HS, part] = dout
        dout_x[HS:, part] = tail(-delta, jnp.zeros((MORE, TILE), F32))
    dq[...] = jnp.zeros_like(dq)

    def key_tile(ki):
        here = slice(ki * TILE, (ki + 1) * TILE)
        rest = count - 1 - ki

        def ahead(slot, qb):
            cols = span(qb, TILE)
            scores[slot] = dot(key_x[here], query_x[:, cols])
            along[slot] = dot(val_x[here], dout_x[:, cols])

        def update(slot, qb, state, diagonal=False):
            dk, dv = state
            cols = span(qb, TILE)
            weights = jnp.exp(scores[slot])
            if diagonal:
                weights = jnp.where(causal(), weights, 0.0)
            ds = (weights * along[slot]).astype(LOW)
            dv = dv + dot(dout_x[:HS, cols], weights.astype(LOW), NT)
            dk = dk + dot(query_x[:HS, cols], ds, NT)
            dq[:, cols] += dot(qkv_ref[HS : 2 * HS, here], ds)
            return (dk, dv)

        def pair(i, state):
            qb = ki + 1 + 2 * i
            ahead(0, qb + 1)
            state = update(1, qb, state)
            ahead(1, qb + 2)
            return update(0, qb + 1, state)

        zero = jnp.zeros((HS, TILE), F32)
        ahead(0, ki)
        if rest:
            ahead(1, ki + 1)
        state = update(0, ki, (zero, zero), True)
        state = lax.fori_loop(0, max(0, (rest - 1) // 2), pair, state)
        if rest % 2:
            state = update(1, count - 1, state)
        elif rest:
            ahead(0, count - 1)
            state = update(1, count - 2, state)
            state = update(0, count - 1, state)
        dk, dv = state
        a, b = turned(dk[:half], dk[half:], cos_ref[:, here], -sin_ref[:, here])
        dqkv_ref[HS : HS + half, here] = a.astype(LOW)
        dqkv_ref[HS + half : 2 * HS, here] = b.astype(LOW)
        if send_ref is None:
            dqkv_ref[2 * HS :, here] = (dv + extra_ref[:, here]).astype(LOW)
        else:
            dqkv_ref[2 * HS :, here] = (0.5 * dv).astype(LOW)
            send_ref[:, here] = 0.5 * dv

    for ki in range(count):
        key_tile(ki)
        after(ki)
    scale = HS**-0.5
    a, b = turned(dq[:half] * scale, dq[half:] * scale, cos_ref[...], -sin_ref[...])
    dqkv_ref[:half] = a.astype(LOW)
    dqkv_ref[half:HS] = b.astype(LOW)


def attend_back_scratch(length):
    wide = HS + MORE
    return [
        pltpu.VMEM((length, wide), LOW),
        pltpu.VMEM((length, wide), LOW),
        pltpu.VMEM((wide, length), LOW),
        pltpu.VMEM((wide, length), LOW),
        pltpu.VMEM((HS, length), F32),
        pltpu.VMEM((2, TILE, TILE), F32),
        pltpu.VMEM((2, TILE, TILE), F32),
    ]


def number_of(y, s, z):
    return (y * 4 + s) * 4 + z


def far_pairs():
    return [
        (number_of(y, s, z), number_of(y, s, (z + 2) % 4))
        for y in range(2)
        for s in range(4)
        for z in range(4)
        if (y + s + z // 2) % 2 == 0
    ]


AXES = ("section", "seq", "tensor")


def on_grid(
    inputs, cotangent, lengths, w_query, w_key, w_value, w_out, w_gate, w_up, w_down, attn_gain, mlp_gain
):
    at = spot()
    y, x, c, half, p = at
    far = far_role(at) == 1
    rows, width = inputs.shape[1:]
    length = 16 * rows
    units = w_gate.shape[2] // 4
    length_row = lax.dynamic_index_in_dim(lengths, half, 0, keepdims=False)
    places = jnp.arange(length, dtype=jnp.int32)
    segment, within = doc_table(length_row, places)
    segment = segment[None]
    frequency = jnp.exp(jnp.arange(HS // 2, dtype=F32) * (-math.log(10000.0) / (HS // 2)))
    angles = within.astype(F32)[None, :] * frequency[:, None]
    tables = [jnp.cos(angles), jnp.sin(angles)]
    a_own = jnp.stack([w_query[0].T, w_key[0].T, w_value[0].T, w_out[0]])
    f_own = jnp.stack([w_gate[0].T, w_up[0].T, w_down[0]])
    dma = pltpu.SemaphoreType.DMA

    def vmem(*shape, dtype=LOW):
        return pltpu.VMEM(shape, dtype)

    def near(*shape, dtype=LOW):
        return (shape, dtype, False)

    def stays(*shape, dtype=LOW):
        return (shape, dtype, True)

    buf = [vmem(16, rows, width)]
    boxes = sum_boxes(rows, width)
    small_boxes = sum_boxes(2 * HS, width)
    wo_buf = [vmem(16, HS, width)]
    low_head = [vmem(HS, length)]
    block, low_block = [vmem(rows, width, dtype=F32)], [vmem(rows, width)]
    hidden = [vmem(length, units)] * 3
    dout_block = [vmem(16, HS, rows)]
    in_sum = [vmem(3 * HS, width, dtype=F32), vmem(4, HS, width)]
    turned_out, head_out, lse_out = near(3 * HS, length), near(HS, length, dtype=F32), near(1, length, dtype=F32)
    att_in_out, every = near(16, HS, rows), stays(16, rows, width)
    block_out, low_out, gain_out = near(rows, width, dtype=F32), near(rows, width), near(1, width, dtype=F32)
    dout_out, f_out = near(HS, length), near(3, units, width)
    hidden_far, home_out = stays(length, units), stays(2, rows, width)
    a_far, f_far = stays(4, HS, width), stays(3, units, width)
    f_half = stays(4, 3, units, width // 4)
    a_shards, f_shards = stays(2, 4, 4, HS, width // 4), stays(2, 4, 3, units, width // 4)

    both = lax.dynamic_index_in_dim(cotangent, 1 - half, 0, keepdims=False)
    own_top = jnp.where(
        far,
        lax.ppermute(both, AXES, far_pairs()),
        lax.dynamic_index_in_dim(cotangent, half, 0, keepdims=False),
    )
    (
        qkv0, att0, lse0, att_in0, wo_all0, own_in, mid0, out0, qkv1,
        normed0, nmid0, normed1, hid0, one0, two0, a0, a1, f0, f1, gains,
    ) = reach(
        first_kernel,
        0,
        [*tables, segment],
        [turned_out, head_out, lse_out, att_in_out, near(16, HS, width), low_out, block_out, low_out, turned_out]
        + [every] * 3
        + [hidden_far] * 3
        + [a_far, a_far, f_far, f_far, stays(2, 2, width, dtype=F32)],
        buf
        + low_head
        + [vmem(4, HS, width), vmem(3, units, width), vmem(2, 2, width, dtype=F32)]
        + hidden
        + attend_scratch(length)
        + boxes
        + [links(), links(), links(), row_sems(), dma((16,))]
        + [head_sems()] * 4
        + [dma((3,)), dma((3,)), dma((7,))],
        "first",
        [inputs, a_own, f_own, jnp.concatenate([attn_gain, mlp_gain])],
    )
    gain_in, gain_mid = [gains[i, 0:1] for i in range(2)], [gains[i, 1:2] for i in range(2)]
    att1, lse1, att_in1, dmid1, gmid1, dout1, f_grad1, mid1, hid1 = reach(
        turn_kernel,
        1,
        [qkv1, segment, a1, f1, gain_mid[1], out0, own_top],
        [head_out, lse_out, att_in_out, block_out, gain_out, dout_out, f_out, block_out, hidden_far],
        buf
        + buf
        + wo_buf
        + low_head
        + dout_block
        + boxes
        + [links(), links(), links(), row_sems(), row_sems(), dma((1,))],
        "turn",
    )
    extra, gin1, dmid0, gmid0, dout0, f_grad0, in_grad1, grad1, out1, home_out0, f_heard1 = reach(
        lower_kernel,
        2,
        [a1, gain_in[1], dmid1, gain_mid[0]],
        [head_out, gain_out, block_out, gain_out, dout_out, f_out, near(3 * HS, width), low_out, low_out, home_out, f_far],
        buf
        + wo_buf
        + [vmem(3 * HS, length)]
        + in_sum[:1]
        + dout_block
        + boxes
        + [links(), links(), row_sems(), dma((2,)), home_sems(), dma((18,)), dma((8,)), pltpu.SemaphoreType.REGULAR],
        "lower",
        [out0, f0, mid0, qkv1, segment, att1, lse1, dout1, *tables, hid0, one0, two0, normed1, nmid0, wo_all0]
        + [hid1, mid1, f1, f_grad1, out0],
    )
    home_grad0, home_out1, home_grad1, f_in0, f_in1, a_in0, a_in1, gain_sums = reach(
        last_kernel,
        3,
        [qkv0, segment, att0, lse0, dout0, *tables, extra, own_in, a0, gain_in[0], dmid0, att_in0, att_in1, dmid1]
        + [in_grad1, jnp.concatenate([gin1, gmid0, gmid1])],
        [home_out] * 3 + [f_half, f_half, a_shards, a_shards, near(6, 4, width, dtype=F32)],
        buf
        + [vmem(3 * HS, length)]
        + low_block
        + [vmem(2, rows, width)]
        + in_sum
        + [vmem(4, HS, width), vmem(1, width, dtype=F32), vmem(5, 4, width, dtype=F32)]
        + [vmem(3, units, width)] * 3
        + attend_back_scratch(length)
        + boxes
        + small_boxes
        + [links(), links()]
        + [shard_sems()] * 4
        + [home_sems()] * 3
        + [dma((2, 5)), dma((4,)), dma((1,))],
        "last",
        [f_grad0, f_grad1, f_heard1, out1, grad1, normed0],
    )
    on_first = y == 0
    a_sum = jnp.sum(jnp.where(on_first, a_in0, a_in1).astype(F32), axis=0)
    f_total = jnp.where(on_first, f_in0, f_in1).astype(F32)
    a_sum = jnp.transpose(a_sum, (1, 0, 2, 3)).reshape(4, 4 * HS, width // 4)
    f_total = jnp.transpose(f_total, (1, 0, 2, 3)).reshape(3, 4 * units, width // 4)
    layer_out = jnp.where(on_first, home_out0, home_out1)
    input_grad = jnp.where(on_first, home_grad0, home_grad1).astype(F32)
    share = width // 16
    first_col = (4 * (2 * x + c) + 2 * half + p) * share
    gain_share = lax.dynamic_slice_in_dim(gain_sums[5], first_col, share, 1)
    gain_in_share = jnp.where(on_first, gain_share[0:1], gain_share[1:2])
    gain_mid_share = jnp.where(on_first, gain_share[2:3], gain_share[3:4])
    return (
        layer_out[None],
        input_grad[None],
        a_sum[0].T[None],
        a_sum[1].T[None],
        a_sum[2].T[None],
        a_sum[3][None],
        f_total[0].T[None],
        f_total[1].T[None],
        f_total[2][None],
        gain_in_share,
        gain_mid_share,
    )


def solution(mesh):
    in_specs = (
        P(None, ("seq", "tensor"), None),
        P(None, ("seq", "tensor"), None),
        P(),
        P("section", "seq", "tensor"),
        P("section", "seq", "tensor"),
        P("section", "seq", "tensor"),
        P("section", "tensor", "seq"),
        P("section", "seq", "tensor"),
        P("section", "seq", "tensor"),
        P("section", "tensor", "seq"),
        P("section", None),
        P("section", None),
    )
    out_specs = (
        P("section", None, ("seq", "tensor"), None),
        P("section", None, ("seq", "tensor"), None),
        P("section", "seq", "tensor"),
        P("section", "seq", "tensor"),
        P("section", "seq", "tensor"),
        P("section", "tensor", "seq"),
        P("section", "seq", "tensor"),
        P("section", "seq", "tensor"),
        P("section", "tensor", "seq"),
        P("section", ("seq", "tensor")),
        P("section", ("seq", "tensor")),
    )
    grid = (mesh.shape["section"], mesh.shape["seq"], mesh.shape["tensor"]) == (2, 4, 4)
    return jax.shard_map(
        on_grid if grid else on_device, mesh=mesh, in_specs=in_specs, out_specs=out_specs, check_vma=False
    )
```

```python
import functools
import math

import jax
import jax.numpy as jnp
from jax import lax
from jax.experimental import pallas as pl
from jax.experimental.pallas import tpu as pltpu
from jax.sharding import PartitionSpec as P

HS = 64


EPSILON = 1e-05
NEGATIVE = -1e30


def shifted(shard, axis, by):
    peers = lax.axis_size(axis)
    pairs = [(i, i + by) for i in range(peers) if 0 <= i + by < peers]
    return lax.ppermute(shard, axis, pairs)


def product(left, right):
    return jnp.dot(left, right, preferred_element_type=jnp.float32)


def inner_rows(left, right):
    return lax.dot_general(
        left, right, (((0,), (0,)), ((), ())), preferred_element_type=jnp.float32
    )


def against(left, right):
    return lax.dot_general(
        left, right, (((1,), (1,)), ((), ())), preferred_element_type=jnp.float32
    )


def doc_table(length_row, places):
    doc_ends = jnp.cumsum(length_row)
    doc_starts = doc_ends - length_row
    segment = jnp.sum((places[:, None] >= doc_ends[None, :]).astype(jnp.int32), axis=1)
    member = segment[:, None] == jnp.arange(length_row.shape[0], dtype=jnp.int32)[None, :]
    offset = jnp.sum(jnp.where(member, doc_starts[None, :], 0), axis=1)
    return (segment, places - offset)


def rotate(matrix, within, direction):
    row_count = matrix.shape[0]
    head_count = matrix.shape[1] // HS
    half_size = HS // 2
    frequency = jnp.exp(jnp.arange(half_size, dtype=jnp.float32) * (-math.log(10000.0) / half_size))
    angles = within.astype(jnp.float32)[:, None] * frequency[None, :]
    cosine = jnp.cos(angles)[:, None, :]
    sine_part = direction * jnp.sin(angles)[:, None, :]
    paired = matrix.reshape(row_count, head_count, 2, half_size)
    former = paired[:, :, 0, :]
    latter = paired[:, :, 1, :]
    turned = jnp.stack(
        [former * cosine - latter * sine_part, latter * cosine + former * sine_part], axis=2
    )
    return turned.reshape(row_count, head_count * HS)


def norm_rows(values, gain_row):
    inverse = lax.rsqrt(jnp.mean(values * values, axis=-1, keepdims=True) + EPSILON)
    unit_rows = values * inverse
    return (unit_rows, inverse, (unit_rows * gain_row).astype(jnp.bfloat16))


def norm_back(grad_normed, unit_rows, inverse, gain_row):
    shaped = grad_normed * gain_row
    inner = jnp.mean(shaped * unit_rows, axis=-1, keepdims=True)
    return (inverse * (shaped - unit_rows * inner), jnp.sum(grad_normed * unit_rows, axis=0))


def spread(values):
    return lax.all_gather(values, "tensor", axis=0, tiled=True)


def fold_rows(values):
    return lax.psum_scatter(
        values.astype(jnp.bfloat16), "tensor", scatter_dimension=0, tiled=True
    ).astype(jnp.float32)


def allowed_mask(places, segment, key_places, key_segment):
    return (key_places[None, :] <= places[:, None]) & (key_segment[None, :] == segment[:, None])


def project(normed_all, matrices, within, mixin, on_first):
    query_rows = rotate(product(normed_all, matrices[0]), within, 1.0).astype(jnp.bfloat16)
    key_rows = rotate(product(normed_all, matrices[1]), within, 1.0).astype(jnp.bfloat16)
    value_raw = product(normed_all, matrices[2])
    value_rows = jnp.where(
        on_first, value_raw, 0.5 * value_raw + 0.5 * mixin.astype(jnp.float32)
    ).astype(jnp.bfloat16)
    return (query_rows, key_rows, value_rows)


def cycle_attend(query_rows, key_rows, value_rows, places, segment, length_row):
    row_count = query_rows.shape[0]
    head_count = query_rows.shape[1] // HS
    query_heads = query_rows.reshape(row_count, head_count, HS)
    largest = jnp.full((head_count, row_count), NEGATIVE, jnp.float32)
    piece_keys = lax.all_gather(key_rows, "seq", axis=0, tiled=True)
    piece_values = lax.all_gather(value_rows, "seq", axis=0, tiled=True)
    piece_rows = piece_keys.shape[0]
    key_places = jnp.arange(piece_rows, dtype=jnp.int32)
    key_segment = doc_table(length_row, key_places)[0]
    allowed = allowed_mask(places, segment, key_places, key_segment)
    scores = jnp.einsum(
        "qhd,khd->hqk",
        query_heads,
        piece_keys.reshape(piece_rows, head_count, HS),
        preferred_element_type=jnp.float32,
    ) * HS ** (-0.5)
    masked = jnp.where(allowed[None], scores, NEGATIVE)
    newest = jnp.maximum(largest, jnp.max(masked, axis=2))
    weights = jnp.where(allowed[None], jnp.exp(masked - newest[:, :, None]), 0.0)
    totals = jnp.sum(weights, axis=2)
    summed = jnp.einsum(
        "hqk,khd->hqd",
        weights.astype(jnp.bfloat16),
        piece_values.reshape(piece_rows, head_count, HS),
        preferred_element_type=jnp.float32,
    )
    largest, totals, summed = (newest, totals, summed)
    attended = summed / totals[:, :, None]
    return jnp.transpose(attended, (1, 0, 2)).reshape(row_count, head_count * HS)


def forward_layer(residual, mixin, on_first, matrices, gain_pair, places, length_row):
    segment, within = doc_table(length_row, places)
    normed_in = norm_rows(residual, gain_pair[0])[2]
    normed_all = spread(normed_in)
    query_rows, key_rows, value_rows = project(normed_all, matrices, within, mixin, on_first)
    attended = cycle_attend(query_rows, key_rows, value_rows, places, segment, length_row)
    middle = residual + fold_rows(product(attended.astype(jnp.bfloat16), matrices[3]))
    normed_mid = norm_rows(middle, gain_pair[1])[2]
    normed_mid_all = spread(normed_mid)
    gate_rows = product(normed_mid_all, matrices[4])
    up_rows = product(normed_mid_all, matrices[5])
    hidden = (jax.nn.silu(gate_rows) * up_rows).astype(jnp.bfloat16)
    return (middle + fold_rows(product(hidden, matrices[6])), value_rows)


def backward_layer(
    residual, mixin, grad_top, extra_values, on_first, matrices, gain_pair, places, length_row
):
    segment, within = doc_table(length_row, places)
    unit_in, inverse_in, normed_in = norm_rows(residual, gain_pair[0])
    normed_all = spread(normed_in)
    query_rows, key_rows, value_rows = project(normed_all, matrices, within, mixin, on_first)
    all_keys, all_values = (
        lax.all_gather(key_rows, "seq", axis=0, tiled=True),
        lax.all_gather(value_rows, "seq", axis=0, tiled=True),
    )
    row_count = query_rows.shape[0]
    head_count = query_rows.shape[1] // HS
    total_rows = all_keys.shape[0]
    block_count = total_rows // row_count
    query_heads = query_rows.reshape(row_count, head_count, HS)
    key_blocks = all_keys.reshape(block_count, row_count, head_count, HS)
    value_blocks = all_values.reshape(block_count, row_count, head_count, HS)
    block_numbers = jnp.arange(block_count, dtype=jnp.int32)

    def block_scores(block_number, block_keys):
        key_places = block_number * row_count + jnp.arange(row_count, dtype=jnp.int32)
        key_segment = doc_table(length_row, key_places)[0]
        allowed = allowed_mask(places, segment, key_places, key_segment)
        scores = jnp.einsum(
            "qhd,khd->hqk", query_heads, block_keys, preferred_element_type=jnp.float32
        ) * HS ** (-0.5)
        return (allowed, jnp.where(allowed[None], scores, NEGATIVE))

    def first_pass(running, block_item):
        largest, totals, summed = running
        block_number, block_keys, block_values = block_item
        allowed, masked = block_scores(block_number, block_keys)
        newest = jnp.maximum(largest, jnp.max(masked, axis=2))
        rescale = jnp.exp(largest - newest)
        weights = jnp.where(allowed[None], jnp.exp(masked - newest[:, :, None]), 0.0)
        totals = totals * rescale + jnp.sum(weights, axis=2)
        summed = summed * rescale[:, :, None] + jnp.einsum(
            "hqk,khd->hqd",
            weights.astype(jnp.bfloat16),
            block_values,
            preferred_element_type=jnp.float32,
        )
        return ((newest, totals, summed), None)

    start_state = (
        jnp.full((head_count, row_count), NEGATIVE, jnp.float32),
        jnp.zeros((head_count, row_count), jnp.float32),
        jnp.zeros((head_count, row_count, HS), jnp.float32),
    )
    (largest, totals, summed), _ = lax.scan(
        first_pass, start_state, (block_numbers, key_blocks, value_blocks)
    )
    attended = summed / totals[:, :, None]
    attended_low = (
        jnp.transpose(attended, (1, 0, 2)).reshape(row_count, head_count * HS).astype(jnp.bfloat16)
    )
    middle = residual + fold_rows(product(attended_low, matrices[3]))
    unit_mid, inverse_mid, normed_mid = norm_rows(middle, gain_pair[1])
    normed_mid_all = spread(normed_mid)
    gate_rows = product(normed_mid_all, matrices[4])
    up_rows = product(normed_mid_all, matrices[5])
    sigmoid_gate = jax.nn.sigmoid(gate_rows)
    activated = gate_rows * sigmoid_gate
    hidden = (activated * up_rows).astype(jnp.bfloat16)
    grad_top_all = spread(grad_top.astype(jnp.bfloat16))
    grad_w_down = inner_rows(hidden, grad_top_all)
    grad_hidden = against(grad_top_all, matrices[6])
    grad_gate = (
        grad_hidden * up_rows * sigmoid_gate * (1.0 + gate_rows * (1.0 - sigmoid_gate))
    ).astype(jnp.bfloat16)
    grad_up = (grad_hidden * activated).astype(jnp.bfloat16)
    grad_w_gate = inner_rows(normed_mid_all, grad_gate)
    grad_w_up = inner_rows(normed_mid_all, grad_up)
    grad_normed_mid = fold_rows(against(grad_gate, matrices[4]) + against(grad_up, matrices[5]))
    grad_middle, grad_gain_mid = norm_back(grad_normed_mid, unit_mid, inverse_mid, gain_pair[1])
    grad_middle = grad_middle + grad_top
    grad_middle_all = spread(grad_middle.astype(jnp.bfloat16))
    grad_w_out = inner_rows(attended_low, grad_middle_all)
    grad_attended = against(grad_middle_all, matrices[3]).astype(jnp.bfloat16)
    grad_heads = jnp.transpose(grad_attended.reshape(row_count, head_count, HS), (1, 0, 2))
    delta = jnp.sum(grad_heads.astype(jnp.float32) * attended, axis=2)
    scaled_grad = grad_heads.astype(jnp.float32) / totals[:, :, None]
    scaled_high = scaled_grad.astype(jnp.bfloat16)
    scaled_rest = (scaled_grad - scaled_high.astype(jnp.float32)).astype(jnp.bfloat16)
    inverse_totals = 1.0 / totals[:, :, None]

    def second_pass(grad_sum, block_item):
        block_number, block_keys, block_values = block_item
        allowed, masked = block_scores(block_number, block_keys)
        weights = jnp.where(allowed[None], jnp.exp(masked - largest[:, :, None]), 0.0)
        low_weights = weights.astype(jnp.bfloat16)
        along = jnp.einsum(
            "hqd,khd->hqk", grad_heads, block_values, preferred_element_type=jnp.float32
        )
        grad_scores = (weights * inverse_totals * (along - delta[:, :, None])).astype(jnp.bfloat16)
        grad_sum = grad_sum + jnp.einsum(
            "hqk,khd->qhd", grad_scores, block_keys, preferred_element_type=jnp.float32
        ) * HS ** (-0.5)
        block_key_grad = jnp.einsum(
            "hqk,qhd->khd", grad_scores, query_heads, preferred_element_type=jnp.float32
        ) * HS ** (-0.5)
        block_value_grad = jnp.einsum(
            "hqk,hqd->khd", low_weights, scaled_high, preferred_element_type=jnp.float32
        ) + jnp.einsum("hqk,hqd->khd", low_weights, scaled_rest, preferred_element_type=jnp.float32)
        return (grad_sum, (block_key_grad, block_value_grad))

    grad_queries, (grad_keys, grad_values) = lax.scan(
        second_pass,
        jnp.zeros((row_count, head_count, HS), jnp.float32),
        (block_numbers, key_blocks, value_blocks),
    )
    own_keys, own_values = (
        lax.psum_scatter(
            grad_keys.reshape(total_rows, head_count * HS).astype(jnp.bfloat16),
            "seq",
            scatter_dimension=0,
            tiled=True,
        ).astype(jnp.float32),
        lax.psum_scatter(
            grad_values.reshape(total_rows, head_count * HS).astype(jnp.bfloat16),
            "seq",
            scatter_dimension=0,
            tiled=True,
        ).astype(jnp.float32),
    )
    grad_value_raw = jnp.where(on_first, own_values + extra_values, 0.5 * own_values).astype(
        jnp.bfloat16
    )
    send_values = 0.5 * own_values
    grad_query_raw = rotate(grad_queries.reshape(row_count, head_count * HS), within, -1.0).astype(
        jnp.bfloat16
    )
    grad_key_raw = rotate(own_keys, within, -1.0).astype(jnp.bfloat16)
    grad_w_query = inner_rows(normed_all, grad_query_raw)
    grad_w_key = inner_rows(normed_all, grad_key_raw)
    grad_w_value = inner_rows(normed_all, grad_value_raw)
    grad_normed_in = fold_rows(
        against(grad_query_raw, matrices[0])
        + against(grad_key_raw, matrices[1])
        + against(grad_value_raw, matrices[2])
    )
    grad_in, grad_gain_in = norm_back(grad_normed_in, unit_in, inverse_in, gain_pair[0])
    weight_terms = (
        grad_w_query,
        grad_w_key,
        grad_w_value,
        grad_w_out,
        grad_w_gate,
        grad_w_up,
        grad_w_down,
    )
    return (grad_in + grad_middle, send_values, weight_terms, (grad_gain_in, grad_gain_mid))


def on_device(
    inputs,
    cotangent,
    lengths,
    w_query,
    w_key,
    w_value,
    w_out,
    w_gate,
    w_up,
    w_down,
    attn_gain,
    mlp_gain,
):
    section_index = lax.axis_index("section")
    on_first = section_index == 0
    micro_count = inputs.shape[0]
    local_rows = inputs.shape[1]
    model_width = inputs.shape[2]
    group_rows = local_rows * lax.axis_size("tensor")
    head_width = w_query.shape[2]
    row_values = local_rows * model_width
    places = lax.axis_index("seq") * group_rows + jnp.arange(group_rows, dtype=jnp.int32)
    gain_pair = (attn_gain[0], mlp_gain[0])
    gathered = (
        lax.all_gather(w_query[0], "seq", axis=0, tiled=True),
        lax.all_gather(w_key[0], "seq", axis=0, tiled=True),
        lax.all_gather(w_value[0], "seq", axis=0, tiled=True),
        lax.all_gather(w_out[0], "seq", axis=1, tiled=True),
        lax.all_gather(w_gate[0], "seq", axis=0, tiled=True),
        lax.all_gather(w_up[0], "seq", axis=0, tiled=True),
        lax.all_gather(w_down[0], "seq", axis=1, tiled=True),
    )
    recv_rows = jnp.zeros((local_rows, model_width), jnp.bfloat16)
    recv_values = jnp.zeros((group_rows, head_width), jnp.bfloat16)
    kept_inputs = jnp.zeros((micro_count, local_rows, model_width), jnp.bfloat16)
    kept_values = jnp.zeros((micro_count, group_rows, head_width), jnp.bfloat16)
    kept_outputs = jnp.zeros((micro_count, local_rows, model_width), jnp.bfloat16)
    for moment in range(micro_count + 1):
        which = moment - section_index
        usable = (which >= 0) & (which < micro_count)
        slot_index = jnp.clip(which, 0, micro_count - 1)
        own_rows = lax.dynamic_index_in_dim(inputs, slot_index, 0, keepdims=False)
        layer_in = jnp.where(on_first, own_rows, recv_rows)
        length_row = lax.dynamic_index_in_dim(lengths, slot_index, 0, keepdims=False)
        result, value_rows = forward_layer(
            layer_in.astype(jnp.float32),
            recv_values,
            on_first,
            gathered,
            gain_pair,
            places,
            length_row,
        )
        result_low = result.astype(jnp.bfloat16)
        kept_inputs = jnp.where(
            usable,
            lax.dynamic_update_index_in_dim(kept_inputs, layer_in, slot_index, 0),
            kept_inputs,
        )
        kept_values = jnp.where(
            usable,
            lax.dynamic_update_index_in_dim(kept_values, recv_values, slot_index, 0),
            kept_values,
        )
        kept_outputs = jnp.where(
            usable,
            lax.dynamic_update_index_in_dim(kept_outputs, result_low, slot_index, 0),
            kept_outputs,
        )
        if moment < micro_count:
            packed = jnp.concatenate([result_low.reshape(-1), value_rows.reshape(-1)])
            arrived = shifted(packed, "section", 1)
            recv_rows = arrived[:row_values].reshape(local_rows, model_width)
            recv_values = arrived[row_values:].reshape(group_rows, head_width)
    grad_rows_in = jnp.zeros((local_rows, model_width), jnp.float32)
    grad_values_in = jnp.zeros((group_rows, head_width), jnp.float32)
    grad_inputs = jnp.zeros((micro_count, local_rows, model_width), jnp.float32)
    weight_sums = tuple((jnp.zeros(matrix.shape, jnp.float32) for matrix in gathered))
    share_sums = (
        jnp.zeros(w_query[0].shape, jnp.float32),
        jnp.zeros(w_key[0].shape, jnp.float32),
        jnp.zeros(w_value[0].shape, jnp.float32),
        jnp.zeros(w_out[0].shape, jnp.float32),
        jnp.zeros(w_gate[0].shape, jnp.float32),
        jnp.zeros(w_up[0].shape, jnp.float32),
        jnp.zeros(w_down[0].shape, jnp.float32),
    )
    gain_sums = (jnp.zeros((model_width,), jnp.float32), jnp.zeros((model_width,), jnp.float32))
    for moment in range(micro_count + 1):
        which = moment - (1 - section_index)
        usable = (which >= 0) & (which < micro_count)
        slot_index = jnp.clip(which, 0, micro_count - 1)
        matrices = (
            lax.all_gather(w_query[0], "seq", axis=0, tiled=True),
            lax.all_gather(w_key[0], "seq", axis=0, tiled=True),
            lax.all_gather(w_value[0], "seq", axis=0, tiled=True),
            lax.all_gather(w_out[0], "seq", axis=1, tiled=True),
            lax.all_gather(w_gate[0], "seq", axis=0, tiled=True),
            lax.all_gather(w_up[0], "seq", axis=0, tiled=True),
            lax.all_gather(w_down[0], "seq", axis=1, tiled=True),
        )
        layer_in = lax.dynamic_index_in_dim(kept_inputs, slot_index, 0, keepdims=False).astype(
            jnp.float32
        )
        mixin = lax.dynamic_index_in_dim(kept_values, slot_index, 0, keepdims=False)
        length_row = lax.dynamic_index_in_dim(lengths, slot_index, 0, keepdims=False)
        own_grad = lax.dynamic_index_in_dim(cotangent, slot_index, 0, keepdims=False).astype(
            jnp.float32
        )
        grad_top = jnp.where(usable, jnp.where(on_first, grad_rows_in, own_grad), 0.0)
        extra_values = jnp.where(usable & on_first, grad_values_in, 0.0)
        grad_in, send_values, weight_terms, gain_terms = backward_layer(
            layer_in,
            mixin,
            grad_top,
            extra_values,
            on_first,
            matrices,
            gain_pair,
            places,
            length_row,
        )
        gain_sums = (gain_sums[0] + gain_terms[0], gain_sums[1] + gain_terms[1])
        weight_sums = tuple((total + term for total, term in zip(weight_sums, weight_terms)))
        grad_inputs = jnp.where(
            usable,
            lax.dynamic_update_index_in_dim(grad_inputs, grad_in, slot_index, 0),
            grad_inputs,
        )
        if moment < micro_count:
            packed = jnp.concatenate([grad_in.reshape(-1), send_values.reshape(-1)])
            arrived = shifted(packed.astype(jnp.bfloat16), "section", -1).astype(packed.dtype)
            grad_rows_in = arrived[:row_values].reshape(local_rows, model_width)
            grad_values_in = arrived[row_values:].reshape(group_rows, head_width)
    share_sums = (
        lax.psum_scatter(
            weight_sums[0].astype(jnp.bfloat16), "seq", scatter_dimension=0, tiled=True
        ).astype(jnp.float32),
        lax.psum_scatter(
            weight_sums[1].astype(jnp.bfloat16), "seq", scatter_dimension=0, tiled=True
        ).astype(jnp.float32),
        lax.psum_scatter(
            weight_sums[2].astype(jnp.bfloat16), "seq", scatter_dimension=0, tiled=True
        ).astype(jnp.float32),
        lax.psum_scatter(
            weight_sums[3].astype(jnp.bfloat16), "seq", scatter_dimension=1, tiled=True
        ).astype(jnp.float32),
        lax.psum_scatter(
            weight_sums[4].astype(jnp.bfloat16), "seq", scatter_dimension=0, tiled=True
        ).astype(jnp.float32),
        lax.psum_scatter(
            weight_sums[5].astype(jnp.bfloat16), "seq", scatter_dimension=0, tiled=True
        ).astype(jnp.float32),
        lax.psum_scatter(
            weight_sums[6].astype(jnp.bfloat16), "seq", scatter_dimension=1, tiled=True
        ).astype(jnp.float32),
    )
    gain_shares = (
        lax.psum_scatter(gain_sums[0], ("seq", "tensor"), scatter_dimension=0, tiled=True),
        lax.psum_scatter(gain_sums[1], ("seq", "tensor"), scatter_dimension=0, tiled=True),
    )
    return (
        kept_outputs[None],
        grad_inputs[None],
        share_sums[0][None],
        share_sums[1][None],
        share_sums[2][None],
        share_sums[3][None],
        share_sums[4][None],
        share_sums[5][None],
        share_sums[6][None],
        gain_shares[0][None],
        gain_shares[1][None],
    )


MESH_ID = pl.DeviceIdType.MESH
LOW = jnp.bfloat16
F32 = jnp.float32
ORDERS = ((1, 2, 4), (2, 4, 1), (4, 1, 2))
LEVELS = ((0,), (1, 2, 4), (3, 5, 6), (7,))
NT = (((1,), (1,)), ((), ()))
NN = (((1,), (0,)), ((), ()))
TN = (((0,), (0,)), ((), ()))
VMEM_BYTES = 53 * 2**20


def dot(left, right, dims=NN):
    return lax.dot_general(left, right, dims, preferred_element_type=F32)


def flip(value, bit):
    if isinstance(bit, int):
        return 1 - value if bit else value
    return value + bit - 2 * value * bit


def spot():
    y, s, z = lax.axis_index("section"), lax.axis_index("seq"), lax.axis_index("tensor")
    return (y, lax.div(s, 2), lax.rem(s, 2), lax.div(z, 2), lax.rem(z, 2))


def device(at):
    y, x, c, h, p = at
    return (y, 2 * x + c, 2 * h + p)


def moved(at, mask, core=0):
    y, x, c, h, p = at
    if isinstance(mask, int):
        bits = (mask & 1, (mask >> 1) & 1, mask >> 2)
    else:
        bits = (lax.rem(mask, 2), lax.rem(lax.div(mask, 2), 2), lax.div(mask, 4))
    return (flip(y, bits[1]), flip(x, bits[0]), flip(c, core), h, flip(p, bits[2]))


def far_role(at):
    return flip(flip(at[0], at[2]), at[3])


def partner_of(at):
    y, x, c, h, p = at
    return (y, x, c, 1 - h, p)


def lane_of(at):
    return 2 * flip(at[3], far_role(at)) + at[4]


def block_of(at):
    return (2 * at[1] + at[2]) * 4 + lane_of(at)


def level_mask(level, i):
    if level == 0:
        return 0 * i
    if level == 1:
        return 1 + i + lax.div(i, 2)
    if level == 2:
        return 3 + i + lax.div(i + 1, 2)
    return 0 * i + 7


def last_bit(k, mask):
    return [bit for bit in ORDERS[k] if bit & mask][-1]


def parts_of(rows):
    units = rows // 16
    small = units // 3
    sizes = (16 * (units - 2 * small), 16 * small, 16 * small)
    return ((0, sizes[0]), (sizes[0], sizes[1]), (sizes[0] + sizes[1], sizes[2]))


def remote(src, dst, send, recv, at):
    return pltpu.make_async_remote_copy(
        src_ref=src, dst_ref=dst, send_sem=send, recv_sem=recv, device_id=device(at), device_id_type=MESH_ID
    )


def others(at):
    return [moved(at, mask, core) for mask in range(8) for core in range(2) if mask + core]


def neighbours(at):
    return [moved(at, mask, core) for mask, core in ((1, 0), (2, 0), (4, 0), (0, 1))]


def greet(at, *pushes, peers=(), all_rows=True):
    met = (others(at) if all_rows else neighbours(at)) + list(peers)
    count = len(met)
    for peer in met:
        signal(peer)
    for push in pushes:
        count = count + push.greet()
    pl.semaphore_wait(pltpu.get_barrier_semaphore(), count)


def run(steps):
    for _ in steps:
        pass


def gather(*args, **kwargs):
    run(gathering(*args, **kwargs))


def gathering(at, buf, sems, on_block=None, keep=None, ready=None):
    send, recv, csend, crecv = sems
    parts = parts_of(buf.shape[1])

    def rows(mask, k, core=0):
        return buf.at[block_of(moved(at, mask, core)), pl.ds(*parts[k])]

    def hop(k, target):
        bit = last_bit(k, target)
        ref = rows(target ^ bit, k)
        return remote(ref, ref, send.at[k, target], recv.at[k, target], moved(at, bit))

    def arrival(k, target):
        ref = rows(target, k)
        return remote(ref, ref, send.at[k, target], recv.at[k, target], moved(at, last_bit(k, target)))

    def across(mask, core=0):
        ref = buf.at[block_of(moved(at, mask, core))]
        return remote(ref, ref, csend.at[mask], crecv.at[mask], moved(at, 0, 1))

    def visit(level, core):
        if on_block is None and keep is None:
            return

        def one(i, none):
            b = block_of(moved(at, level_mask(level, i), core))
            if keep is not None:
                pltpu.make_async_copy(buf.at[b], keep[0].at[b], keep[1].at[b]).start()
            if on_block is not None:
                on_block(b)
            return none

        lax.fori_loop(0, len(LEVELS[level]), one, 0)

    for i in range(2):
        for k in range(3):
            hop(k, ORDERS[k][i]).start()
        if i == 0:
            across(0).start()
    if ready is not None:
        ready()
    visit(0, 0)
    across(0, 1).wait_recv()
    visit(0, 1)
    yield
    for k in range(3):
        first, second, third = ORDERS[k]
        arrival(k, first).wait_recv()
        hop(k, first | second).start()
    for k in range(3):
        first, second, third = ORDERS[k]
        hop(k, third).start()
        hop(k, first | third).start()
    yield
    for k in range(3):
        first, second, third = ORDERS[k]
        arrival(k, second).wait_recv()
        hop(k, second | third).start()
    yield
    for k in range(3):
        first, second, third = ORDERS[k]
        arrival(k, first | second).wait_recv()
        hop(k, 7).start()
    yield
    for level in (1, 2, 3):
        for mask in LEVELS[level]:
            for k in range(3):
                first, second, third = ORDERS[k]
                if mask not in (first, second, first | second):
                    arrival(k, mask).wait_recv()
            across(mask).start()
        visit(level, 0)
        for mask in LEVELS[level]:
            across(mask, 1).wait_recv()
        visit(level, 1)
        yield
    for k in range(3):
        for target in range(1, 8):
            hop(k, target).wait_send()
    for mask in range(8):
        across(mask).wait_send()


def kept(buf, keep):
    for b in range(16):
        pltpu.make_async_copy(buf.at[b], keep[0].at[b], keep[1].at[b]).wait()


def scatter(*args, **kwargs):
    run(scattering(*args, **kwargs))


def scattering(at, total, boxes, sems, partial, before_last=None):
    out_c, in_c, rin = boxes
    send, recv, csend, crecv = sems
    parts = parts_of(total.shape[0])

    def hop(k, target):
        rows = pl.ds(*parts[k])
        return remote(
            in_c.at[target, rows],
            rin.at[target - 1, rows],
            send.at[k, target],
            recv.at[k, target],
            moved(at, last_bit(k, target)),
        )

    def across(mask):
        slot = 0 if mask in (0, 7) else 1 + (LEVELS[1] + LEVELS[2]).index(mask) % 3
        return remote(out_c.at[slot], in_c.at[mask], csend.at[mask], crecv.at[mask], moved(at, 0, 1))

    def emit(level):
        if level < 2:
            for mask in LEVELS[3 - level]:
                across(mask).wait_send()

        def one(i, none):
            slot = 1 + i if level in (1, 2) else 0
            out_c[slot] = partial(block_of(moved(at, level_mask(level, i), 1))).astype(LOW)
            return none

        lax.fori_loop(0, len(LEVELS[level]), one, 0)
        for mask in LEVELS[level]:
            across(mask).start()

    def settle(level):
        for mask in LEVELS[level]:
            across(mask).wait_recv()

        def one(i, none):
            mask = level_mask(level, i)
            mine = partial(block_of(moved(at, mask))) + in_c[mask].astype(F32)
            if level == 0:
                total[...] = mine
            else:
                in_c[mask] = mine.astype(LOW)
            return none

        lax.fori_loop(0, len(LEVELS[level]), one, 0)
        for mask in LEVELS[level]:
            for k in range(3):
                if mask & ORDERS[k][2]:
                    hop(k, mask).start()

    def arrived(k, target):
        hop(k, target).wait_recv()
        return rin[target - 1, pl.ds(*parts[k])].astype(F32)

    emit(3)
    emit(2)
    yield
    settle(3)
    settle(2)
    emit(1)
    yield
    settle(1)
    if before_last is not None:
        before_last()
    emit(0)
    settle(0)
    yield
    for mask_of in (lambda a, b: a | b, lambda a, b: b):
        for k in range(3):
            first, second, third = ORDERS[k]
            mask, rows = mask_of(first, second), pl.ds(*parts[k])
            in_c[mask, rows] = (in_c[mask, rows].astype(F32) + arrived(k, mask | third)).astype(LOW)
            hop(k, mask).start()
        yield
    for k in range(3):
        first, second, third = ORDERS[k]
        rows = pl.ds(*parts[k])
        in_c[first, rows] = (
            in_c[first, rows].astype(F32) + arrived(k, first | third) + arrived(k, first | second)
        ).astype(LOW)
        hop(k, first).start()
    yield
    for k in range(3):
        first, second, third = ORDERS[k]
        rows = pl.ds(*parts[k])
        total[rows] = total[rows] + arrived(k, third) + arrived(k, second) + arrived(k, first)
    for k in range(3):
        for target in range(1, 8):
            hop(k, target).wait_send()
    for mask in LEVELS[0] + LEVELS[1]:
        across(mask).wait_send()


class ToRows:
    def __init__(self, at, block, place, sems):
        self.at, self.block, self.place = at, block, place
        self.send, self.recv, self.local = sems
        self.mine = block_of(at)

    def copy(self, b):
        lane, (y, x, c, h, p) = b % 4, self.at
        x, c = b // 8, (b // 4) % 2
        home = ((c + lane // 2) % 2, x, c, h, lane % 2)
        return remote(self.block(b), self.place(self.mine), self.send.at[b], self.recv.at[self.mine], home)

    def start(self, b):
        @pl.when(same(b, self.mine) == 0)
        def _():
            self.copy(b).start()

        @pl.when(same(b, self.mine) == 1)
        def _():
            pltpu.make_async_copy(self.block(b), self.place(b), self.local).start()

    def finish(self):
        for b in range(16):

            @pl.when(same(b, self.mine) == 0)
            def _(b=b):
                dst = self.place(b)
                remote(dst, dst, self.send.at[b], self.recv.at[b], self.at).wait_recv()
                self.copy(b).wait_send()

            @pl.when(same(b, self.mine) == 1)
            def _(b=b):
                pltpu.make_async_copy(self.block(b), self.place(b), self.local).wait()


def row_sems():
    dma = pltpu.SemaphoreType.DMA
    return (dma((16,)), dma((16,)), dma)


def same(a, b):
    return 1 - jnp.minimum(jnp.abs(a - b), 1)


def signal(at):
    pl.semaphore_signal(pltpu.get_barrier_semaphore(), inc=1, device_id=device(at), device_id_type=MESH_ID)


class ToHeads:
    def __init__(self, at, layer, piece, place, sems):
        self.at, self.layer, self.piece, self.place = at, layer, piece, place
        self.send, self.recv, self.local, self.forth = sems
        y, x, c, h, p = at
        self.s = 2 * x + c
        self.sends = same(y, layer)
        self.near = 1 - far_role(at)

    def is_me(self, j):
        return self.sends * self.near * same(self.s, j)

    def greet(self):
        h, p = self.at[3], self.at[4]
        for k in range(4):

            @pl.when(self.near - self.is_me(k) == 1)
            def _(k=k):
                signal((self.layer, k // 2, k % 2, h, p))

        return self.sends * (4 - self.near)

    def copy(self, j):
        h, p = self.at[3], self.at[4]
        home = (flip(h, j % 2), j // 2, j % 2, h, p)
        return remote(self.piece(j), self.place(self.s), self.send.at[j], self.recv.at[self.s], home)

    def on(self, k):
        return remote(self.place(k), self.place(k), self.forth.at[k], self.recv.at[k], partner_of(self.at))

    def start(self):
        for j in range(4):

            @pl.when(self.sends - self.is_me(j) == 1)
            def _(j=j):
                self.copy(j).start()

            @pl.when(self.is_me(j) == 1)
            def _(j=j):
                pltpu.make_async_copy(self.piece(j), self.place(j), self.local).start()

    def forward(self):
        for k in range(4):

            @pl.when(self.near - self.is_me(k) == 1)
            def _(k=k):
                self.on(k).wait_recv()

            @pl.when(self.is_me(k) == 1)
            def _(k=k):
                pltpu.make_async_copy(self.piece(k), self.place(k), self.local).wait()

            @pl.when(self.near == 1)
            def _(k=k):
                self.on(k).start()

    def finish(self):
        for k in range(4):

            @pl.when(self.near == 0)
            def _(k=k):
                self.on(k).wait_recv()

            @pl.when(self.near == 1)
            def _(k=k):
                self.on(k).wait_send()

            @pl.when(self.sends - self.is_me(k) == 1)
            def _(k=k):
                self.copy(k).wait_send()


class ToShards:
    def __init__(self, at, layer, piece, place, sems, roles=(0, 1)):
        self.at, self.layer, self.piece, self.place, self.roles = at, layer, piece, place, roles
        self.send, self.recv, self.local = sems
        y, x, c, h, p = at
        self.s = 2 * x + c
        self.gets = same(y, layer)
        self.role = far_role(at)
        self.active = {(0, 1): 1, (0,): 1 - self.role, (1,): self.role}[roles]

    def is_me(self, k):
        return self.gets * (1 - self.role) * same(self.s, k) if 0 in self.roles else 0 * self.gets

    def greet(self):
        h, p = self.at[3], self.at[4]
        for j in range(4):
            if 1 in self.roles:

                @pl.when(self.gets == 1)
                def _(j=j):
                    signal((flip(h, j % 2), j // 2, j % 2, 1 - h, p))

            if 0 in self.roles:

                @pl.when(self.gets - self.is_me(j) == 1)
                def _(j=j):
                    signal((flip(h, j % 2), j // 2, j % 2, h, p))

        return self.active * (4 - self.gets * (1 - self.role))

    def copy(self, k):
        home = (self.layer, k // 2, k % 2, flip(self.at[3], self.role), self.at[4])
        return remote(
            self.piece(k), self.place(self.role, self.s), self.send.at[k], self.recv.at[self.role, self.s], home
        )

    def start(self):
        for k in range(4):

            @pl.when(self.active - self.is_me(k) == 1)
            def _(k=k):
                self.copy(k).start()

            @pl.when(self.is_me(k) == 1)
            def _(k=k):
                pltpu.make_async_copy(self.piece(k), self.place(0, k), self.local).start()

    def finish(self):
        for role in self.roles:
            for j in range(4):
                dst = self.place(role, j)
                comes = self.gets if role else self.gets - self.is_me(j)

                @pl.when(comes == 1)
                def _(role=role, j=j, dst=dst):
                    remote(dst, dst, self.send.at[0], self.recv.at[role, j], self.at).wait_recv()

        for k in range(4):

            @pl.when(self.active - self.is_me(k) == 1)
            def _(k=k):
                self.copy(k).wait_send()

            @pl.when(self.is_me(k) == 1)
            def _(k=k):
                pltpu.make_async_copy(self.piece(k), self.place(0, k), self.local).wait()


class ToHome:
    def __init__(self, at, layer, block, place, sems):
        self.at, self.layer, self.block, self.place = at, layer, block, place
        self.send, self.recv, self.local = sems
        y, x, c, h, p = at
        self.gets = same(y, layer)
        self.role = far_role(at)
        self.is_me = self.gets * (1 - self.role)

    def holder(self, micro):
        y, x, c, h, p = self.at
        return (flip(h, c), x, c, micro, p), (1 - flip(h, micro)) * self.is_me

    def greet(self):
        for micro in range(2):
            holder, is_me = self.holder(micro)

            @pl.when(self.gets - is_me == 1)
            def _(holder=holder):
                signal(holder)

        return 1 - self.is_me

    def copy(self):
        y, x, c, h, p = self.at
        home = (self.layer, x, c, flip(h, self.role), p)
        return remote(self.block, self.place(h), self.send, self.recv.at[h], home)

    def keep(self):
        return pltpu.make_async_copy(self.block, self.place(self.at[3]), self.local)

    def start(self):
        @pl.when(self.is_me == 0)
        def _():
            self.copy().start()

        @pl.when(self.is_me == 1)
        def _():
            self.keep().start()

    def finish(self):
        for micro in range(2):
            dst = self.place(micro)

            @pl.when(self.gets - self.holder(micro)[1] == 1)
            def _(micro=micro, dst=dst):
                remote(dst, dst, self.send, self.recv.at[micro], self.at).wait_recv()

        @pl.when(self.is_me == 0)
        def _():
            self.copy().wait_send()

        @pl.when(self.is_me == 1)
        def _():
            self.keep().wait()


def home_sems():
    dma = pltpu.SemaphoreType.DMA
    return (dma, dma((2,)), dma)


def head_sems():
    dma = pltpu.SemaphoreType.DMA
    return (dma((4,)), dma((4,)), dma, dma((4,)))


def shard_sems():
    dma = pltpu.SemaphoreType.DMA
    return (dma((4,)), dma((2, 4)), dma)


def slices(ref, size):
    return lambda j: ref.at[:, pl.ds(j * size, size)]


def columns(ref):
    wide = ref.shape[-1] // 4

    def place(s):
        start = s * wide
        return ref.at[:, :, pl.ds(start if isinstance(s, int) else pl.multiple_of(start, wide), wide)]

    return place


def unit_of(values):
    inverse = lax.rsqrt(jnp.mean(values * values, axis=-1, keepdims=True) + EPSILON)
    return (values * inverse, inverse)


def back_of(grad_normed, values, gain_row):
    unit, inverse = unit_of(values)
    shaped = grad_normed * gain_row
    inner = jnp.mean(shaped * unit, axis=-1, keepdims=True)
    return (inverse * (shaped - unit * inner), jnp.sum(grad_normed * unit, axis=0, keepdims=True))


def span(b, rows):
    return pl.ds(pl.multiple_of(b * rows, rows), rows)


def turned(top, bottom, cosine, sine):
    return (top * cosine - bottom * sine, bottom * cosine + top * sine)


def project_block(b, buf, w_ref, cos_ref, sin_ref, mix_ref, qkv_ref):
    rows, half = buf.shape[1], HS // 2
    cols = span(b, rows)
    raw = dot(w_ref[:3].reshape(3 * HS, buf.shape[2]), buf[b], NT)
    cosine, sine = cos_ref[:, cols], sin_ref[:, cols]
    for first, scale in ((0, HS**-0.5), (HS, 1.0)):
        a, bb = turned(raw[first : first + half], raw[first + half : first + HS], cosine, sine)
        qkv_ref[first : first + half, cols] = (a.astype(LOW) * scale).astype(LOW)
        qkv_ref[first + half : first + HS, cols] = (bb.astype(LOW) * scale).astype(LOW)
    value = raw[2 * HS :]
    if mix_ref is not None:
        value = 0.5 * value + 0.5 * mix_ref[:, cols].astype(F32)
    qkv_ref[2 * HS :, cols] = value.astype(LOW)


def up_block(b, buf, f_ref, hidden_ref, one_ref, two_ref):
    rows = span(b, buf.shape[1])
    x = buf[b]
    gate, up = dot(x, f_ref[0], NT), dot(x, f_ref[1], NT)
    sigmoid = 1.0 / (1.0 + jnp.exp(-gate))
    activated = gate * sigmoid
    hidden_ref[rows] = (activated * up).astype(LOW)
    one_ref[rows] = (up * sigmoid * (1.0 + gate * (1.0 - sigmoid))).astype(LOW)
    two_ref[rows] = activated.astype(LOW)


def held(buf):
    def blocks(use):
        def one(b, none):
            use(b, buf[b])
            return none

        lax.fori_loop(0, buf.shape[0], one, 0)

    return blocks


def streamed(far, ring, sems):
    half = ring.shape[0]

    def copy(b, slot):
        return pltpu.make_async_copy(far.at[b], ring.at[slot], sems.at[slot])

    for slot in range(half):
        copy(slot, slot).start()

    def blocks(use):
        def first(b, none):
            copy(b, b).wait()
            use(b, ring[b])
            copy(b + half, b).start()
            return none

        def second(b, none):
            copy(b + half, b).wait()
            use(b + half, ring[b])
            return none

        lax.fori_loop(0, half, first, 0)
        lax.fori_loop(0, half, second, 0)

    return blocks


class Stage:
    def __init__(self, sems):
        self.sems, self.count = sems, 0

    def copy(self, src, dst):
        copy = pltpu.make_async_copy(src, dst, self.sems.at[self.count])
        self.count += 1
        copy.start()
        return copy


def taking_turns(*steps):
    steps = list(steps)
    while steps:
        for one in list(steps):
            if next(one, True):
                steps.remove(one)
        yield


def feed_scratch(length, f_ref):
    return [pltpu.VMEM((length, f_ref.shape[1]), LOW)] * 3 + [pltpu.VMEM(f_ref.shape, F32)]


def out_project(at, push, att_in, wo_all, x_ref):
    push.finish()
    heads = att_in.shape[0] * HS
    summed = dot(att_in[...].reshape(heads, -1), wo_all[...].reshape(heads, -1), TN)
    return x_ref[...].astype(F32) + summed


def attend_and_share(at, steps, push, before, *refs):
    def after(qi):
        if qi == 0 and before is not None:
            before()
        each = TILE * 16 // refs[0].shape[1]
        for b in range(qi * each, (qi + 1) * each):
            push.start(b)
        next(steps, None)

    attend_body(*refs, after)
    run(steps)


def hidden_back(b, buf, f_ref, hidden_ref, one_ref, two_ref, sums_ref):
    here = span(b, buf.shape[1])
    grad = dot(buf[b], f_ref[2], NT)
    one_ref[here] = (grad * one_ref[here].astype(F32)).astype(LOW)
    two_ref[here] = (grad * two_ref[here].astype(F32)).astype(LOW)
    sums_ref[2] += dot(hidden_ref[here], buf[b], TN)


def down_back(
    at, top, ready, buf, blocks, total, boxes, ag_sems, rs_sems, f_ref, hidden_ref, one_ref, two_ref,
    gain_ref, middle_ref, sums_ref, wo_all, dout_block, push, dmid_ref, gain_grad_ref,
):
    rows = buf.shape[1]
    if not ready:
        sums_ref[...] = jnp.zeros_like(sums_ref)
        buf[block_of(at)] = top().astype(LOW)
        gather(at, buf, ag_sems, lambda b: hidden_back(b, buf, f_ref, hidden_ref, one_ref, two_ref, sums_ref))

    def partial(b):
        here = span(b, rows)
        return dot(one_ref[here], f_ref[0]) + dot(two_ref[here], f_ref[1])

    scatter(at, total, boxes, rs_sems, partial)
    grad, gain_grad = back_of(total[...], middle_ref[...], gain_ref[...])
    gain_grad_ref[...] = gain_grad
    grad = grad + top()
    dmid_ref[...] = grad
    heads = wo_all.shape[0] * HS
    found = dot(wo_all[...].reshape(heads, -1), grad.astype(LOW), NT).astype(LOW)
    dout_block[...] = found.reshape(dout_block.shape)
    for b in range(16):
        push.start(b)

    def gate_up(b, normed):
        here = span(b, rows)
        sums_ref[0] += dot(one_ref[here], normed, TN)
        sums_ref[1] += dot(two_ref[here], normed, TN)

    blocks(gate_up)
    push.finish()


def tables(lengths_ref, micro, cos_ref, sin_ref, seg_ref):
    half, length = cos_ref.shape
    index = lax.broadcasted_iota(jnp.int32, (half, 1), 0).astype(F32)
    frequency = jnp.exp(index * (-math.log(10000.0) / half))
    ends, end = [], 0
    for i in range(lengths_ref.shape[1]):
        end = end + lengths_ref[micro, i]
        ends.append(end)
    for part in tiles(length):
        places = part.start + lax.broadcasted_iota(jnp.int32, (1, TILE), 1)
        segment, start = jnp.zeros_like(places), jnp.zeros_like(places)
        for end in ends:
            past = places >= end
            segment = segment + jnp.where(past, 1, 0)
            start = jnp.where(past, end, start)
        seg_ref[:, part] = segment
        angles = (places - start).astype(F32) * frequency
        cos_ref[:, part] = jnp.cos(angles)
        sin_ref[:, part] = jnp.sin(angles)


def first_kernel(
    lengths_ref, in_ref, top_ref, a_ref, f_ref, gain_ref,
    cos_ref, sin_ref, seg_ref, qkv0_ref, att_ref, lse_ref, att_in, wo_all, x_here, middle_ref, out_ref, qkv1_ref,
    normed0_far, nmid_far, normed1_far, hidden_far, one_far, two_far, a0, a1, f0, f1, gains, top_here,
    buf, low_ref, a_here, f_here, gain_here, hidden_ref, one_ref, two_ref,
    key_x, query_x, val_x, scores, total, out_c, in_c, rin,
    ag_sems, wo_sems, rs_sems, share_sems, block_sems, a0_sems, a1_sems, f0_sems, f1_sems, swap, top_swap, gain_sems, loads,
):
    at = spot()
    y, x, c, h, p = at
    rows = x_here.shape[0]
    far = far_role(at)
    stage = Stage(loads)
    partner, above = partner_of(at), (1 - y, x, c, h, p)
    size = f_ref.shape[1] // 4
    a_pushes = [
        ToHeads(at, layer, slices(a_ref, HS), columns(into), sems)
        for layer, into, sems in ((0, a0, a0_sems), (1, a1, a1_sems))
    ]
    f_pushes = [
        ToHeads(at, layer, slices(f_ref, size), columns(into), sems)
        for layer, into, sems in ((0, f0, f0_sems), (1, f1, f1_sems))
    ]
    share = ToRows(at, lambda b: low_ref.at[:, pl.ds(b * rows, rows)], lambda b: att_in.at[b], share_sems)
    greet(at, *a_pushes, *f_pushes, peers=(partner,))
    swapped = remote(in_ref.at[1 - h], x_here, swap.at[0], swap.at[1], partner)
    stays = pltpu.make_async_copy(in_ref.at[h], x_here, swap.at[2])

    @pl.when(far == 0)
    def _():
        swapped.start()
        stays.start()

    top_swapped = remote(top_ref.at[1 - h], top_here, top_swap.at[0], top_swap.at[1], partner)
    top_stays = pltpu.make_async_copy(top_ref.at[h], top_here, top_swap.at[2])
    across = remote(gain_ref, gains.at[y], gain_sems.at[0], gain_sems.at[1], above)
    across.start()
    keeps = pltpu.make_async_copy(gain_ref, gains.at[y], gain_sems.at[2])
    keeps.start()
    for push in (a_pushes[0], f_pushes[0], a_pushes[1], f_pushes[1]):
        push.start()
    tables(lengths_ref, h, cos_ref, sin_ref, seg_ref)
    a_pushes[0].forward()
    keeps.wait()
    across.wait_send()
    remote(gain_ref, gains.at[1 - y], gain_sems.at[0], gain_sems.at[1], above).wait_recv()
    gain_copy = stage.copy(gains, gain_here)

    @pl.when(far == 1)
    def _():
        swapped.wait_recv()

    @pl.when(far == 0)
    def _():
        stays.wait()
        swapped.wait_send()

    gain_copy.wait()
    buf[block_of(at)] = (unit_of(x_here[...].astype(F32))[0] * gain_here[0, 0:1]).astype(LOW)

    def ready():
        a_pushes[0].finish()
        copy = stage.copy(a0, a_here)
        copy.wait()

    keep = (normed0_far, block_sems)
    gather(at, buf, ag_sems, lambda b: project_block(b, buf, a_here, cos_ref, sin_ref, None, qkv0_ref), keep, ready)
    wo_all[block_of(at)] = a_here[3]
    f_pushes[0].forward()
    attend_and_share(
        at, gathering(at, wo_all, wo_sems), share, lambda: kept(buf, keep),
        qkv0_ref, seg_ref, att_ref, low_ref, lse_ref, key_x, query_x, val_x, scores,
    )
    middle = out_project(at, share, att_in, wo_all, x_here)
    middle_ref[...] = middle
    buf[block_of(at)] = (unit_of(middle)[0] * gain_here[0, 1:2]).astype(LOW)
    keep = (nmid_far, block_sems)

    def more():
        f_pushes[0].finish()
        copy = stage.copy(f0, f_here)
        a_pushes[1].forward()
        f_pushes[1].forward()
        copy.wait()

        @pl.when(far == 0)
        def _():
            top_swapped.start()
            top_stays.start()

    gather(at, buf, ag_sems, lambda b: up_block(b, buf, f_here, hidden_ref, one_ref, two_ref), keep, more)
    saves = [stage.copy(*pair) for pair in ((hidden_ref, hidden_far), (one_ref, one_far), (two_ref, two_far))]
    boxes = (out_c, in_c, rin)
    scatter(
        at, total, boxes, rs_sems, lambda b: dot(hidden_ref[span(b, rows)], f_here[2]), lambda: kept(buf, keep)
    )
    out = (middle_ref[...] + total[...]).astype(LOW)
    out_ref[...] = out
    buf[block_of(at)] = (unit_of(out.astype(F32))[0] * gain_here[1, 0:1]).astype(LOW)
    keep = (normed1_far, block_sems)

    def last():
        a_pushes[1].finish()
        stage.copy(a1, a_here).wait()

    mix_ref = qkv0_ref.at[pl.ds(2 * HS, HS)]
    gather(
        at, buf, ag_sems, lambda b: project_block(b, buf, a_here, cos_ref, sin_ref, mix_ref, qkv1_ref), keep, last
    )
    kept(buf, keep)
    for save in saves:
        save.wait()
    f_pushes[1].finish()

    @pl.when(far == 1)
    def _():
        top_swapped.wait_recv()

    @pl.when(far == 0)
    def _():
        top_stays.wait()
        top_swapped.wait_send()


def turn_kernel(
    qkv_ref, seg_ref, a_ref, f_ref, gain_ref, x_ref, top_ref,
    att_ref, lse_ref, att_in, dmid_ref, gain_grad_ref, dout_ref, f_grad_ref, middle_ref, hidden_far,
    buf, nmid, wo_all, low_ref, dout_block, total, out_c, in_c, rin,
    ag_sems, wo_sems, rs_sems, share_sems, back_sems, loads,
):
    at = spot()
    rows = x_ref.shape[0]
    share = ToRows(at, lambda b: low_ref.at[:, pl.ds(b * rows, rows)], lambda b: att_in.at[b], share_sems)

    def column(b):
        start = b * rows
        return dout_ref.at[:, pl.ds(start if isinstance(b, int) else pl.multiple_of(start, rows), rows)]

    back = ToRows(at, lambda b: dout_block.at[b], column, back_sems)
    greet(at)
    wo_all[block_of(at)] = a_ref[3]
    buf[block_of(at)] = top_ref[...]
    steps = taking_turns(gathering(at, wo_all, wo_sems), gathering(at, buf, ag_sems))
    pl.run_scoped(
        functools.partial(attend_and_share, at, steps, share, None, qkv_ref, seg_ref, att_ref, low_ref, lse_ref),
        *attend_scratch(qkv_ref.shape[1]),
    )
    middle = out_project(at, share, att_in, wo_all, x_ref)
    middle_ref[...] = middle
    nmid[block_of(at)] = (unit_of(middle)[0] * gain_ref[...]).astype(LOW)

    def rest(hidden_ref, one_ref, two_ref, sums_ref):
        sums_ref[...] = jnp.zeros_like(sums_ref)

        def both_ways(b):
            up_block(b, nmid, f_ref, hidden_ref, one_ref, two_ref)
            hidden_back(b, buf, f_ref, hidden_ref, one_ref, two_ref, sums_ref)

        gather(at, nmid, ag_sems, both_ways)
        save = Stage(loads).copy(hidden_ref, hidden_far)
        boxes = (out_c, in_c, rin)
        down_back(
            at, lambda: top_ref[...].astype(F32), True, buf, held(nmid), total, boxes, ag_sems, rs_sems, f_ref, hidden_ref, one_ref,
            two_ref, gain_ref, middle_ref, sums_ref, wo_all, dout_block, back, dmid_ref, gain_grad_ref,
        )
        f_grad_ref[...] = sums_ref[...].astype(LOW)
        save.wait()

    pl.run_scoped(rest, *feed_scratch(qkv_ref.shape[1], f_ref))


def input_back(
    at, dqkv_ref, a_ref, x_ref, gain_ref, dmid_ref, gain_grad_ref, total, boxes, rs_sems, normed, load, sum_ref, after
):
    rows, width = total.shape

    def weight_sum():
        load.wait()
        sum_ref[...] = jnp.zeros_like(sum_ref)

        def one(b, none):
            sum_ref[...] += dot(dqkv_ref[:, span(b, rows)], normed[b])
            return none

        lax.fori_loop(0, 16, one, 0)
        if after is not None:
            after()

    def partial(b):
        return dot(dqkv_ref[:, span(b, rows)], a_ref[:3].reshape(3 * HS, width), TN)

    scatter(at, total, boxes, rs_sems, partial, weight_sum)
    grad, gain_grad = back_of(total[...], x_ref[...].astype(F32), gain_ref[...])
    gain_grad_ref[...] = gain_grad
    return grad + dmid_ref[...]


def staged_scratch(refs):
    return [pltpu.VMEM(ref.shape, ref.dtype) for ref in refs]


def attend_back_staged(stage, far, outs, steps, early, *refs):
    near, scratch = refs[: len(far)], refs[len(far) :]
    copies = [stage.copy(*pair) for pair in zip(far, near)]
    for _ in range(early):
        next(steps, None)
    for copy in copies:
        copy.wait()
    attend_back_body(*near, *outs, *scratch, lambda ki: next(steps, None))
    run(steps)


def meet(at, sem):
    for mask, core in ((1, 0), (2, 0), (4, 0), (0, 1)):
        peer = device(moved(at, mask, core))
        pl.semaphore_signal(sem, inc=1, device_id=peer, device_id_type=MESH_ID)
    pl.semaphore_wait(sem, 4)


def put_grads(a_grad_ref, in_sum_ref, out_total):
    for i in range(3):
        a_grad_ref[i] = in_sum_ref[i * HS : (i + 1) * HS].astype(LOW)
    a_grad_ref[3] = out_total.astype(LOW)


def by_columns(ref):
    wide = ref.shape[-1] // 4
    return lambda k: ref.at[:, :, pl.ds(k * wide, wide)]


def lower_kernel(
    a_ref, gain_in_ref, dmid_above, gain_mid_ref,
    x_far, f_far, middle_far, qkv_far, seg_far, att_far, lse_far, dout_far, cos_far, sin_far,
    hidden_far, one_far, two_far, normed_far, nmid_far, wo_far, hidden_above, middle_above, f_above, f_grad_above,
    out_below,
    send_ref, gain_in_grad_ref, dmid_ref, gain_mid_grad_ref, dout_ref, f_grad_ref, in_grad_ref, low_ref, out_ref, out_home, f_heard,
    buf, wo_all, dqkv_ref, in_sum_ref, dout_block,
    total, out_c, in_c, rin,
    ag_sems, rs_sems, back_sems, heard_sems, out_homing, loads, ring_sems, meeting,
):
    at = spot()
    rows = low_ref.shape[0]
    stage = Stage(loads)
    normed_copy = stage.copy(normed_far, buf)
    wo_copy = stage.copy(wo_far, wo_all)
    length = dqkv_ref.shape[1]
    home = ToHome(at, 0, out_below, lambda m: out_home.at[m], out_homing)
    far = far_role(at)
    push = remote(f_grad_above, f_heard, heard_sems.at[0], heard_sems.at[1], partner_of(at))

    def column(b):
        start = b * rows
        return dout_ref.at[:, pl.ds(start if isinstance(b, int) else pl.multiple_of(start, rows), rows)]

    back = ToRows(at, lambda b: dout_block.at[b], column, back_sems)
    greet(at, home, peers=(partner_of(at),))

    @pl.when(far == 1)
    def _():
        push.start()

    home.start()
    boxes = (out_c, in_c, rin)

    def out_steps(hidden_ref, down_ref):
        yield from scattering(
            at, total, boxes, rs_sems, lambda b: dot(hidden_ref[span(b, rows)], down_ref[...])
        )
        out_ref[...] = (dmid_ref[...] + total[...]).astype(LOW)

    def attention(hidden_ref, down_ref, *refs):
        copies = [
            stage.copy(*pair)
            for pair in ((hidden_above, hidden_ref), (f_above.at[2], down_ref), (middle_above, dmid_ref))
        ]
        for copy in copies:
            copy.wait()
        steps = out_steps(hidden_ref, down_ref)
        attend_back_staged(
            stage, (qkv_far, seg_far, att_far, lse_far, dout_far, cos_far, sin_far), (None, dqkv_ref, send_ref),
            steps, 1, *refs,
        )

    pl.run_scoped(
        attention,
        pltpu.VMEM(hidden_above.shape, LOW),
        pltpu.VMEM(f_above.shape[1:], LOW),
        *staged_scratch((qkv_far, seg_far, att_far, lse_far, dout_far, cos_far, sin_far)),
        *attend_back_scratch(length),
    )

    meet(at, meeting)

    def rest(hidden_ref, one_ref, two_ref, sums_ref, x_ref, f_ref, middle_ref, ring):
        blocks = streamed(nmid_far, ring, ring_sems)
        pairs = (
            (x_far, x_ref),
            (f_far, f_ref),
            (middle_far, middle_ref),
            (hidden_far, hidden_ref),
            (one_far, one_ref),
            (two_far, two_ref),
        )
        copies = [stage.copy(*pair) for pair in pairs]
        copies.pop(0).wait()
        grad = input_back(
            at, dqkv_ref, a_ref, x_ref, gain_in_ref, dmid_above, gain_in_grad_ref, total, boxes, rs_sems, buf,
            normed_copy, in_sum_ref, None,
        )
        dmid_ref[...] = grad
        low_ref[...] = grad.astype(LOW)
        in_grad_ref[...] = in_sum_ref[...].astype(LOW)
        for copy in copies + [wo_copy]:
            copy.wait()
        down_back(
            at, lambda: dmid_ref[...], False, buf, blocks, total, boxes, ag_sems, rs_sems, f_ref, hidden_ref, one_ref, two_ref,
            gain_mid_ref, middle_ref, sums_ref, wo_all, dout_block, back, dmid_ref, gain_mid_grad_ref,
        )
        f_grad_ref[...] = sums_ref[...].astype(LOW)

    ring_type = pltpu.VMEM((8, *nmid_far.shape[1:]), LOW)
    pl.run_scoped(rest, *feed_scratch(length, f_far), *staged_scratch((x_far, f_far, middle_far)), ring_type)

    home.finish()

    @pl.when(far == 1)
    def _():
        push.wait_send()

    @pl.when(far == 0)
    def _():
        push.wait_recv()


def last_kernel(
    qkv_ref, seg_ref, att_ref, lse_ref, dout_in, cos_ref, sin_ref, extra_ref, x_ref, a_ref, gain_ref, dmid_ref,
    att_in, att_in_above, dmid_above, in_grad_above, gains_ref, f_grad, f_above, f_heard, out_above, grad_above, normed_far,
    out_home, grad_home, f_in, a_in, gain_sum,
    buf, dqkv_ref, low_ref, two_low, in_sum_ref, a_grad_ref, a_above, gain_grad_ref, heard, f_sum, f_sum_above, f_got,
    key_x, val_x, query_x, dout_x, dq, scores, along,
    total, out_c, in_c, rin, out_total, out_c2, in_c2, rin2,
    rs_sems, rs2_sems, f_sems, f1_sems, a_sems, a1_sems, homing, out1_homing, grad_homing, gain_sems, got_sems, loads,
):
    at = spot()
    y, x, c, h, p = at
    stage = Stage(loads)
    far = far_role(at)
    copy = stage.copy(normed_far, buf)
    home = ToHome(at, 0, low_ref, lambda m: grad_home.at[m], homing)
    homes = [
        ToHome(at, layer, ref, lambda m, into=into: into.at[m], sems)
        for layer, ref, into, sems in (
            (1, out_above, out_home, out1_homing),
            (1, grad_above, grad_home, grad_homing),
        )
    ]
    f_push, f_push_above = (
        ToShards(at, layer, by_columns(ref), lambda role, j: f_in.at[j], sems, (0,))
        for layer, ref, sems in ((0, f_sum, f_sems), (1, f_sum_above, f1_sems))
    )
    a_push, a_push_above = (
        ToShards(at, layer, by_columns(ref), lambda role, j: a_in.at[role, j], sems)
        for layer, ref, sems in ((0, a_grad_ref, a_sems), (1, a_above, a1_sems))
    )
    peers = [moved(at, 0, 1), moved(at, 1), moved(at, 2), moved(at, 4), partner_of(at)]
    greet(at, home, *homes, f_push, f_push_above, a_push, a_push_above, peers=peers[4:], all_rows=False)
    give = remote(f_grad, f_got, got_sems.at[0], got_sems.at[1], partner_of(at))

    @pl.when(far == 1)
    def _():
        give.start()

    @pl.when(far == 0)
    def _():
        pairs = ((f_above, f_sum_above), (f_heard, f_sum))
        copies = [pltpu.make_async_copy(*pair, got_sems.at[2 + i]) for i, pair in enumerate(pairs)]
        for one in copies:
            one.start()
        for one in copies:
            one.wait()
        f_sum_above[...] = (f_sum_above[...].astype(F32) + f_sum[...].astype(F32)).astype(LOW)
        pltpu.make_async_copy(f_grad, f_sum, got_sems.at[2]).start()

    f_push_above.start()
    for one in homes:
        one.start()
    two_low[0] = dmid_ref[...].astype(LOW)
    two_low[1] = dmid_above[...].astype(LOW)

    def two_layers(b):
        return jnp.concatenate([dot(att_in[b], two_low[0]), dot(att_in_above[b], two_low[1])])

    steps = scattering(at, out_total, (out_c2, in_c2, rin2), rs2_sems, two_layers)
    attend_back_body(
        qkv_ref, seg_ref, att_ref, lse_ref, dout_in, cos_ref, sin_ref, extra_ref, dqkv_ref, None,
        key_x, val_x, query_x, dout_x, dq, scores, along, lambda ki: next(steps, None),
    )
    run(steps)

    for i in range(3):
        a_above[i] = in_grad_above[i * HS : (i + 1) * HS]
    a_above[3] = out_total[HS:].astype(LOW)
    a_push_above.start()

    @pl.when(far == 0)
    def _():
        pltpu.make_async_copy(f_grad, f_sum, got_sems.at[2]).wait()
        give.wait_recv()
        f_sum[...] = (f_sum[...].astype(F32) + f_got[...].astype(F32)).astype(LOW)

    f_push.start()

    def after():
        put_grads(a_grad_ref, in_sum_ref, out_total[:HS])
        a_push.start()

    grad = input_back(
        at, dqkv_ref, a_ref, x_ref, gain_ref, dmid_ref, gain_grad_ref, total, (out_c, in_c, rin), rs_sems, buf, copy,
        in_sum_ref, after,
    )
    low_ref[...] = grad.astype(LOW)
    home.start()
    gain_sum[0, 0:1] = gain_grad_ref[...]
    gain_sum[0, 1:4] = gains_ref[...]
    for i, peer in enumerate(peers):
        copy = remote(gain_sum.at[i], heard.at[i], gain_sems.at[0, i], gain_sems.at[1, i], peer)
        copy.start()
        copy.wait()
        gain_sum[i + 1] = gain_sum[i] + heard[i]

    @pl.when(far == 1)
    def _():
        give.wait_send()

    for push in (*homes, f_push_above, f_push, a_push_above, a_push, home):
        push.finish()


VMEM_SPEC = pl.BlockSpec(memory_space=pltpu.VMEM)
ANY_SPEC = pl.BlockSpec(memory_space=pl.ANY)


def links():
    dma = pltpu.SemaphoreType.DMA
    return (dma((3, 8)), dma((3, 8)), dma((8,)), dma((8,)))


def sum_boxes(rows, width):
    return [
        pltpu.VMEM((rows, width), F32),
        pltpu.VMEM((4, rows, width), LOW),
        pltpu.VMEM((8, rows, width), LOW),
        pltpu.VMEM((7, rows, width), LOW),
    ]


def reach(kernel, number, args, outs, scratch, name, far=(), scalars=()):
    return pl.pallas_call(
        kernel,
        out_shape=[jax.ShapeDtypeStruct(shape, dtype) for shape, dtype, _ in outs],
        in_specs=[pl.BlockSpec(memory_space=pltpu.SMEM)] * len(scalars)
        + [VMEM_SPEC] * len(args)
        + [ANY_SPEC] * len(far),
        out_specs=[ANY_SPEC if stays else VMEM_SPEC for _, _, stays in outs],
        scratch_shapes=scratch,
        compiler_params=pltpu.CompilerParams(
            collective_id=number, has_side_effects=number is not None, vmem_limit_bytes=VMEM_BYTES
        ),
        name=name,
    )(*scalars, *args, *far)


TILE = 512
MORE = 16
DOC_ROOM = 13
FLOOR = -1e20


def one_hot(seg_ref, part):
    rows = lax.broadcasted_iota(jnp.int32, (MORE, TILE), 0)
    return (rows, rows == seg_ref[:, part])


def tiles(length):
    return [slice(i * TILE, (i + 1) * TILE) for i in range(length // TILE)]


def causal():
    return lax.broadcasted_iota(jnp.int32, (TILE, 1), 0) <= lax.broadcasted_iota(jnp.int32, (1, TILE), 1)


def attend_body(qkv_ref, seg_ref, att_ref, low_ref, lse_ref, key_x, query_x, val_x, scores, after):
    length = qkv_ref.shape[1]
    for part in tiles(length):
        rows, hot = one_hot(seg_ref, part)
        key = jnp.concatenate([qkv_ref[HS : 2 * HS, part].astype(F32), jnp.where(hot, 1.0, 0.0)])
        key_x[part] = key.T.astype(LOW)
        query_x[:HS, part] = qkv_ref[:HS, part]
        query_x[HS:, part] = jnp.where(hot | (rows >= DOC_ROOM), 0.0, NEGATIVE).astype(LOW)
        val_x[:HS, part] = qkv_ref[2 * HS :, part]
        val_x[HS:, part] = jnp.where(rows == 0, 1.0, 0.0).astype(LOW)

    def query_tile(qi):
        cols = slice(qi * TILE, (qi + 1) * TILE)
        query = query_x[:, cols]

        def ahead(slot, kb):
            scores[slot] = dot(key_x[span(kb, TILE)], query)

        def update(slot, kb, state, diagonal=False):
            largest, summed = state
            found = scores[slot]
            if diagonal:
                found = jnp.where(causal(), found, NEGATIVE)
            newest = jnp.maximum(largest, jnp.max(found, axis=0, keepdims=True))
            weights = jnp.exp(found - newest).astype(LOW)
            summed = summed * jnp.exp(largest - newest) + dot(val_x[:, span(kb, TILE)], weights)
            return (newest, summed)

        def pair(i, state):
            ahead(1, 2 * i + 1)
            state = update(0, 2 * i, state)
            ahead(0, 2 * i + 2)
            return update(1, 2 * i + 1, state)

        state = (jnp.full((1, TILE), FLOOR, F32), jnp.zeros((HS + MORE, TILE), F32))
        ahead(0, 0)
        state = lax.fori_loop(0, qi // 2, pair, state)
        if qi % 2:
            ahead(1, qi)
            state = update(0, qi - 1, state)
        largest, summed = update(qi % 2, qi, state, True)
        totals = summed[HS : HS + 1]
        attended = summed[:HS] / totals
        att_ref[:, cols] = attended
        low_ref[:, cols] = attended.astype(LOW)
        lse_ref[:, cols] = largest + jnp.log(totals)

    for qi in range(length // TILE):
        query_tile(qi)
        after(qi)


def attend_scratch(length):
    return [
        pltpu.VMEM((length, HS + MORE), LOW),
        pltpu.VMEM((HS + MORE, length), LOW),
        pltpu.VMEM((HS + MORE, length), LOW),
        pltpu.VMEM((2, TILE, TILE), F32),
    ]


def three(values):
    high = values.astype(LOW).astype(F32)
    mid = (values - high).astype(LOW).astype(F32)
    return (high, mid, values - high - mid)


def attend_back_body(
    qkv_ref, seg_ref, att_ref, lse_ref, dout_ref, cos_ref, sin_ref, extra_ref, dqkv_ref, send_ref,
    key_x, val_x, query_x, dout_x, dq, scores, along, after,
):
    length = qkv_ref.shape[1]
    half, count = HS // 2, length // TILE
    for part in tiles(length):
        rows, hot = one_hot(seg_ref, part)
        ones = jnp.where(rows >= DOC_ROOM, 1.0, 0.0)
        key = jnp.concatenate([qkv_ref[HS : 2 * HS, part].astype(F32), jnp.where(hot, 1.0, ones)])
        key_x[part] = key.T.astype(LOW)
        val_x[part] = jnp.concatenate([qkv_ref[2 * HS :, part].astype(F32), ones]).T.astype(LOW)

        def tail(values, rest, rows=rows):
            for i, piece in enumerate(three(values)):
                rest = jnp.where(rows == DOC_ROOM + i, piece, rest)
            return rest.astype(LOW)

        dout = dout_ref[:, part]
        delta = jnp.sum(dout.astype(F32) * att_ref[:, part], axis=0, keepdims=True)
        query_x[:HS, part] = qkv_ref[:HS, part]
        query_x[HS:, part] = tail(-lse_ref[:, part], jnp.where(hot, 0.0, NEGATIVE))
        dout_x[:HS, part] = dout
        dout_x[HS:, part] = tail(-delta, jnp.zeros((MORE, TILE), F32))
    dq[...] = jnp.zeros_like(dq)

    def key_tile(ki):
        here = slice(ki * TILE, (ki + 1) * TILE)
        rest = count - 1 - ki

        def ahead(slot, qb):
            cols = span(qb, TILE)
            scores[slot] = dot(key_x[here], query_x[:, cols])
            along[slot] = dot(val_x[here], dout_x[:, cols])

        def update(slot, qb, state, diagonal=False):
            dk, dv = state
            cols = span(qb, TILE)
            weights = jnp.exp(scores[slot])
            if diagonal:
                weights = jnp.where(causal(), weights, 0.0)
            ds = (weights * along[slot]).astype(LOW)
            dv = dv + dot(dout_x[:HS, cols], weights.astype(LOW), NT)
            dk = dk + dot(query_x[:HS, cols], ds, NT)
            dq[:, cols] += dot(qkv_ref[HS : 2 * HS, here], ds)
            return (dk, dv)

        def pair(i, state):
            qb = ki + 1 + 2 * i
            ahead(0, qb + 1)
            state = update(1, qb, state)
            ahead(1, qb + 2)
            return update(0, qb + 1, state)

        zero = jnp.zeros((HS, TILE), F32)
        ahead(0, ki)
        if rest:
            ahead(1, ki + 1)
        state = update(0, ki, (zero, zero), True)
        state = lax.fori_loop(0, max(0, (rest - 1) // 2), pair, state)
        if rest % 2:
            state = update(1, count - 1, state)
        elif rest:
            ahead(0, count - 1)
            state = update(1, count - 2, state)
            state = update(0, count - 1, state)
        dk, dv = state
        a, b = turned(dk[:half], dk[half:], cos_ref[:, here], -sin_ref[:, here])
        dqkv_ref[HS : HS + half, here] = a.astype(LOW)
        dqkv_ref[HS + half : 2 * HS, here] = b.astype(LOW)
        if send_ref is None:
            dqkv_ref[2 * HS :, here] = (dv + extra_ref[:, here]).astype(LOW)
        else:
            dqkv_ref[2 * HS :, here] = (0.5 * dv).astype(LOW)
            send_ref[:, here] = 0.5 * dv

    for ki in range(count):
        key_tile(ki)
        after(ki)
    scale = HS**-0.5
    a, b = turned(dq[:half] * scale, dq[half:] * scale, cos_ref[...], -sin_ref[...])
    dqkv_ref[:half] = a.astype(LOW)
    dqkv_ref[half:HS] = b.astype(LOW)


def attend_back_scratch(length):
    wide = HS + MORE
    return [
        pltpu.VMEM((length, wide), LOW),
        pltpu.VMEM((length, wide), LOW),
        pltpu.VMEM((wide, length), LOW),
        pltpu.VMEM((wide, length), LOW),
        pltpu.VMEM((HS, length), F32),
        pltpu.VMEM((2, TILE, TILE), F32),
        pltpu.VMEM((2, TILE, TILE), F32),
    ]


def on_grid(
    inputs, cotangent, lengths, w_query, w_key, w_value, w_out, w_gate, w_up, w_down, attn_gain, mlp_gain
):
    at = spot()
    y, x, c, half, p = at
    rows, width = inputs.shape[1:]
    length = 16 * rows
    units = w_gate.shape[2] // 4
    a_own = jnp.stack([w_query[0].T, w_key[0].T, w_value[0].T, w_out[0]])
    f_own = jnp.stack([w_gate[0].T, w_up[0].T, w_down[0]])
    dma = pltpu.SemaphoreType.DMA

    def vmem(*shape, dtype=LOW):
        return pltpu.VMEM(shape, dtype)

    def near(*shape, dtype=LOW):
        return (shape, dtype, False)

    def stays(*shape, dtype=LOW):
        return (shape, dtype, True)

    buf = [vmem(16, rows, width)]
    boxes = sum_boxes(rows, width)
    small_boxes = sum_boxes(2 * HS, width)
    wo_buf = [vmem(16, HS, width)]
    low_head = [vmem(HS, length)]
    block, low_block = [vmem(rows, width, dtype=F32)], [vmem(rows, width)]
    hidden = [vmem(length, units)] * 3
    dout_block = [vmem(16, HS, rows)]
    in_sum = [vmem(3 * HS, width, dtype=F32), vmem(4, HS, width)]
    turned_out, head_out, lse_out = near(3 * HS, length), near(HS, length, dtype=F32), near(1, length, dtype=F32)
    att_in_out, every = near(16, HS, rows), stays(16, rows, width)
    block_out, low_out, gain_out = near(rows, width, dtype=F32), near(rows, width), near(1, width, dtype=F32)
    dout_out, f_out = near(HS, length), near(3, units, width)
    hidden_far, home_out = stays(length, units), stays(2, rows, width)
    a_far, f_far = stays(4, HS, width), stays(3, units, width)
    f_half = stays(4, 3, units, width // 4)
    a_shards, f_shards = stays(2, 4, 4, HS, width // 4), stays(2, 4, 3, units, width // 4)

    table = near(HS // 2, length, dtype=F32)
    (
        cosine, sine, segment, qkv0, att0, lse0, att_in0, wo_all0, own_in, mid0, out0, qkv1,
        normed0, nmid0, normed1, hid0, one0, two0, a0, a1, f0, f1, gains, own_top,
    ) = reach(
        first_kernel,
        0,
        [],
        [table, table, near(1, length, dtype=jnp.int32), turned_out, head_out, lse_out, att_in_out, near(16, HS, width), low_out, block_out, low_out, turned_out]
        + [every] * 3
        + [hidden_far] * 3
        + [a_far, a_far, f_far, f_far, stays(2, 2, width, dtype=F32), stays(rows, width)],
        buf
        + low_head
        + [vmem(4, HS, width), vmem(3, units, width), vmem(2, 2, width, dtype=F32)]
        + hidden
        + attend_scratch(length)
        + boxes
        + [links(), links(), links(), row_sems(), dma((16,))]
        + [head_sems()] * 4
        + [dma((3,)), dma((3,)), dma((3,)), dma((7,))],
        "first",
        [inputs, cotangent, a_own, f_own, jnp.concatenate([attn_gain, mlp_gain])],
        [lengths],
    )
    gain_in, gain_mid = [gains[i, 0:1] for i in range(2)], [gains[i, 1:2] for i in range(2)]
    att1, lse1, att_in1, dmid1, gmid1, dout1, f_grad1, mid1, hid1 = reach(
        turn_kernel,
        1,
        [qkv1, segment, a1, f1, gain_mid[1], out0, own_top],
        [head_out, lse_out, att_in_out, block_out, gain_out, dout_out, f_out, block_out, hidden_far],
        buf
        + buf
        + wo_buf
        + low_head
        + dout_block
        + boxes
        + [links(), links(), links(), row_sems(), row_sems(), dma((1,))],
        "turn",
    )
    extra, gin1, dmid0, gmid0, dout0, f_grad0, in_grad1, grad1, out1, home_out0, f_heard1 = reach(
        lower_kernel,
        2,
        [a1, gain_in[1], dmid1, gain_mid[0]],
        [head_out, gain_out, block_out, gain_out, dout_out, f_out, near(3 * HS, width), low_out, low_out, home_out, f_far],
        buf
        + wo_buf
        + [vmem(3 * HS, length)]
        + in_sum[:1]
        + dout_block
        + boxes
        + [links(), links(), row_sems(), dma((2,)), home_sems(), dma((18,)), dma((8,)), pltpu.SemaphoreType.REGULAR],
        "lower",
        [out0, f0, mid0, qkv1, segment, att1, lse1, dout1, cosine, sine, hid0, one0, two0, normed1, nmid0, wo_all0]
        + [hid1, mid1, f1, f_grad1, out0],
    )
    home_out1, grad_home, f_in, a_in, gain_sums = reach(
        last_kernel,
        3,
        [qkv0, segment, att0, lse0, dout0, cosine, sine, extra, own_in, a0, gain_in[0], dmid0, att_in0, att_in1, dmid1]
        + [in_grad1, jnp.concatenate([gin1, gmid0, gmid1])],
        [home_out, home_out, f_half, a_shards, near(6, 4, width, dtype=F32)],
        buf
        + [vmem(3 * HS, length)]
        + low_block
        + [vmem(2, rows, width)]
        + in_sum
        + [vmem(4, HS, width), vmem(1, width, dtype=F32), vmem(5, 4, width, dtype=F32)]
        + [vmem(3, units, width)] * 3
        + attend_back_scratch(length)
        + boxes
        + small_boxes
        + [links(), links()]
        + [shard_sems()] * 4
        + [home_sems()] * 3
        + [dma((2, 5)), dma((4,)), dma((1,))],
        "last",
        [f_grad0, f_grad1, f_heard1, out1, grad1, normed0],
    )
    on_first = y == 0
    a_sum = jnp.sum(a_in.astype(F32), axis=0)
    f_total = f_in.astype(F32)
    a_sum = jnp.transpose(a_sum, (1, 0, 2, 3)).reshape(4, 4 * HS, width // 4)
    f_total = jnp.transpose(f_total, (1, 0, 2, 3)).reshape(3, 4 * units, width // 4)
    share = width // 16
    first_col = (4 * (2 * x + c) + 2 * half + p) * share
    gain_share = lax.dynamic_slice_in_dim(gain_sums[5], first_col, share, 1)
    gain_in_share = jnp.where(on_first, gain_share[0:1], gain_share[1:2])
    gain_mid_share = jnp.where(on_first, gain_share[2:3], gain_share[3:4])
    return (
        jnp.where(on_first, home_out0, home_out1)[None],
        grad_home.astype(F32)[None],
        a_sum[0].T[None],
        a_sum[1].T[None],
        a_sum[2].T[None],
        a_sum[3][None],
        f_total[0].T[None],
        f_total[1].T[None],
        f_total[2][None],
        gain_in_share,
        gain_mid_share,
    )


def solution(mesh):
    in_specs = (
        P(None, ("seq", "tensor"), None),
        P(None, ("seq", "tensor"), None),
        P(),
        P("section", "seq", "tensor"),
        P("section", "seq", "tensor"),
        P("section", "seq", "tensor"),
        P("section", "tensor", "seq"),
        P("section", "seq", "tensor"),
        P("section", "seq", "tensor"),
        P("section", "tensor", "seq"),
        P("section", None),
        P("section", None),
    )
    out_specs = (
        P("section", None, ("seq", "tensor"), None),
        P("section", None, ("seq", "tensor"), None),
        P("section", "seq", "tensor"),
        P("section", "seq", "tensor"),
        P("section", "seq", "tensor"),
        P("section", "tensor", "seq"),
        P("section", "seq", "tensor"),
        P("section", "seq", "tensor"),
        P("section", "tensor", "seq"),
        P("section", ("seq", "tensor")),
        P("section", ("seq", "tensor")),
    )
    grid = (mesh.shape["section"], mesh.shape["seq"], mesh.shape["tensor"]) == (2, 4, 4)
    return jax.shard_map(
        on_grid if grid else on_device, mesh=mesh, in_specs=in_specs, out_specs=out_specs, check_vma=False
    )
```
